256 devices in a mesh: dom: 32 (over z, x), band: 8 (over y, core).
Axes of the slice: x: 4, y: 4, z: 8, core: 2. Of those that a mesh axis runs over, the one named last changes fastest.
Arguments:
- orbitals: float32 [8, 384, 16, 128], P('band', 'dom'), may hold values from -6 to 6
- potential: float32 [384, 16, 128], P('dom'), may hold values from -1.5 to 0.5
- atom_pos: int32 [1024, 3], P('dom'), may hold values from 0 to 127, as said below
- atom_count: int32 [32], P('dom'), may hold values from 8 to 32, as said below
- projectors: float32 [1024, 8, 384], P('dom'), may hold values from -0.4375 to 0.4375
- gammas: float32 [1024, 8], P('dom'), may hold values from 0.3 to 2
- ritz: float32 [8, 8], replicated, may hold values from -2 to 2
Outputs:
- filtered: float32 [8, 384, 16, 128], P('band', 'dom')
- rotated: float32 [8, 384, 16, 128], P('band', 'dom')
The draws below stay inside these ranges and needn't reach their ends.
Inputs may be any that keep to these rules, and one draw needn't show every extreme that they name: `atom_pos`: row a is the corner of slot a's support box: a plane within the 12 planes of slab a // 32, then a second grid index below 16 and a third below 128. Slab d's first atom_count[d] slots are live; some slab has all 32 live and some has 8.
All inputs are finite; a program needn't handle non-finite values.
Results may differ from the reference program's by a relative error of at most 0.00016.
Values sent between devices are 32-bit elements; how exact they have to be, the bound alone decides.
No kernel may reach another device: no remote copies, remote signals or barrier semaphores. Data moves between devices by JAX's collectives and lax.ppermute only.
A program may use at most 64 MiB of HBM per device.

```python
import math
import jax
import jax.numpy as jnp
from jax import lax

CX = 12
NY = 16
NZ = 128
ASLOT = 32
DEGREE = 4
NPROJ = 8
BX = 6
BY = 8
BZ = 8
SUP = 384
NX = 384
NORB = 8
ATOMS = 1024


def draw_atom_pos(key, part):
    key = jax.random.fold_in(key, 11)
    key_x, key_y, key_z = jax.random.split(key, 3)
    planes = jax.random.randint(key_x, (ATOMS,), 0, CX)
    rows = jax.random.randint(key_y, (ATOMS,), 0, NY)
    columns = jax.random.randint(key_z, (ATOMS,), 0, NZ)
    planes = planes.at[0].set(CX - 1).at[1].set(0)
    rows = rows.at[1].set(NY - 1).at[2].set(0)
    columns = columns.at[2].set(NZ - 1).at[0].set(0)
    return jnp.stack([planes, rows, columns], axis=1).astype(jnp.int32)


def draw_atom_count(key, part):
    key = jax.random.fold_in(key, 23)
    key_count, key_order = jax.random.split(key)
    slabs = ATOMS // ASLOT
    counts = jax.random.randint(key_count, (slabs,), ASLOT // 4, ASLOT + 1)
    order = jax.random.permutation(key_order, slabs)
    counts = counts.at[order[0]].set(ASLOT).at[order[1]].set(ASLOT // 4)
    return counts.astype(jnp.int32)


def steps_of(key, shape, shards, least, largest):
    def one(position, shards_of):
        draws = jax.random.uniform(jax.random.fold_in(jax.random.fold_in(key, 6), position), (shards_of,), jnp.float32, least / len(shards), largest / len(shards))
        return jnp.repeat(jnp.exp(draws), shape[position] // shards_of).reshape((-1,) + (1,) * (len(shape) - position - 1))

    factor_of = one(*shards[0])
    for cut in shards[1:]:
        factor_of = factor_of * one(*cut)
    return factor_of


def scatter_about(key, shape, deviation, bound, shards=(), kind=jnp.bfloat16):
    entries = deviation * jax.random.normal(key, shape, jnp.float32)
    if shards:
        entries = entries * steps_of(key, shape, shards, -0.22, 0.18)
    return jnp.clip(entries, -bound, bound).astype(kind)


def setup_inputs(seed: int = 0) -> dict:
    seeds = jax.random.split(jax.random.key(seed), 8)
    return {
        "orbitals": scatter_about(seeds[0], (NORB, NX, NY, NZ), 1.0, 6.0, ((0, 8), (1, 32)), jnp.float32),
        "potential": jnp.clip(-1.5 + 2.0 * jax.random.uniform(seeds[1], (NX, NY, NZ), jnp.float32) ** steps_of(seeds[1], (NX, NY, NZ), ((0, 32),), -0.2, 0.2), -1.5, 0.5),
        "atom_pos": draw_atom_pos(jax.random.fold_in(seeds[7], 71), 0),
        "atom_count": draw_atom_count(jax.random.fold_in(seeds[7], 71), 0),
        "projectors": scatter_about(seeds[4], (ATOMS, NPROJ, SUP), (SUP // 2) ** -0.5, 0.4375, ((0, 32),), jnp.float32),
        "gammas": jnp.clip(jnp.exp(math.log(2.0) - 1.89712 * jax.random.uniform(seeds[5], (ATOMS, NPROJ), jnp.float32) ** steps_of(seeds[5], (ATOMS, NPROJ), ((0, 32),), -0.2, 0.2)), 0.3, 2.0),
        "ritz": scatter_about(seeds[6], (NORB, NORB), NORB ** -0.5, 2.0, (), jnp.float32),
    }


STENCIL = (-5369.0 / 1800.0, 12.0 / 7.0, -15.0 / 56.0, 10.0 / 189.0, -1.0 / 112.0, 2.0 / 1925.0, -1.0 / 16632.0)
LOWER = -1.6
UPPER = 24.0


def box_offsets():
    cells = jnp.arange(BX * BY * BZ, dtype=jnp.int32)
    return cells // (BY * BZ), (cells // BZ) % BY, cells % BZ


def laplace_full(field):
    summed = 3.0 * STENCIL[0] * field
    for reach in range(1, 7):
        for axis in (1, 2, 3):
            summed = summed + STENCIL[reach] * (jnp.roll(field, reach, axis) + jnp.roll(field, -reach, axis))
    return summed


def nonlocal_full(field, atom_pos, atom_count, projectors, gammas):
    slot_idx = jnp.arange(ATOMS, dtype=jnp.int32)
    domain = slot_idx // ASLOT
    active = ((slot_idx % ASLOT) < atom_count[domain]).astype(jnp.float32)
    box_x, box_y, box_z = box_offsets()
    plane_idx = (domain[:, None] * CX + atom_pos[:, 0:1] + box_x[None]) % NX
    row_idx = (atom_pos[:, 1:2] + box_y[None]) % NY
    col_idx = (atom_pos[:, 2:3] + box_z[None]) % NZ
    flat_idx = ((plane_idx * NY + row_idx) * NZ + col_idx).astype(jnp.int32)
    orbits = field.shape[0]
    values = field.reshape(orbits, -1)[:, flat_idx]
    coeffs = jnp.einsum("nas,als->nal", values, projectors, precision=lax.Precision.HIGHEST)
    coeffs = coeffs * (gammas * active[:, None])[None]
    contrib = jnp.einsum("nal,als->nas", coeffs, projectors, precision=lax.Precision.HIGHEST)
    summed = jnp.zeros((orbits, NX * NY * NZ), jnp.float32).at[:, flat_idx].add(contrib)
    return summed.reshape(field.shape)


def reference(orbitals, potential, atom_pos, atom_count, projectors, gammas, ritz):
    center = 0.5 * (UPPER + LOWER)
    half = 0.5 * (UPPER - LOWER)
    previous = orbitals
    current = orbitals
    for iteration in range(DEGREE):
        applied = -0.5 * laplace_full(current) + potential[None] * current
        applied = applied + nonlocal_full(current, atom_pos, atom_count, projectors, gammas)
        if iteration == 0:
            updated = (applied - center * current) / half
        else:
            updated = (2.0 / half) * (applied - center * current) - previous
        previous = current
        current = updated
    rotated = jnp.einsum("ij,ixyz->jxyz", ritz, current, precision=lax.Precision.HIGHEST)
    return current, rotated
```

```python
import jax
import jax.numpy as jnp
import numpy as np
from jax import lax
from jax.experimental import pallas as pl
from jax.experimental.pallas import tpu as pltpu
from jax.sharding import PartitionSpec as P

STENCIL = (
    -5369.0 / 1800.0,
    12.0 / 7.0,
    -15.0 / 56.0,
    10.0 / 189.0,
    -1.0 / 112.0,
    2.0 / 1925.0,
    -1.0 / 16632.0,
)
LOWER = -1.6
UPPER = 24.0
CENTER = 0.5 * (UPPER + LOWER)
HALF = 0.5 * (UPPER - LOWER)

CX, NY, NZ = 12, 16, 128
ATOMS = 32
NPROJ, BX, BY, BZ = 8, 6, 8, 8
LANES = ATOMS * BZ
SPAN = CX + BX - 1
ROW_Y, ROW_POT, ROW_P, ROW_META, ROWS = 0, 192, 288, 1056, 1088
META_Z, META_XY, META_ROWS = 8, 9, 16


def z_stencil():
    full = np.zeros((NZ, NZ), np.float32)
    cells = np.arange(NZ)
    for reach in range(1, 7):
        full[cells, (cells + reach) % NZ] += STENCIL[reach]
        full[cells, (cells - reach) % NZ] += STENCIL[reach]
    high = full.astype(jnp.bfloat16)
    low = (full - high.astype(np.float32)).astype(jnp.bfloat16)
    return np.concatenate([high, high, low], 0)


def group_sum():
    atoms = np.arange(LANES) // BZ
    return (atoms[:, None] == atoms[None]).astype(jnp.bfloat16)


def two_terms(value, axis):
    high = value.astype(jnp.bfloat16)
    low = (value - high.astype(jnp.float32)).astype(jnp.bfloat16)
    return jnp.concatenate([high, low], axis)


def dot(left, right):
    return jnp.dot(left, right, preferred_element_type=jnp.float32)


def pack_kernel(y_ref, pot_ref, proj_ref, meta_ref, up_ref, down_ref):
    for out, planes in ((up_ref, slice(6, 12)), (down_ref, slice(0, 6))):
        out[ROW_Y : ROW_Y + 192, :] = y_ref[...].reshape(192, NZ)
        out[ROW_POT : ROW_POT + 96, :] = pot_ref[planes].reshape(96, NZ)
        for part in range(3):
            first = ROW_P + 256 * part
            out[first : first + 256, :] = proj_ref[:, :, 128 * part : 128 * part + 128].reshape(256, NZ)
        for tile in range(2):
            first = ROW_META + META_ROWS * tile
            out[first : first + META_ROWS, :] = meta_ref[:, 128 * tile : 128 * tile + 128]


def spread_projectors(read, work, table, group):
    lane = lax.broadcasted_iota(jnp.int32, (8, 128), 1)
    for tile in range(2):
        cols = slice(128 * tile, 128 * tile + 128)
        for part in range(3):
            items = [read(part, 16 * tile + a) for a in range(16)]
            for bit in (1, 2, 4, 8):
                upper = (lane & (8 * bit)) != 0
                for p in range(16):
                    if p & bit:
                        continue
                    q = p | bit
                    first, second = items[p], items[q]
                    items[p] = jnp.where(upper, pltpu.roll(second, 8 * bit, 1), first)
                    items[q] = jnp.where(upper, second, pltpu.roll(first, 128 - 8 * bit, 1))
            for g in range(16):
                i, j = 2 * part + g // 8, g % 8
                work[i, 8 * j : 8 * j + 8, :] = items[g]
        for i in range(BX):
            for l in range(NPROJ):
                table[group, l * BX + i, :, cols] = work.at[i][pl.ds(l, 8, stride=8), :]


def fill(padded, plane, value):
    count = value.shape[0]
    padded[plane : plane + count, 8:24, :] = value
    padded[plane : plane + count, 0:8, :] = value[:, 8:16]
    padded[plane : plane + count, 24:32, :] = value[:, 0:8]


def nonlocal_group(group, field2, first_in, planes_in, skip, gathered, placed, table, place, weight, onehot, sums):
    rows = slice(NY * first_in, NY * (first_in + planes_in))
    columns = dot(field2[rows, :], jnp.concatenate([onehot, onehot], 0)).reshape(planes_in, NY, LANES)
    for tile in range(2):
        part = columns[:, :, 128 * tile : 128 * tile + 128]
        gathered[group, tile, skip : skip + planes_in, 0:16, :] = part
        gathered[group, tile, skip : skip + planes_in, 16:24, :] = part[:, 0:8]
    lane = lax.broadcasted_iota(jnp.int32, (8, 128), 1)
    values = [[jnp.zeros((8, 128), jnp.float32)] * 2 for _ in range(BX)]
    for a in range(16):
        mine = (lane >> 3) == a
        for tile in range(2):
            x0, y0 = place(group, 16 * tile + a)
            for i in range(BX):
                values[i][tile] = jnp.where(mine, gathered[group, tile, x0 + i, pl.ds(y0, 8), :], values[i][tile])
    values = [jnp.concatenate(v, 1) for v in values]
    coeffs = []
    for l in range(NPROJ):
        total = values[0] * table[group, l * BX]
        for i in range(1, BX):
            total = total + values[i] * table[group, l * BX + i]
        coeffs.append(jnp.sum(total, 0, keepdims=True))
    coeffs = jnp.concatenate(coeffs, 0)
    both = dot(two_terms(coeffs, 0), sums)
    coeffs = (both[:8] + both[8:]) * weight
    contrib = []
    for i in range(BX):
        total = coeffs[0:1] * table[group, i]
        for l in range(1, NPROJ):
            total = total + coeffs[l : l + 1] * table[group, l * BX + i]
        contrib.append(total)
    for a in range(16):
        mine = (lane >> 3) == a
        for tile in range(2):
            x0, y0 = place(group, 16 * tile + a)
            cols = slice(128 * tile, 128 * tile + 128)
            for i in range(BX):
                pltpu.store(placed.at[group, tile, x0 + i, pl.ds(y0, 8), :], contrib[i][:, cols], mask=mine)


def spread_group(group, first, count, placed, onehot):
    planes = slice(first, first + count)
    tiles = []
    for tile in range(2):
        folded = placed[group, tile, planes, 0:8, :] + placed[group, tile, planes, 16:24, :]
        tiles.append(jnp.concatenate([folded, placed[group, tile, planes, 8:16, :]], 1).reshape(count * NY, 128))
    value = jnp.concatenate(tiles, 1)
    twice = jnp.concatenate([onehot, onehot], 1)
    spread = lax.dot_general(
        two_terms(value, 1), twice, (((1,), (1,)), ((), ())), preferred_element_type=jnp.float32
    )
    return spread.reshape(count, NY, NZ)


def stencil_plane(padded, plane):
    total = 3.0 * STENCIL[0] * padded[plane, 8:24, :]
    for reach in range(1, 7):
        along_x = padded[plane + reach, 8:24, :] + padded[plane - reach, 8:24, :]
        along_y = padded[plane, 8 + reach : 24 + reach, :] + padded[plane, 8 - reach : 24 - reach, :]
        total = total + STENCIL[reach] * (along_x + along_y)
    return total


def pair_kernel(first_pair, *refs):
    if first_pair:
        (mid_ref, low_ref, high_ref, pot_ref, proj_ref, meta_ref, zst_ref, sums_ref,
         out_ref, kept_ref, table,
         low_xy, high_xy, own_xy, padded, padded1, field2, gathered, placed, local, nonlocal_, work, sems) = refs
    else:
        (mid_ref, lowy_ref, highy_ref, kept_ref, table, low_ref, high_ref, pot_ref, meta_ref, zst_ref, sums_ref,
         out_ref,
         low_xy, high_xy, own_xy, padded, padded1, field2, gathered, placed, local, nonlocal_, sems) = refs

    copies = []
    for n, (source, target) in enumerate(((low_ref, low_xy), (meta_ref, own_xy), (high_ref, high_xy))):
        rows = pl.ds(8, 8) if n == 1 else pl.ds(ROW_META + 8, 8)
        copies.append(pltpu.make_async_copy(source.at[rows, pl.ds(0, 128)], target, sems.at[n]))
        copies[-1].start()

    def place(group, atom):
        held = (low_xy, own_xy, high_xy)[group]
        return held[1, atom].astype(jnp.int32), held[1, 32 + atom].astype(jnp.int32)

    def meta(group, rows):
        if group == 1:
            return meta_ref[rows, :]
        source = (low_ref, None, high_ref)[group]
        return jnp.concatenate(
            [source[ROW_META + META_ROWS * t + rows.start : ROW_META + META_ROWS * t + rows.stop, :] for t in range(2)], 1
        )

    def one_hot(group):
        column = lax.broadcasted_iota(jnp.int32, (NZ, LANES), 0).astype(jnp.float32)
        return jnp.where(column == meta(group, slice(META_Z, META_Z + 1)), 1.0, 0.0).astype(jnp.bfloat16)

    if first_pair:
        low_y, high_y = low_ref[ROW_Y : ROW_Y + 192, :], high_ref[ROW_Y : ROW_Y + 192, :]
    else:
        low_y, high_y = lowy_ref[...].reshape(192, NZ), highy_ref[...].reshape(192, NZ)
    mid_y = mid_ref[...].reshape(192, NZ)
    for n, value in enumerate((low_y, mid_y, high_y)):
        fill(padded, 12 * n, value.reshape(CX, NY, NZ))
        field2[192 * n : 192 * n + 192, :] = two_terms(value, 1)
    placed[...] = jnp.zeros_like(placed)
    gathered[2, :, 12:SPAN] = jnp.zeros((2, SPAN - 12, 24, 128), jnp.float32)

    if first_pair:
        for group, source in enumerate((low_ref, None, high_ref)):
            if group == 1:
                read = lambda part, a: proj_ref[a, :, 128 * part : 128 * part + 128]
            else:
                read = lambda part, a, s=source: s[ROW_P + 256 * part + 8 * a : ROW_P + 256 * part + 8 * a + 8, :]
            spread_projectors(read, work, table, group)
    hots = [one_hot(g) for g in range(3)]
    weights = [meta(g, slice(0, 8)) for g in range(3)]
    for copy in copies:
        copy.wait()

    for group, planes in ((0, SPAN), (1, SPAN), (2, 12)):
        nonlocal_group(group, field2, 12 * group, planes, 0, gathered, placed, table, place, weights[group],
                       hots[group], sums_ref[...])
    along_z = dot(field2[96:480, :], zst_ref[0:256, :]) + dot(field2[96:480, 0:128], zst_ref[256:384, :])
    local[...] = along_z.reshape(24, NY, NZ)
    nonlocal_[0:11] = spread_group(0, 6, 11, placed, hots[0])
    nonlocal_[11:24] = jnp.zeros((13, NY, NZ), jnp.float32)
    nonlocal_[6:23] += spread_group(1, 0, 17, placed, hots[1])
    nonlocal_[18:24] += spread_group(2, 0, 6, placed, hots[2])
    scale = (1.0 if first_pair else 2.0) / HALF
    for p in range(24):
        if p < 6:
            pot = low_ref[ROW_POT + 16 * p : ROW_POT + 16 * p + 16, :]
        elif p < 18:
            pot = pot_ref[p - 6]
        else:
            pot = high_ref[ROW_POT + 16 * (p - 18) : ROW_POT + 16 * (p - 18) + 16, :]
        here = padded[p + 6, 8:24, :]
        laplace = stencil_plane(padded, p + 6) + local[p]
        applied = -0.5 * laplace + (pot - CENTER) * here + nonlocal_[p]
        updated = scale * applied
        if first_pair:
            kept_ref[p] = updated
        else:
            updated = updated - kept_ref[p]
        fill(padded1, p, updated[None])
        field2[16 * p : 16 * p + 16, :] = two_terms(updated, 1)

    nonlocal_group(0, field2, 0, 11, 6, gathered, placed, table, place, weights[0], hots[0], sums_ref[...])
    nonlocal_group(1, field2, 6, SPAN, 0, gathered, placed, table, place, weights[1], hots[1], sums_ref[...])
    along_z = dot(field2[96:288, :], zst_ref[0:256, :]) + dot(field2[96:288, 0:128], zst_ref[256:384, :])
    local[0:12] = along_z.reshape(12, NY, NZ)
    nonlocal_[0:12] = spread_group(1, 0, 12, placed, hots[1])
    nonlocal_[0:5] += spread_group(0, 12, 5, placed, hots[0])
    for p in range(12):
        here = padded1[p + 6, 8:24, :]
        laplace = stencil_plane(padded1, p + 6) + local[p]
        applied = -0.5 * laplace + (pot_ref[p] - CENTER) * here + nonlocal_[p]
        out_ref[0, p] = (2.0 / HALF) * applied - padded[p + 12, 8:24, :]


def run_pair(first_pair, args):
    shape = lambda *dims: jax.ShapeDtypeStruct(dims, jnp.float32)
    outs = [shape(1, CX, NY, NZ)]
    scratch = [pltpu.SMEM((8, 128), jnp.float32)] * 3 + [
        pltpu.VMEM((36, 32, NZ), jnp.float32),
        pltpu.VMEM((24, 32, NZ), jnp.float32),
        pltpu.VMEM((576, 2 * NZ), jnp.bfloat16),
        pltpu.VMEM((3, 2, SPAN, 24, 128), jnp.float32),
        pltpu.VMEM((3, 2, SPAN, 24, 128), jnp.float32),
        pltpu.VMEM((24, NY, NZ), jnp.float32),
        pltpu.VMEM((24, NY, NZ), jnp.float32),
    ]
    if first_pair:
        outs += [shape(24, NY, NZ), shape(3, NPROJ * BX, BY, LANES)]
        scratch += [pltpu.VMEM((BX, BY * NPROJ, 128), jnp.float32)]
    scratch += [pltpu.SemaphoreType.DMA((3,))]
    vmem = pl.BlockSpec(memory_space=pltpu.VMEM)
    return pl.pallas_call(
        lambda *refs: pair_kernel(first_pair, *refs),
        out_shape=outs,
        in_specs=[vmem] * len(args),
        out_specs=[vmem] * len(outs),
        scratch_shapes=scratch,
        compiler_params=pltpu.CompilerParams(vmem_limit_bytes=40 * 2**20),
        name="two_steps",
    )(*args)


def ring(axis, step):
    count = lax.axis_size(axis)
    return [(i, (i + step) % count) for i in range(count)]


def shards(orbitals, potential, atom_pos, atom_count, projectors, gammas, ritz):
    live = (jnp.arange(ATOMS, dtype=jnp.int32) < atom_count[0]).astype(jnp.float32)
    weight = jnp.repeat((gammas * live[:, None]).T, BZ, axis=1)
    columns = (atom_pos[:, 2:3] + jnp.arange(BZ, dtype=jnp.int32)[None]) % NZ
    corners = jnp.concatenate([atom_pos[:, 0], atom_pos[:, 1]])
    meta = jnp.concatenate(
        [
            weight,
            columns.reshape(1, LANES).astype(jnp.float32),
            jnp.pad(corners.astype(jnp.float32), (0, LANES - 2 * ATOMS))[None],
            jnp.zeros((META_ROWS - 10, LANES), jnp.float32),
        ],
        0,
    )
    vmem = pl.BlockSpec(memory_space=pltpu.VMEM)
    up, down = pl.pallas_call(
        pack_kernel,
        out_shape=[jax.ShapeDtypeStruct((ROWS, NZ), jnp.float32)] * 2,
        in_specs=[vmem] * 4,
        out_specs=[vmem] * 2,
        compiler_params=pltpu.CompilerParams(vmem_limit_bytes=16 * 2**20),
        name="pack",
    )(orbitals, potential, projectors, meta)
    low = lax.ppermute(up, "dom", ring("dom", 1))
    high = lax.ppermute(down, "dom", ring("dom", -1))
    zst, sums = jnp.asarray(z_stencil()), jnp.asarray(group_sum())
    second, first, table = run_pair(True, (orbitals, low, high, potential, projectors, meta, zst, sums))
    low_y = lax.ppermute(second, "dom", ring("dom", 1))
    high_y = lax.ppermute(second, "dom", ring("dom", -1))
    (filtered,) = run_pair(
        False, (second, low_y, high_y, first, table, low, high, potential, meta, zst, sums)
    )

    count = lax.axis_size("band")
    band = lax.axis_index("band")
    other = lax.ppermute(filtered, "band", [(i, i ^ 1) for i in range(count)])
    picked = jnp.arange(count, dtype=jnp.int32)
    own_row = jnp.sum(jnp.where((picked == band)[:, None], ritz, 0.0), 0)
    other_row = jnp.sum(jnp.where((picked == band ^ 1)[:, None], ritz, 0.0), 0)

    def part(hop):
        to = picked == band ^ (2 * hop)
        return (
            jnp.sum(jnp.where(to, own_row, 0.0)) * filtered
            + jnp.sum(jnp.where(to, other_row, 0.0)) * other
        )

    rotated = part(0)
    arrived = [lax.ppermute(part(hop), "band", [(i, i ^ (2 * hop)) for i in range(count)]) for hop in (1, 2, 3)]
    for value in arrived:
        rotated = rotated + value
    return (filtered, rotated)


def solution(mesh):
    in_specs = (
        P("band", "dom", None, None),
        P("dom", None, None),
        P("dom", None),
        P("dom"),
        P("dom", None, None),
        P("dom", None),
        P(),
    )
    out_specs = (P("band", "dom", None, None), P("band", "dom", None, None))
    return jax.shard_map(shards, mesh=mesh, in_specs=in_specs, out_specs=out_specs, check_vma=False)
```

```python
import jax
import jax.numpy as jnp
from jax import lax
from jax.experimental import pallas as pl
from jax.experimental.pallas import tpu as pltpu
from jax.sharding import PartitionSpec as P

STENCIL = (
    -5369.0 / 1800.0,
    12.0 / 7.0,
    -15.0 / 56.0,
    10.0 / 189.0,
    -1.0 / 112.0,
    2.0 / 1925.0,
    -1.0 / 16632.0,
)
LOWER = -1.6
UPPER = 24.0
CENTER = 0.5 * (UPPER + LOWER)
HALF = 0.5 * (UPPER - LOWER)

CX, NY, NZ = 12, 16, 128
ATOMS = 32
NPROJ, BX, BY, BZ = 8, 6, 8, 8
LANES = ATOMS * BZ
SPAN = CX + BX - 1
PAIRS = NPROJ * BX
TILE_Y, TILE_POT, TILE_P, TILE_META, TILES = 0, 24, 36, 84, 88
ROW_Z, ROW_X0, ROW_Y0 = 0, 1, 2

VMEM = pl.BlockSpec(memory_space=pltpu.VMEM)
HBM = pl.BlockSpec(memory_space=pltpu.HBM)
SMEM = pl.BlockSpec(memory_space=pltpu.SMEM)


def shape(*dims, dtype=jnp.float32):
    return jax.ShapeDtypeStruct(dims, dtype)


def call(kernel, outs, ins, args, name, scratch=(), out_specs=None, flops=1_000_000):
    return pl.pallas_call(
        kernel,
        out_shape=outs,
        in_specs=ins,
        out_specs=out_specs or [VMEM] * len(outs),
        scratch_shapes=list(scratch),
        compiler_params=pltpu.CompilerParams(vmem_limit_bytes=32 * 2**20),
        cost_estimate=pl.CostEstimate(flops=flops, bytes_accessed=2_000_000, transcendentals=0),
        name=name,
    )(*args)


def two_terms(value, axis):
    high = value.astype(jnp.bfloat16)
    low = (value - high.astype(jnp.float32)).astype(jnp.bfloat16)
    return jnp.concatenate([high, low], axis)


def dot(left, right):
    return jnp.dot(left, right, preferred_element_type=jnp.float32)


def half(tile):
    return slice(128 * tile, 128 * tile + 128)


def pack_kernel(y_hbm, pot_hbm, proj_hbm, gamma_hbm, pos_hbm, count_ref,
                up_ref, down_ref, pot_ref, proj_ref, gamma_ref, pos_ref, sems):
    core = lax.axis_index("band") % 2
    first = 16 * core
    copies = [
        pltpu.make_async_copy(gamma_hbm, gamma_ref, sems.at[0]),
        pltpu.make_async_copy(pos_hbm, pos_ref, sems.at[1]),
    ]
    moves = [
        (pot_hbm, pot_ref),
        (pot_hbm.at[pl.ds(12, 12)], up_ref.at[pl.ds(TILE_POT, 12)]),
        (pot_hbm.at[pl.ds(0, 12)], down_ref.at[pl.ds(TILE_POT, 12)]),
    ]
    for out in (up_ref, down_ref):
        moves.append((y_hbm, out.at[pl.ds(TILE_Y, 24)]))
        for part in range(3):
            source = proj_hbm.at[pl.ds(first, 16), pl.ds(0, 8), pl.ds(128 * part, 128)]
            moves.append((source, out.at[pl.ds(TILE_P + 16 * part, 16)]))
    for part in range(3):
        source = proj_hbm.at[pl.ds(0, ATOMS), pl.ds(0, 8), pl.ds(128 * part, 128)]
        moves.append((source, proj_ref.at[pl.ds(ATOMS * part, ATOMS)]))
    for n, (source, target) in enumerate(moves):
        copies.append(pltpu.make_async_copy(source, target, sems.at[2 + n]))
    for copy in copies:
        copy.start()
    copies[0].wait()
    copies[1].wait()
    live = lax.broadcasted_iota(jnp.int32, (1, ATOMS), 1) < count_ref[0]
    weight = jnp.where(live, gamma_ref[...], 0.0)
    repeat = lax.broadcasted_iota(jnp.int32, (ATOMS, LANES), 1) >> 3
    repeat = jnp.where(repeat == lax.broadcasted_iota(jnp.int32, (ATOMS, LANES), 0), 1.0, 0.0)
    corner = pos_ref[...].astype(jnp.float32)
    spread = lambda v: jnp.dot(v, repeat, preferred_element_type=jnp.float32, precision=lax.Precision.HIGHEST)
    weight = spread(weight)
    column = spread(corner)[2:3] + (lax.broadcasted_iota(jnp.int32, (1, LANES), 1) & 7).astype(jnp.float32)
    column = jnp.where(column >= NZ, column - NZ, column)
    for out in (up_ref, down_ref):
        for tile in range(2):
            out[TILE_META + 2 * tile] = weight[:, half(tile)]
            out[TILE_META + 2 * tile + 1] = jnp.broadcast_to(column[:, half(tile)], (8, 128))
        out[TILE_META + 1, ROW_X0 : ROW_X0 + 1, 0:ATOMS] = corner[0:1]
        out[TILE_META + 1, ROW_Y0 : ROW_Y0 + 1, 0:ATOMS] = corner[1:2]
    for copy in copies[2:]:
        copy.wait()


def spread_projectors(read, work, table):
    lane = lax.broadcasted_iota(jnp.int32, (8, 128), 1)
    for part in range(3):
        items = [read(part, a) for a in range(16)]
        for bit in (1, 2, 4, 8):
            upper = (lane & (8 * bit)) != 0
            for p in range(16):
                if p & bit:
                    continue
                q = p | bit
                first, second = items[p], items[q]
                items[p] = jnp.where(upper, pltpu.roll(second, 8 * bit, 1), first)
                items[q] = jnp.where(upper, second, pltpu.roll(first, 128 - 8 * bit, 1))
        for g in range(16):
            i, j = 2 * part + g // 8, g % 8
            work[i, 8 * j : 8 * j + 8, :] = items[g]
    for i in range(BX):
        for l in range(NPROJ):
            table[l * BX + i] = work.at[i][pl.ds(l, 8, stride=8), :]


def prepare_kernel(proj_ref, table_ref, zst_ref, sums_ref, work):
    for tile in range(2):
        read = lambda part, a: proj_ref[ATOMS * part + 16 * tile + a]
        spread_projectors(read, work, table_ref.at[tile])
    apart = lax.broadcasted_iota(jnp.int32, (NZ, NZ), 0) - lax.broadcasted_iota(jnp.int32, (NZ, NZ), 1)
    full = jnp.zeros((NZ, NZ), jnp.float32)
    for reach in range(1, 7):
        near = ((apart & (NZ - 1)) == reach) | ((apart & (NZ - 1)) == NZ - reach)
        full = jnp.where(near, STENCIL[reach], full)
    high = full.astype(jnp.bfloat16)
    zst_ref[0:128, :] = high
    zst_ref[128:256, :] = high
    zst_ref[256:384, :] = (full - high.astype(jnp.float32)).astype(jnp.bfloat16)
    atom = lambda axis: lax.broadcasted_iota(jnp.int32, (LANES, LANES), axis) >> 3
    sums_ref[...] = jnp.where(atom(0) == atom(1), 1.0, 0.0).astype(jnp.bfloat16)


def fill(padded, plane, value):
    count = value.shape[0]
    padded[plane : plane + count, 8:24, :] = value
    padded[plane : plane + count, 0:8, :] = value[:, 8:16]
    padded[plane : plane + count, 24:32, :] = value[:, 0:8]


class Boxes:
    def __init__(self, sources, held, sems):
        self.sources, self.held = sources, held
        self.copies = [
            pltpu.make_async_copy(s.at[TILE_META + 1], h, sems.at[n]) for n, (s, h) in enumerate(zip(sources, held))
        ]
        for copy in self.copies:
            copy.start()

    def wait(self):
        for copy in self.copies:
            copy.wait()

    def place(self, group, atom):
        held = self.held[group]
        return held[ROW_X0, atom].astype(jnp.int32), held[ROW_Y0, atom].astype(jnp.int32)

    def weight(self, group):
        source = self.sources[group]
        return jnp.concatenate([source[TILE_META], source[TILE_META + 2]], 1)

    def one_hot(self, group):
        source = self.sources[group]
        column = jnp.concatenate(
            [source[TILE_META + 1 + 2 * t, ROW_Z : ROW_Z + 1, :] for t in range(2)], 1
        )
        cells = lax.broadcasted_iota(jnp.int32, (NZ, LANES), 0).astype(jnp.float32)
        return jnp.where(cells == column, 1.0, 0.0).astype(jnp.bfloat16)


def gather_columns(group, field2, first_in, planes_in, skip, gathered, onehot):
    rows = slice(NY * first_in, NY * (first_in + planes_in))
    columns = dot(field2[rows, :], jnp.concatenate([onehot, onehot], 0)).reshape(planes_in, NY, LANES)
    for tile in range(2):
        part = columns[:, :, half(tile)]
        gathered[group, tile, skip : skip + planes_in, 0:16, :] = part
        gathered[group, tile, skip : skip + planes_in, 16:24, :] = part[:, 0:8]


def read_windows(group, gathered, boxes):
    lane = lax.broadcasted_iota(jnp.int32, (8, 128), 1)
    values = [[jnp.zeros((8, 128), jnp.float32)] * 2 for _ in range(BX)]
    for a in range(16):
        mine = (lane >> 3) == a
        for tile in range(2):
            x0, y0 = boxes.place(group, 16 * tile + a)
            for i in range(BX):
                values[i][tile] = jnp.where(mine, gathered[group, tile, x0 + i, pl.ds(y0, 8), :], values[i][tile])
    return values


def contributions(group, values, table, placed, boxes, sums):
    coeffs = []
    for tile in range(2):
        rows = []
        for l in range(NPROJ):
            total = values[0][tile] * table[tile, l * BX]
            for i in range(1, BX):
                total = total + values[i][tile] * table[tile, l * BX + i]
            rows.append(jnp.sum(total, 0, keepdims=True))
        coeffs.append(jnp.concatenate(rows, 0))
    both = dot(two_terms(jnp.concatenate(coeffs, 1), 0), sums)
    coeffs = (both[:8] + both[8:]) * boxes.weight(group)
    lane = lax.broadcasted_iota(jnp.int32, (8, 128), 1)
    contrib = [[None] * 2 for _ in range(BX)]
    for tile in range(2):
        rows = [jnp.broadcast_to(coeffs[l : l + 1, half(tile)], (8, 128)) for l in range(NPROJ)]
        for i in range(BX):
            total = rows[0] * table[tile, i]
            for l in range(1, NPROJ):
                total = total + rows[l] * table[tile, l * BX + i]
            contrib[i][tile] = total
    for a in range(16):
        mine = (lane >> 3) == a
        for tile in range(2):
            x0, y0 = boxes.place(group, 16 * tile + a)
            for i in range(BX):
                pltpu.store(placed.at[group, tile, x0 + i, pl.ds(y0, 8), :], contrib[i][tile], mask=mine)


def spread_group(group, first, count, placed, onehot):
    planes = slice(first, first + count)
    tiles = []
    for tile in range(2):
        folded = placed[group, tile, planes, 0:8, :] + placed[group, tile, planes, 16:24, :]
        tiles.append(jnp.concatenate([folded, placed[group, tile, planes, 8:16, :]], 1).reshape(count * NY, 128))
    twice = jnp.concatenate([onehot, onehot], 1)
    spread = lax.dot_general(
        two_terms(jnp.concatenate(tiles, 1), 1), twice, (((1,), (1,)), ((), ())),
        preferred_element_type=jnp.float32,
    )
    return spread.reshape(count, NY, NZ)


def along_z(field2, rows, zst_ref):
    return dot(field2[rows, :], zst_ref[0:256, :]) + dot(field2[rows, 0:128], zst_ref[256:384, :])


def stencil_plane(padded, plane):
    total = 3.0 * STENCIL[0] * padded[plane, 8:24, :]
    for reach in range(1, 7):
        along_x = padded[plane + reach, 8:24, :] + padded[plane - reach, 8:24, :]
        along_y = padded[plane, 8 + reach : 24 + reach, :] + padded[plane, 8 - reach : 24 - reach, :]
        total = total + STENCIL[reach] * (along_x + along_y)
    return total


def potential_plane(p, low_ref, pot_ref, high_ref):
    source, tile = (
        (low_ref, TILE_POT + 2 * p) if p < 6 else (pot_ref, 2 * (p - 6)) if p < 18 else (high_ref, TILE_POT + 2 * (p - 18))
    )
    return source[tile : tile + 2].reshape(NY, NZ)


def load_fields(fields, padded, field2):
    for n, value in enumerate(fields):
        fill(padded, 12 * n, value.reshape(CX, NY, NZ))
        field2[192 * n : 192 * n + 192, :] = two_terms(value.reshape(192, NZ), 1)


def head_kernel(up_ref, low_ref, high_ref, pot_ref, table_ref, zst_ref, sums_ref,
                half_ref, values_ref, partial_ref,
                low_xy, own_xy, high_xy, padded, field2, gathered, placed, local, nonlocal_, work, sems):
    boxes = Boxes((low_ref, up_ref, high_ref), (low_xy, own_xy, high_xy), sems)
    load_fields([r[TILE_Y : TILE_Y + 24] for r in (low_ref, up_ref, high_ref)], padded, field2)
    placed[...] = jnp.zeros_like(placed)
    gathered[2, :, 12:SPAN] = jnp.zeros((2, SPAN - 12, 24, 128), jnp.float32)
    own_hot = boxes.one_hot(1)
    gather_columns(1, field2, 12, SPAN, 0, gathered, own_hot)
    gather_columns(0, field2, 0, SPAN, 0, gathered, boxes.one_hot(0))
    gather_columns(2, field2, 24, 12, 0, gathered, boxes.one_hot(2))
    boxes.wait()
    contributions(1, read_windows(1, gathered, boxes), table_ref, placed, boxes, sums_ref[...])
    for n, group in enumerate((0, 2)):
        values = read_windows(group, gathered, boxes)
        for i in range(BX):
            for tile in range(2):
                values_ref[n, i, tile] = values[i][tile]
    local[...] = along_z(field2, slice(96, 480), zst_ref).reshape(24, NY, NZ)
    nonlocal_[0:6] = jnp.zeros((6, NY, NZ), jnp.float32)
    nonlocal_[6:23] = spread_group(1, 0, 17, placed, own_hot)
    nonlocal_[23] = jnp.zeros((NY, NZ), jnp.float32)
    for n, source in enumerate((low_ref, high_ref)):
        spread_projectors(lambda part, a: source[TILE_P + 16 * part + a], work, half_ref.at[n])
    for p in range(24):
        laplace = stencil_plane(padded, p + 6) + local[p]
        pot = potential_plane(p, low_ref, pot_ref, high_ref)
        partial_ref[p] = (-0.5 * laplace + (pot - CENTER) * padded[p + 6, 8:24, :] + nonlocal_[p]) * (1.0 / HALF)


def second_step(boxes, hots, padded1, field2, gathered, placed, local, nonlocal_, pot_ref, tables, zst_ref, sums):
    for group, first, planes, skip in ((0, 0, 11, 6), (1, 6, SPAN, 0)):
        gather_columns(group, field2, first, planes, skip, gathered, hots[group])
    for group in range(2):
        contributions(group, read_windows(group, gathered, boxes), tables[group], placed, boxes, sums)
    local[0:12] = along_z(field2, slice(96, 288), zst_ref).reshape(12, NY, NZ)
    nonlocal_[0:12] = spread_group(1, 0, 12, placed, hots[1])
    nonlocal_[0:5] += spread_group(0, 12, 5, placed, hots[0])
    for p in range(12):
        here = padded1[p + 6, 8:24, :]
        laplace = stencil_plane(padded1, p + 6) + local[p]
        pot = potential_plane(p + 6, None, pot_ref, None)
        yield p, (-0.5 * laplace + (pot - CENTER) * here + nonlocal_[p]) * (2.0 / HALF)


def tail_kernel(up_ref, low_ref, high_ref, pot_ref, table_ref, zst_ref, sums_ref,
                half_ref, values_ref, partial_ref, lowsib_ref, highsib_ref,
                out_ref, kept_ref, tables_ref,
                low_xy, own_xy, high_xy, padded1, field2, gathered, placed, local, nonlocal_, work, sems):
    core = lax.axis_index("band") % 2
    boxes = Boxes((low_ref, up_ref, high_ref), (low_xy, own_xy, high_xy), sems)
    placed[...] = jnp.zeros_like(placed)
    gathered[0, :, 0:6] = jnp.zeros((2, 6, 24, 128), jnp.float32)
    for n, source in enumerate((lowsib_ref, highsib_ref)):
        spread_projectors(lambda part, a: source[TILE_P + 16 * part + a], work, tables_ref.at[n, 1 - core])
        tables_ref[n, core] = half_ref[n]
    hots = [boxes.one_hot(g) for g in range(3)]
    boxes.wait()
    sums = sums_ref[...]
    for n, group in enumerate((0, 2)):
        values = [[values_ref[n, i, tile] for tile in range(2)] for i in range(BX)]
        contributions(group, values, tables_ref.at[n], placed, boxes, sums)
    nonlocal_[0:11] = spread_group(0, 6, 11, placed, hots[0])
    nonlocal_[11:18] = jnp.zeros((7, NY, NZ), jnp.float32)
    nonlocal_[18:24] = spread_group(2, 0, 6, placed, hots[2])
    for p in range(24):
        updated = partial_ref[p] + nonlocal_[p] * (1.0 / HALF)
        kept_ref[p] = updated
        fill(padded1, p, updated[None])
        field2[16 * p : 16 * p + 16, :] = two_terms(updated, 1)
    tables = (tables_ref.at[0], table_ref)
    for p, value in second_step(boxes, hots, padded1, field2, gathered, placed, local, nonlocal_, pot_ref, tables,
                                zst_ref, sums):
        out_ref[2 * p : 2 * p + 2] = (value - up_ref[TILE_Y + 2 * p : TILE_Y + 2 * p + 2].reshape(NY, NZ)).reshape(2, 8, 128)


def last_kernel(up_ref, low_ref, high_ref, pot_ref, table_ref, zst_ref, sums_ref, kept_ref, tables_ref,
                mid_ref, lowy_ref, highy_ref,
                out_ref,
                low_xy, own_xy, high_xy, padded, padded1, field2, gathered, placed, local, nonlocal_, sems):
    boxes = Boxes((low_ref, up_ref, high_ref), (low_xy, own_xy, high_xy), sems)
    load_fields([r[...] for r in (lowy_ref, mid_ref, highy_ref)], padded, field2)
    placed[...] = jnp.zeros_like(placed)
    gathered[2, :, 12:SPAN] = jnp.zeros((2, SPAN - 12, 24, 128), jnp.float32)
    hots = [boxes.one_hot(g) for g in range(3)]
    boxes.wait()
    sums = sums_ref[...]
    tables = (tables_ref.at[0], table_ref, tables_ref.at[1])
    for group, planes in ((0, SPAN), (1, SPAN), (2, 12)):
        gather_columns(group, field2, 12 * group, planes, 0, gathered, hots[group])
    for group in range(3):
        contributions(group, read_windows(group, gathered, boxes), tables[group], placed, boxes, sums)
    local[...] = along_z(field2, slice(96, 480), zst_ref).reshape(24, NY, NZ)
    nonlocal_[0:11] = spread_group(0, 6, 11, placed, hots[0])
    nonlocal_[11:24] = jnp.zeros((13, NY, NZ), jnp.float32)
    nonlocal_[6:23] += spread_group(1, 0, 17, placed, hots[1])
    nonlocal_[18:24] += spread_group(2, 0, 6, placed, hots[2])
    for p in range(24):
        laplace = stencil_plane(padded, p + 6) + local[p]
        pot = potential_plane(p, low_ref, pot_ref, high_ref)
        applied = -0.5 * laplace + (pot - CENTER) * padded[p + 6, 8:24, :] + nonlocal_[p]
        updated = applied * (2.0 / HALF) - kept_ref[p]
        fill(padded1, p, updated[None])
        field2[16 * p : 16 * p + 16, :] = two_terms(updated, 1)
    for p, value in second_step(boxes, hots, padded1, field2, gathered, placed, local, nonlocal_, pot_ref, tables,
                                zst_ref, sums):
        out_ref[2 * p : 2 * p + 2] = (value - padded[p + 12, 8:24, :]).reshape(2, 8, 128)


XY = [pltpu.SMEM((8, 128), jnp.float32)] * 3
PADDED = pltpu.VMEM((36, 32, NZ), jnp.float32)
PADDED1 = pltpu.VMEM((24, 32, NZ), jnp.float32)
FIELD2 = pltpu.VMEM((576, 2 * NZ), jnp.bfloat16)
BOXED = pltpu.VMEM((3, 2, SPAN, 24, 128), jnp.float32)
PLANES = pltpu.VMEM((24, NY, NZ), jnp.float32)
WORK = pltpu.VMEM((BX, BY * NPROJ, 128), jnp.float32)
COPIES = pltpu.SemaphoreType.DMA((3,))


def parts_kernel(ritz_ref, own_ref, other_ref, base_ref, one_ref, two_ref, three_ref, out_hbm, sem):
    copy = pltpu.make_async_copy(own_ref, out_hbm, sem.at[0])
    copy.start()
    band = lax.axis_index("band")
    for hop, target in enumerate((base_ref, one_ref, two_ref, three_ref)):
        to = band ^ (2 * hop)
        target[...] = ritz_ref[band, to] * own_ref[...] + ritz_ref[band ^ 1, to] * other_ref[...]
    copy.wait()


def total_kernel(base_ref, one_ref, two_ref, three_ref, out_ref):
    out_ref[...] = (base_ref[...] + one_ref[...]) + (two_ref[...] + three_ref[...])


def ring(axis, step):
    count = lax.axis_size(axis)
    return [(i, (i + step) % count) for i in range(count)]


def meet(axis, bits):
    return [(i, i ^ bits) for i in range(lax.axis_size(axis))]


def shards(orbitals, potential, atom_pos, atom_count, projectors, gammas, ritz):
    up, down, pot, proj = call(
        pack_kernel,
        [shape(TILES, 8, 128), shape(TILES, 8, 128), shape(24, 8, 128), shape(3 * ATOMS, 8, 128)],
        [HBM] * 5 + [SMEM],
        (orbitals.reshape(24, 8, 128), potential.reshape(24, 8, 128), projectors, gammas.T, atom_pos.T, atom_count),
        "pack",
        [pltpu.VMEM((NPROJ, ATOMS), jnp.float32), pltpu.VMEM((3, ATOMS), jnp.int32), pltpu.SemaphoreType.DMA((16,))],
    )
    low = lax.ppermute(up, "dom", ring("dom", 1))
    high = lax.ppermute(down, "dom", ring("dom", -1))
    table, zst, sums = call(
        prepare_kernel,
        [shape(2, PAIRS, 8, 128), shape(384, NZ, dtype=jnp.bfloat16), shape(LANES, LANES, dtype=jnp.bfloat16)],
        [VMEM],
        (proj,),
        "prepare",
        [WORK],
    )
    lowsib = lax.ppermute(low, "band", meet("band", 1))
    highsib = lax.ppermute(high, "band", meet("band", 1))
    common = (up, low, high, pot, table, zst, sums)
    halves, values, partial = call(
        head_kernel,
        [shape(2, PAIRS, 8, 128), shape(2, BX, 2, 8, 128), shape(24, NY, NZ)],
        [VMEM] * 7,
        common,
        "head",
        XY + [PADDED, FIELD2, BOXED, BOXED, PLANES, PLANES, WORK, COPIES],
    )
    second, first, tables = call(
        tail_kernel,
        [shape(24, 8, 128), shape(24, NY, NZ), shape(2, 2, PAIRS, 8, 128)],
        [VMEM] * 12,
        common + (halves, values, partial, lowsib, highsib),
        "tail",
        XY + [PADDED1, FIELD2, BOXED, BOXED, PLANES, PLANES, WORK, COPIES],
    )
    low_y = lax.ppermute(second, "dom", ring("dom", 1))
    high_y = lax.ppermute(second, "dom", ring("dom", -1))
    (fourth,) = call(
        last_kernel,
        [shape(24, 8, 128)],
        [VMEM] * 12,
        common + (first, tables, second, low_y, high_y),
        "last",
        XY + [PADDED, PADDED1, FIELD2, BOXED, BOXED, PLANES, PLANES, COPIES],
    )
    other = lax.ppermute(fourth, "band", meet("band", 1))
    field = shape(24, 8, 128)
    base, one, two, three, filtered = call(
        parts_kernel,
        [field] * 5,
        [SMEM, VMEM, VMEM],
        (ritz, fourth, other),
        "parts",
        [pltpu.SemaphoreType.DMA((1,))],
        [VMEM] * 4 + [HBM],
    )
    arrived = [lax.ppermute(v, "band", meet("band", 2 * hop)) for hop, v in ((1, one), (2, two), (3, three))]
    (rotated,) = call(total_kernel, [field], [VMEM] * 4, (base, *arrived), "total")
    return (filtered.reshape(orbitals.shape), rotated.reshape(orbitals.shape))


def solution(mesh):
    in_specs = (
        P("band", "dom", None, None),
        P("dom", None, None),
        P("dom", None),
        P("dom"),
        P("dom", None, None),
        P("dom", None),
        P(),
    )
    out_specs = (P("band", "dom", None, None), P("band", "dom", None, None))
    return jax.shard_map(shards, mesh=mesh, in_specs=in_specs, out_specs=out_specs, check_vma=False)
```

```python
import jax
import jax.numpy as jnp
from jax import lax
from jax.experimental import pallas as pl
from jax.experimental.pallas import tpu as pltpu
from jax.sharding import PartitionSpec as P

STENCIL = (
    -5369.0 / 1800.0,
    12.0 / 7.0,
    -15.0 / 56.0,
    10.0 / 189.0,
    -1.0 / 112.0,
    2.0 / 1925.0,
    -1.0 / 16632.0,
)
LOWER = -1.6
UPPER = 24.0
CENTER = 0.5 * (UPPER + LOWER)
HALF = 0.5 * (UPPER - LOWER)

CX, NY, NZ = 12, 16, 128
ATOMS = 32
NPROJ, BX, BY, BZ = 8, 6, 8, 8
LANES = ATOMS * BZ
SPAN = CX + BX - 1
PAIRS = NPROJ * BX
TILE_Y, TILE_POT, TILE_P, TILE_META, TILES = 0, 24, 36, 84, 88
ROW_Z, ROW_X0, ROW_Y0 = 0, 1, 2

VMEM = pl.BlockSpec(memory_space=pltpu.VMEM)
HBM = pl.BlockSpec(memory_space=pltpu.HBM)
SMEM = pl.BlockSpec(memory_space=pltpu.SMEM)


def shape(*dims, dtype=jnp.float32):
    return jax.ShapeDtypeStruct(dims, dtype)


def call(kernel, outs, ins, args, name, scratch=(), out_specs=None, flops=1_000_000):
    return pl.pallas_call(
        kernel,
        out_shape=outs,
        in_specs=ins,
        out_specs=out_specs or [VMEM] * len(outs),
        scratch_shapes=list(scratch),
        compiler_params=pltpu.CompilerParams(vmem_limit_bytes=32 * 2**20),
        cost_estimate=pl.CostEstimate(flops=flops, bytes_accessed=2_000_000, transcendentals=0),
        name=name,
    )(*args)


def two_terms(value, axis):
    high = value.astype(jnp.bfloat16)
    low = (value - high.astype(jnp.float32)).astype(jnp.bfloat16)
    return jnp.concatenate([high, low], axis)


def dot(left, right):
    return jnp.dot(left, right, preferred_element_type=jnp.float32)


def half(tile):
    return slice(128 * tile, 128 * tile + 128)


def pack_kernel(y_hbm, pot_hbm, proj_hbm, gamma_hbm, pos_hbm, count_ref,
                up_ref, down_ref, pot_ref, proj_ref, gamma_ref, pos_ref, sems):
    core = lax.axis_index("band") % 2
    first = 16 * core
    copies = [
        pltpu.make_async_copy(gamma_hbm, gamma_ref, sems.at[0]),
        pltpu.make_async_copy(pos_hbm, pos_ref, sems.at[1]),
    ]
    moves = [
        (pot_hbm, pot_ref),
        (pot_hbm.at[pl.ds(12, 12)], up_ref.at[pl.ds(TILE_POT, 12)]),
        (pot_hbm.at[pl.ds(0, 12)], down_ref.at[pl.ds(TILE_POT, 12)]),
    ]
    for out in (up_ref, down_ref):
        moves.append((y_hbm, out.at[pl.ds(TILE_Y, 24)]))
        for part in range(3):
            source = proj_hbm.at[pl.ds(first, 16), pl.ds(0, 8), pl.ds(128 * part, 128)]
            moves.append((source, out.at[pl.ds(TILE_P + 16 * part, 16)]))
    for part in range(3):
        source = proj_hbm.at[pl.ds(0, ATOMS), pl.ds(0, 8), pl.ds(128 * part, 128)]
        moves.append((source, proj_ref.at[pl.ds(ATOMS * part, ATOMS)]))
    for n, (source, target) in enumerate(moves):
        copies.append(pltpu.make_async_copy(source, target, sems.at[2 + n]))
    for copy in copies:
        copy.start()
    copies[0].wait()
    copies[1].wait()
    live = lax.broadcasted_iota(jnp.int32, (1, ATOMS), 1) < count_ref[0]
    weight = jnp.where(live, gamma_ref[...], 0.0)
    repeat = lax.broadcasted_iota(jnp.int32, (ATOMS, LANES), 1) >> 3
    repeat = jnp.where(repeat == lax.broadcasted_iota(jnp.int32, (ATOMS, LANES), 0), 1.0, 0.0)
    corner = pos_ref[...].astype(jnp.float32)
    spread = lambda v: jnp.dot(v, repeat, preferred_element_type=jnp.float32, precision=lax.Precision.HIGHEST)
    weight = spread(weight)
    column = spread(corner)[2:3] + (lax.broadcasted_iota(jnp.int32, (1, LANES), 1) & 7).astype(jnp.float32)
    column = jnp.where(column >= NZ, column - NZ, column)
    for out in (up_ref, down_ref):
        for tile in range(2):
            out[TILE_META + 2 * tile] = weight[:, half(tile)]
            out[TILE_META + 2 * tile + 1] = jnp.broadcast_to(column[:, half(tile)], (8, 128))
        out[TILE_META + 1, ROW_X0 : ROW_X0 + 1, 0:ATOMS] = corner[0:1]
        out[TILE_META + 1, ROW_Y0 : ROW_Y0 + 1, 0:ATOMS] = corner[1:2]
    for copy in copies[2:]:
        copy.wait()


def spread_projectors(read, work, table):
    lane = lax.broadcasted_iota(jnp.int32, (8, 128), 1)
    for part in range(3):
        items = [read(part, a) for a in range(16)]
        for bit in (1, 2, 4, 8):
            upper = (lane & (8 * bit)) != 0
            for p in range(16):
                if p & bit:
                    continue
                q = p | bit
                first, second = items[p], items[q]
                items[p] = jnp.where(upper, pltpu.roll(second, 8 * bit, 1), first)
                items[q] = jnp.where(upper, second, pltpu.roll(first, 128 - 8 * bit, 1))
        for g in range(16):
            i, j = 2 * part + g // 8, g % 8
            work[i, 8 * j : 8 * j + 8, :] = items[g]
    for i in range(BX):
        for l in range(NPROJ):
            table[l * BX + i] = work.at[i][pl.ds(l, 8, stride=8), :]


def prepare_kernel(proj_ref, ritz_ref, table_ref, zst_ref, sums_ref, factors_ref, work):
    band = lax.axis_index("band")
    row = lax.broadcasted_iota(jnp.int32, (8, 8), 0)
    column = lax.broadcasted_iota(jnp.int32, (8, 8), 1)
    for hop in range(4):
        for n, orbital in enumerate((band, band ^ 1)):
            picked = jnp.where((row == orbital) & (column == band ^ (2 * hop)), ritz_ref[...], 0.0)
            picked = jnp.sum(jnp.sum(picked, 1, keepdims=True), 0, keepdims=True)
            factors_ref[2 * hop + n] = jnp.broadcast_to(picked, (8, 128))
    for tile in range(2):
        read = lambda part, a: proj_ref[ATOMS * part + 16 * tile + a]
        spread_projectors(read, work, table_ref.at[tile])
    apart = lax.broadcasted_iota(jnp.int32, (NZ, NZ), 0) - lax.broadcasted_iota(jnp.int32, (NZ, NZ), 1)
    full = jnp.zeros((NZ, NZ), jnp.float32)
    for reach in range(1, 7):
        near = ((apart & (NZ - 1)) == reach) | ((apart & (NZ - 1)) == NZ - reach)
        full = jnp.where(near, STENCIL[reach], full)
    high = full.astype(jnp.bfloat16)
    zst_ref[0:128, :] = high
    zst_ref[128:256, :] = high
    zst_ref[256:384, :] = (full - high.astype(jnp.float32)).astype(jnp.bfloat16)
    atom = lambda axis: lax.broadcasted_iota(jnp.int32, (LANES, LANES), axis) >> 3
    sums_ref[...] = jnp.where(atom(0) == atom(1), 1.0, 0.0).astype(jnp.bfloat16)


def fill(padded, plane, value):
    count = value.shape[0]
    padded[plane : plane + count, 8:24, :] = value
    padded[plane : plane + count, 0:8, :] = value[:, 8:16]
    padded[plane : plane + count, 24:32, :] = value[:, 0:8]


class Boxes:
    def __init__(self, sources, held, sems):
        self.sources, self.held = sources, held
        self.copies = [
            pltpu.make_async_copy(s.at[TILE_META + 1], h, sems.at[n]) for n, (s, h) in enumerate(zip(sources, held))
        ]
        for copy in self.copies:
            copy.start()

    def wait(self):
        for copy in self.copies:
            copy.wait()

    def place(self, group, atom):
        held = self.held[group]
        return held[ROW_X0, atom].astype(jnp.int32), held[ROW_Y0, atom].astype(jnp.int32)

    def weight(self, group):
        source = self.sources[group]
        return jnp.concatenate([source[TILE_META], source[TILE_META + 2]], 1)

    def one_hot(self, group):
        source = self.sources[group]
        column = jnp.concatenate(
            [source[TILE_META + 1 + 2 * t, ROW_Z : ROW_Z + 1, :] for t in range(2)], 1
        )
        cells = lax.broadcasted_iota(jnp.int32, (NZ, LANES), 0).astype(jnp.float32)
        return jnp.where(cells == column, 1.0, 0.0).astype(jnp.bfloat16)


def gather_columns(group, field2, first_in, planes_in, skip, gathered, onehot):
    rows = slice(NY * first_in, NY * (first_in + planes_in))
    columns = dot(field2[rows, :], jnp.concatenate([onehot, onehot], 0)).reshape(planes_in, NY, LANES)
    for tile in range(2):
        part = columns[:, :, half(tile)]
        gathered[group][tile, skip : skip + planes_in, 0:16, :] = part
        gathered[group][tile, skip : skip + planes_in, 16:24, :] = part[:, 0:8]


def read_windows(group, gathered, boxes):
    lane = lax.broadcasted_iota(jnp.int32, (8, 128), 1)
    values = [[jnp.zeros((8, 128), jnp.float32)] * 2 for _ in range(BX)]
    for a in range(16):
        mine = (lane >> 3) == a
        for tile in range(2):
            x0, y0 = boxes.place(group, 16 * tile + a)
            for i in range(BX):
                values[i][tile] = jnp.where(mine, gathered[group][tile, x0 + i, pl.ds(y0, 8), :], values[i][tile])
    return values


def contributions(group, values, table, placed, boxes, sums):
    coeffs = []
    for tile in range(2):
        rows = []
        for l in range(NPROJ):
            total = values[0][tile] * table[tile, l * BX]
            for i in range(1, BX):
                total = total + values[i][tile] * table[tile, l * BX + i]
            rows.append(jnp.sum(total, 0, keepdims=True))
        coeffs.append(jnp.concatenate(rows, 0))
    both = dot(two_terms(jnp.concatenate(coeffs, 1), 0), sums)
    coeffs = (both[:8] + both[8:]) * boxes.weight(group)
    lane = lax.broadcasted_iota(jnp.int32, (8, 128), 1)
    contrib = [[None] * 2 for _ in range(BX)]
    for tile in range(2):
        rows = [jnp.broadcast_to(coeffs[l : l + 1, half(tile)], (8, 128)) for l in range(NPROJ)]
        for i in range(BX):
            total = rows[0] * table[tile, i]
            for l in range(1, NPROJ):
                total = total + rows[l] * table[tile, l * BX + i]
            contrib[i][tile] = total
    for a in range(16):
        mine = (lane >> 3) == a
        for tile in range(2):
            x0, y0 = boxes.place(group, 16 * tile + a)
            for i in range(BX):
                pltpu.store(placed[group].at[tile, x0 + i, pl.ds(y0, 8), :], contrib[i][tile], mask=mine)


def spread_group(group, first, count, placed, onehot):
    planes = slice(first, first + count)
    tiles = []
    for tile in range(2):
        folded = placed[group][tile, planes, 0:8, :] + placed[group][tile, planes, 16:24, :]
        tiles.append(jnp.concatenate([folded, placed[group][tile, planes, 8:16, :]], 1).reshape(count * NY, 128))
    twice = jnp.concatenate([onehot, onehot], 1)
    spread = lax.dot_general(
        two_terms(jnp.concatenate(tiles, 1), 1), twice, (((1,), (1,)), ((), ())),
        preferred_element_type=jnp.float32,
    )
    return spread.reshape(count, NY, NZ)


def along_z(field2, rows, zst_ref):
    return dot(field2[rows, :], zst_ref[0:256, :]) + dot(field2[rows, 0:128], zst_ref[256:384, :])


def stencil_plane(padded, plane):
    total = 3.0 * STENCIL[0] * padded[plane, 8:24, :]
    for reach in range(1, 7):
        along_x = padded[plane + reach, 8:24, :] + padded[plane - reach, 8:24, :]
        along_y = padded[plane, 8 + reach : 24 + reach, :] + padded[plane, 8 - reach : 24 - reach, :]
        total = total + STENCIL[reach] * (along_x + along_y)
    return total


def potential_plane(p, low_ref, pot_ref, high_ref):
    source, tile = (
        (low_ref, TILE_POT + 2 * p) if p < 6 else (pot_ref, 2 * (p - 6)) if p < 18 else (high_ref, TILE_POT + 2 * (p - 18))
    )
    return source[tile : tile + 2].reshape(NY, NZ)


def clear(boxed):
    for ref in boxed:
        ref[...] = jnp.zeros_like(ref)


def load_fields(fields, padded, field2):
    for n, value in enumerate(fields):
        fill(padded, 12 * n, value.reshape(CX, NY, NZ))
        field2[192 * n : 192 * n + 192, :] = two_terms(value.reshape(192, NZ), 1)


def head_kernel(up_ref, low_ref, high_ref, pot_ref, table_ref, zst_ref, sums_ref,
                half_ref, values_ref, partial_ref,
                low_xy, own_xy, high_xy, padded, field2, gathered, placed, local, work, sems):
    boxes = Boxes((low_ref, up_ref, high_ref), (low_xy, own_xy, high_xy), sems)
    load_fields([r[TILE_Y : TILE_Y + 24] for r in (low_ref, up_ref, high_ref)], padded, field2)
    clear(placed)
    gathered[2][:, 12:SPAN] = jnp.zeros((2, SPAN - 12, 24, 128), jnp.float32)
    own_hot = boxes.one_hot(1)
    gather_columns(1, field2, 12, SPAN, 0, gathered, own_hot)
    gather_columns(0, field2, 0, SPAN, 0, gathered, boxes.one_hot(0))
    gather_columns(2, field2, 24, 12, 0, gathered, boxes.one_hot(2))
    local[...] = along_z(field2, slice(96, 480), zst_ref).reshape(24, NY, NZ)
    for p in range(24):
        laplace = stencil_plane(padded, p + 6) + local[p]
        pot = potential_plane(p, low_ref, pot_ref, high_ref)
        local[p] = (-0.5 * laplace + (pot - CENTER) * padded[p + 6, 8:24, :]) * (1.0 / HALF)
    for n, source in enumerate((low_ref, high_ref)):
        spread_projectors(lambda part, a: source[TILE_P + 16 * part + a], work, half_ref.at[n])
    boxes.wait()
    contributions(1, read_windows(1, gathered, boxes), table_ref, placed, boxes, sums_ref[...])
    for n, group in enumerate((0, 2)):
        values = read_windows(group, gathered, boxes)
        for i in range(BX):
            for tile in range(2):
                values_ref[n, i, tile] = values[i][tile]
    partial_ref[0:6] = local[0:6]
    partial_ref[6:23] = local[6:23] + spread_group(1, 0, 17, placed, own_hot) * (1.0 / HALF)
    partial_ref[23] = local[23]


def second_step(boxes, hots, padded1, field2, gathered, placed, local, nonlocal_, pot_ref, tables, zst_ref, sums):
    for group, first, planes, skip in ((0, 0, 11, 6), (1, 6, SPAN, 0)):
        gather_columns(group, field2, first, planes, skip, gathered, hots[group])
    for group in range(2):
        contributions(group, read_windows(group, gathered, boxes), tables[group], placed, boxes, sums)
    local[0:12] = along_z(field2, slice(96, 288), zst_ref).reshape(12, NY, NZ)
    for p in range(12):
        here = padded1[p + 6, 8:24, :]
        laplace = stencil_plane(padded1, p + 6) + local[p]
        pot = potential_plane(p + 6, None, pot_ref, None)
        local[p] = -0.5 * laplace + (pot - CENTER) * here
    nonlocal_[0:12] = spread_group(1, 0, 12, placed, hots[1])
    nonlocal_[0:5] += spread_group(0, 12, 5, placed, hots[0])
    for p in range(12):
        yield p, (local[p] + nonlocal_[p]) * (2.0 / HALF)


def tail_kernel(up_ref, low_ref, high_ref, pot_ref, table_ref, zst_ref, sums_ref,
                half_ref, values_ref, partial_ref, lowsib_ref, highsib_ref,
                out_ref, kept_ref, tables_ref,
                low_xy, own_xy, high_xy, padded1, field2, gathered, placed, local, nonlocal_, work, sems):
    core = lax.axis_index("band") % 2
    boxes = Boxes((low_ref, up_ref, high_ref), (low_xy, own_xy, high_xy), sems)
    clear(placed)
    gathered[0][:, 0:6] = jnp.zeros((2, 6, 24, 128), jnp.float32)
    for n, source in enumerate((lowsib_ref, highsib_ref)):
        spread_projectors(lambda part, a: source[TILE_P + 16 * part + a], work, tables_ref.at[n, 1 - core])
        tables_ref[n, core] = half_ref[n]
    hots = [boxes.one_hot(g) for g in range(3)]
    boxes.wait()
    sums = sums_ref[...]
    for n, group in enumerate((0, 2)):
        values = [[values_ref[n, i, tile] for tile in range(2)] for i in range(BX)]
        contributions(group, values, tables_ref.at[n], placed, boxes, sums)
    nonlocal_[0:11] = spread_group(0, 6, 11, placed, hots[0])
    nonlocal_[11:18] = jnp.zeros((7, NY, NZ), jnp.float32)
    nonlocal_[18:24] = spread_group(2, 0, 6, placed, hots[2])
    for p in range(24):
        updated = partial_ref[p] + nonlocal_[p] * (1.0 / HALF)
        kept_ref[p] = updated
        fill(padded1, p, updated[None])
        field2[16 * p : 16 * p + 16, :] = two_terms(updated, 1)
    tables = (tables_ref.at[0], table_ref)
    for p, value in second_step(boxes, hots, padded1, field2, gathered, placed, local, nonlocal_, pot_ref, tables,
                                zst_ref, sums):
        out_ref[2 * p : 2 * p + 2] = (value - up_ref[TILE_Y + 2 * p : TILE_Y + 2 * p + 2].reshape(NY, NZ)).reshape(2, 8, 128)


def last_kernel(up_ref, low_ref, high_ref, pot_ref, table_ref, zst_ref, sums_ref, kept_ref, tables_ref,
                mid_ref, lowy_ref, highy_ref,
                out_ref,
                low_xy, own_xy, high_xy, padded, padded1, field2, gathered, placed, local, nonlocal_, sems):
    boxes = Boxes((low_ref, up_ref, high_ref), (low_xy, own_xy, high_xy), sems)
    load_fields([r[...] for r in (lowy_ref, mid_ref, highy_ref)], padded, field2)
    clear(placed)
    gathered[2][:, 12:SPAN] = jnp.zeros((2, SPAN - 12, 24, 128), jnp.float32)
    hots = [boxes.one_hot(g) for g in range(3)]
    sums = sums_ref[...]
    tables = (tables_ref.at[0], table_ref, tables_ref.at[1])
    for group, planes in ((0, SPAN), (1, SPAN), (2, 12)):
        gather_columns(group, field2, 12 * group, planes, 0, gathered, hots[group])
    local[...] = along_z(field2, slice(96, 480), zst_ref).reshape(24, NY, NZ)
    for p in range(24):
        laplace = stencil_plane(padded, p + 6) + local[p]
        pot = potential_plane(p, low_ref, pot_ref, high_ref)
        applied = -0.5 * laplace + (pot - CENTER) * padded[p + 6, 8:24, :]
        local[p] = applied * (2.0 / HALF) - kept_ref[p]
    boxes.wait()
    windows = [read_windows(group, gathered, boxes) for group in range(3)]
    for group in range(3):
        contributions(group, windows[group], tables[group], placed, boxes, sums)
    nonlocal_[0:11] = spread_group(0, 6, 11, placed, hots[0])
    nonlocal_[11:24] = jnp.zeros((13, NY, NZ), jnp.float32)
    nonlocal_[6:23] += spread_group(1, 0, 17, placed, hots[1])
    nonlocal_[18:24] += spread_group(2, 0, 6, placed, hots[2])
    for p in range(24):
        updated = local[p] + nonlocal_[p] * (2.0 / HALF)
        fill(padded1, p, updated[None])
        field2[16 * p : 16 * p + 16, :] = two_terms(updated, 1)
    for p, value in second_step(boxes, hots, padded1, field2, gathered, placed, local, nonlocal_, pot_ref, tables,
                                zst_ref, sums):
        out_ref[2 * p : 2 * p + 2] = (value - padded[p + 12, 8:24, :]).reshape(2, 8, 128)


XY = [pltpu.SMEM((8, 128), jnp.float32)] * 3
PADDED = pltpu.VMEM((36, 32, NZ), jnp.float32)
PADDED1 = pltpu.VMEM((24, 32, NZ), jnp.float32)
FIELD2 = pltpu.VMEM((576, 2 * NZ), jnp.bfloat16)
BOXED = [pltpu.VMEM((2, SPAN, 24, 128), jnp.float32)] * 3
PLANES = pltpu.VMEM((24, NY, NZ), jnp.float32)
WORK = pltpu.VMEM((BX, BY * NPROJ, 128), jnp.float32)
COPIES = pltpu.SemaphoreType.DMA((3,))


def parts_kernel(factors_ref, own_ref, other_ref, base_ref, one_ref, two_ref, three_ref):
    own, other = own_ref[...], other_ref[...]
    for hop, target in enumerate((base_ref, one_ref, two_ref, three_ref)):
        target[...] = factors_ref[2 * hop] * own + factors_ref[2 * hop + 1] * other


def store_kernel(own_ref, out_ref):
    out_ref[...] = own_ref[...]


def total_kernel(base_ref, one_ref, two_ref, three_ref, out_ref):
    out_ref[...] = (base_ref[...] + one_ref[...]) + (two_ref[...] + three_ref[...])


def ring(axis, step):
    count = lax.axis_size(axis)
    return [(i, (i + step) % count) for i in range(count)]


def meet(axis, bits):
    return [(i, i ^ bits) for i in range(lax.axis_size(axis))]


def shards(orbitals, potential, atom_pos, atom_count, projectors, gammas, ritz):
    stay = lambda v: pltpu.with_memory_space_constraint(v, pltpu.HBM)
    up, down, pot, proj = call(
        pack_kernel,
        [shape(TILES, 8, 128), shape(TILES, 8, 128), shape(24, 8, 128), shape(3 * ATOMS, 8, 128)],
        [HBM] * 5 + [SMEM],
        (
            stay(orbitals.reshape(24, 8, 128)),
            stay(potential.reshape(24, 8, 128)),
            stay(projectors),
            stay(gammas.T),
            stay(atom_pos.T),
            atom_count,
        ),
        "pack",
        [pltpu.VMEM((NPROJ, ATOMS), jnp.float32), pltpu.VMEM((3, ATOMS), jnp.int32), pltpu.SemaphoreType.DMA((16,))],
    )
    low = lax.ppermute(up, "dom", ring("dom", 1))
    high = lax.ppermute(down, "dom", ring("dom", -1))
    table, zst, sums, factors = call(
        prepare_kernel,
        [
            shape(2, PAIRS, 8, 128),
            shape(384, NZ, dtype=jnp.bfloat16),
            shape(LANES, LANES, dtype=jnp.bfloat16),
            shape(8, 8, 128),
        ],
        [VMEM] * 2,
        (proj, ritz),
        "prepare",
        [WORK],
    )
    lowsib = lax.ppermute(low, "band", meet("band", 1))
    highsib = lax.ppermute(high, "band", meet("band", 1))
    common = (up, low, high, pot, table, zst, sums)
    halves, values, partial = call(
        head_kernel,
        [shape(2, PAIRS, 8, 128), shape(2, BX, 2, 8, 128), shape(24, NY, NZ)],
        [VMEM] * 7,
        common,
        "head",
        XY + [PADDED, FIELD2, BOXED, BOXED, PLANES, WORK, COPIES],
        flops=10_000_000_000,
    )
    second, first, tables = call(
        tail_kernel,
        [shape(24, 8, 128), shape(24, NY, NZ), shape(2, 2, PAIRS, 8, 128)],
        [VMEM] * 12,
        common + (halves, values, partial, lowsib, highsib),
        "tail",
        XY + [PADDED1, FIELD2, BOXED, BOXED, PLANES, PLANES, WORK, COPIES],
    )
    low_y = lax.ppermute(second, "dom", ring("dom", 1))
    high_y = lax.ppermute(second, "dom", ring("dom", -1))
    (fourth,) = call(
        last_kernel,
        [shape(24, 8, 128)],
        [VMEM] * 12,
        common + (first, tables, second, low_y, high_y),
        "last",
        XY + [PADDED, PADDED1, FIELD2, BOXED, BOXED, PLANES, PLANES, COPIES],
    )
    other = lax.ppermute(fourth, "band", meet("band", 1))
    field = shape(24, 8, 128)
    base, one, two, three = call(
        parts_kernel, [field] * 4, [VMEM] * 3, (factors, fourth, other), "parts"
    )
    arrived = [lax.ppermute(v, "band", meet("band", 2 * hop)) for hop, v in ((2, two), (1, one), (3, three))]
    (filtered,) = call(store_kernel, [field], [VMEM], (fourth,), "store")
    (rotated,) = call(total_kernel, [field], [VMEM] * 4, (base, *arrived), "total")
    return (filtered.reshape(orbitals.shape), rotated.reshape(orbitals.shape))


def solution(mesh):
    in_specs = (
        P("band", "dom", None, None),
        P("dom", None, None),
        P("dom", None),
        P("dom"),
        P("dom", None, None),
        P("dom", None),
        P(),
    )
    out_specs = (P("band", "dom", None, None), P("band", "dom", None, None))
    return jax.shard_map(shards, mesh=mesh, in_specs=in_specs, out_specs=out_specs, check_vma=False)
```

```python
import jax
import jax.numpy as jnp
from jax import lax
from jax.experimental import pallas as pl
from jax.experimental.pallas import tpu as pltpu
from jax.sharding import PartitionSpec as P

STENCIL = (
    -5369.0 / 1800.0,
    12.0 / 7.0,
    -15.0 / 56.0,
    10.0 / 189.0,
    -1.0 / 112.0,
    2.0 / 1925.0,
    -1.0 / 16632.0,
)
LOWER = -1.6
UPPER = 24.0
CENTER = 0.5 * (UPPER + LOWER)
HALF = 0.5 * (UPPER - LOWER)

CX, NY, NZ = 12, 16, 128
ATOMS = 32
NPROJ, BX, BY, BZ = 8, 6, 8, 8
LANES = ATOMS * BZ
SPAN = CX + BX - 1
PAIRS = NPROJ * BX
TILE_Y, TILE_POT, TILE_P, TILE_META, TILES = 0, 24, 36, 84, 88
ROW_Z, ROW_X0, ROW_Y0 = 0, 1, 2

VMEM = pl.BlockSpec(memory_space=pltpu.VMEM)
HBM = pl.BlockSpec(memory_space=pltpu.HBM)
SMEM = pl.BlockSpec(memory_space=pltpu.SMEM)


def shape(*dims, dtype=jnp.float32):
    return jax.ShapeDtypeStruct(dims, dtype)


def call(kernel, outs, ins, args, name, scratch=(), out_specs=None, flops=1_000_000):
    return pl.pallas_call(
        kernel,
        out_shape=outs,
        in_specs=ins,
        out_specs=out_specs or [VMEM] * len(outs),
        scratch_shapes=list(scratch),
        compiler_params=pltpu.CompilerParams(vmem_limit_bytes=32 * 2**20),
        cost_estimate=pl.CostEstimate(flops=flops, bytes_accessed=2_000_000, transcendentals=0),
        name=name,
    )(*args)


def two_terms(value, axis):
    high = value.astype(jnp.bfloat16)
    low = (value - high.astype(jnp.float32)).astype(jnp.bfloat16)
    return jnp.concatenate([high, low], axis)


def dot(left, right):
    return jnp.dot(left, right, preferred_element_type=jnp.float32)


def half(tile):
    return slice(128 * tile, 128 * tile + 128)


def pack_kernel(y_hbm, pot_hbm, proj_hbm, gamma_hbm, pos_hbm, count_ref,
                up_ref, down_ref, pot_ref, proj_ref, gamma_ref, pos_ref, sems):
    core = lax.axis_index("band") % 2
    first = 16 * core
    copies = [
        pltpu.make_async_copy(gamma_hbm, gamma_ref, sems.at[0]),
        pltpu.make_async_copy(pos_hbm, pos_ref, sems.at[1]),
    ]
    moves = [
        (pot_hbm, pot_ref),
        (pot_hbm.at[pl.ds(12, 12)], up_ref.at[pl.ds(TILE_POT, 12)]),
        (pot_hbm.at[pl.ds(0, 12)], down_ref.at[pl.ds(TILE_POT, 12)]),
    ]
    for out in (up_ref, down_ref):
        moves.append((y_hbm, out.at[pl.ds(TILE_Y, 24)]))
        for part in range(3):
            source = proj_hbm.at[pl.ds(first, 16), pl.ds(0, 8), pl.ds(128 * part, 128)]
            moves.append((source, out.at[pl.ds(TILE_P + 16 * part, 16)]))
    for part in range(3):
        source = proj_hbm.at[pl.ds(0, ATOMS), pl.ds(0, 8), pl.ds(128 * part, 128)]
        moves.append((source, proj_ref.at[pl.ds(ATOMS * part, ATOMS)]))
    for n, (source, target) in enumerate(moves):
        copies.append(pltpu.make_async_copy(source, target, sems.at[2 + n]))
    for copy in copies:
        copy.start()
    copies[0].wait()
    copies[1].wait()
    live = lax.broadcasted_iota(jnp.int32, (1, ATOMS), 1) < count_ref[0]
    weight = jnp.where(live, gamma_ref[...], 0.0)
    repeat = lax.broadcasted_iota(jnp.int32, (ATOMS, LANES), 1) >> 3
    repeat = jnp.where(repeat == lax.broadcasted_iota(jnp.int32, (ATOMS, LANES), 0), 1.0, 0.0)
    corner = pos_ref[...].astype(jnp.float32)
    spread = lambda v: jnp.dot(v, repeat, preferred_element_type=jnp.float32, precision=lax.Precision.HIGHEST)
    weight = spread(weight)
    column = spread(corner)[2:3] + (lax.broadcasted_iota(jnp.int32, (1, LANES), 1) & 7).astype(jnp.float32)
    column = jnp.where(column >= NZ, column - NZ, column)
    for out in (up_ref, down_ref):
        for tile in range(2):
            out[TILE_META + 2 * tile] = weight[:, half(tile)]
            out[TILE_META + 2 * tile + 1] = jnp.broadcast_to(column[:, half(tile)], (8, 128))
        out[TILE_META + 1, ROW_X0 : ROW_X0 + 1, 0:ATOMS] = corner[0:1]
        out[TILE_META + 1, ROW_Y0 : ROW_Y0 + 1, 0:ATOMS] = corner[1:2]
    for copy in copies[2:]:
        copy.wait()


def spread_projectors(read, work, table):
    lane = lax.broadcasted_iota(jnp.int32, (8, 128), 1)
    for part in range(3):
        items = [read(part, a) for a in range(16)]
        for bit in (1, 2, 4, 8):
            upper = (lane & (8 * bit)) != 0
            for p in range(16):
                if p & bit:
                    continue
                q = p | bit
                first, second = items[p], items[q]
                items[p] = jnp.where(upper, pltpu.roll(second, 8 * bit, 1), first)
                items[q] = jnp.where(upper, second, pltpu.roll(first, 128 - 8 * bit, 1))
        for g in range(16):
            i, j = 2 * part + g // 8, g % 8
            work[i, 8 * j : 8 * j + 8, :] = items[g]
    for i in range(BX):
        for l in range(NPROJ):
            table[l * BX + i] = work.at[i][pl.ds(l, 8, stride=8), :]


def prepare_kernel(proj_ref, up_ref, ritz_ref, table_ref, zst_ref, sums_ref, hot_ref, back_ref, factors_ref, work):
    write_one_hot(up_ref, hot_ref, back_ref)
    band = lax.axis_index("band")
    row = lax.broadcasted_iota(jnp.int32, (8, 8), 0)
    column = lax.broadcasted_iota(jnp.int32, (8, 8), 1)
    for hop in range(4):
        for n, orbital in enumerate((band, band ^ 1)):
            picked = jnp.where((row == orbital) & (column == band ^ (2 * hop)), ritz_ref[...], 0.0)
            picked = jnp.sum(jnp.sum(picked, 1, keepdims=True), 0, keepdims=True)
            factors_ref[2 * hop + n] = jnp.broadcast_to(picked, (8, 128))
    for tile in range(2):
        read = lambda part, a: proj_ref[ATOMS * part + 16 * tile + a]
        spread_projectors(read, work, table_ref.at[tile])
    apart = lax.broadcasted_iota(jnp.int32, (NZ, NZ), 0) - lax.broadcasted_iota(jnp.int32, (NZ, NZ), 1)
    full = jnp.zeros((NZ, NZ), jnp.float32)
    for reach in range(1, 7):
        near = ((apart & (NZ - 1)) == reach) | ((apart & (NZ - 1)) == NZ - reach)
        full = jnp.where(near, STENCIL[reach], full)
    high = full.astype(jnp.bfloat16)
    zst_ref[0:128, :] = high
    zst_ref[128:256, :] = high
    zst_ref[256:384, :] = (full - high.astype(jnp.float32)).astype(jnp.bfloat16)
    atom = lambda axis: lax.broadcasted_iota(jnp.int32, (LANES, LANES), axis) >> 3
    sums_ref[...] = jnp.where(atom(0) == atom(1), 1.0, 0.0).astype(jnp.bfloat16)


def fill(padded, plane, value):
    count = value.shape[0]
    padded[plane : plane + count, 8:24, :] = value
    padded[plane : plane + count, 0:8, :] = value[:, 8:16]
    padded[plane : plane + count, 24:32, :] = value[:, 0:8]


class Boxes:
    def __init__(self, sources, held, sems):
        self.sources, self.held = sources, held
        self.copies = [
            pltpu.make_async_copy(s.at[TILE_META + 1], h, sems.at[n]) for n, (s, h) in enumerate(zip(sources, held))
        ]
        for copy in self.copies:
            copy.start()

    def wait(self):
        for copy in self.copies:
            copy.wait()

    def place(self, group, atom):
        held = self.held[group]
        return held[ROW_X0, atom].astype(jnp.int32), held[ROW_Y0, atom].astype(jnp.int32)

    def weight(self, group):
        source = self.sources[group]
        return jnp.concatenate([source[TILE_META], source[TILE_META + 2]], 1)


def write_one_hot(source, hot_ref, back_ref):
    column = jnp.concatenate([source[TILE_META + 1 + 2 * t, ROW_Z : ROW_Z + 1, :] for t in range(2)], 1)
    cells = lax.broadcasted_iota(jnp.int32, (NZ, LANES), 0).astype(jnp.float32)
    hot = jnp.where(cells == column, 1.0, 0.0)
    back = hot.T.astype(jnp.bfloat16)
    hot = hot.astype(jnp.bfloat16)
    for term in range(2):
        hot_ref[NZ * term : NZ * term + NZ, :] = hot
        back_ref[LANES * term : LANES * term + LANES, :] = back


def gather_columns(group, field2, first_in, planes_in, skip, gathered, onehot):
    rows = slice(NY * first_in, NY * (first_in + planes_in))
    columns = dot(field2[rows, :], onehot[...]).reshape(planes_in, NY, LANES)
    for tile in range(2):
        part = columns[:, :, half(tile)]
        gathered[group][tile, skip : skip + planes_in, 0:16, :] = part
        gathered[group][tile, skip : skip + planes_in, 16:24, :] = part[:, 0:8]


def read_windows(group, gathered, boxes):
    lane = lax.broadcasted_iota(jnp.int32, (8, 128), 1)
    values = [[jnp.zeros((8, 128), jnp.float32)] * 2 for _ in range(BX)]
    for a in range(16):
        mine = (lane >> 3) == a
        for tile in range(2):
            x0, y0 = boxes.place(group, 16 * tile + a)
            for i in range(BX):
                values[i][tile] = jnp.where(mine, gathered[group][tile, x0 + i, pl.ds(y0, 8), :], values[i][tile])
    return values


def contributions(group, values, table, placed, boxes, sums):
    coeffs = []
    for tile in range(2):
        rows = []
        for l in range(NPROJ):
            total = values[0][tile] * table[tile, l * BX]
            for i in range(1, BX):
                total = total + values[i][tile] * table[tile, l * BX + i]
            rows.append(jnp.sum(total, 0, keepdims=True))
        coeffs.append(jnp.concatenate(rows, 0))
    both = dot(two_terms(jnp.concatenate(coeffs, 1), 0), sums)
    coeffs = (both[:8] + both[8:]) * boxes.weight(group)
    lane = lax.broadcasted_iota(jnp.int32, (8, 128), 1)
    contrib = [[None] * 2 for _ in range(BX)]
    for tile in range(2):
        rows = [jnp.broadcast_to(coeffs[l : l + 1, half(tile)], (8, 128)) for l in range(NPROJ)]
        for i in range(BX):
            total = rows[0] * table[tile, i]
            for l in range(1, NPROJ):
                total = total + rows[l] * table[tile, l * BX + i]
            contrib[i][tile] = total
    for a in range(16):
        mine = (lane >> 3) == a
        for tile in range(2):
            x0, y0 = boxes.place(group, 16 * tile + a)
            for i in range(BX):
                pltpu.store(placed[group].at[tile, x0 + i, pl.ds(y0, 8), :], contrib[i][tile], mask=mine)


def spread_group(group, first, count, placed, back):
    planes = slice(first, first + count)
    tiles = []
    for tile in range(2):
        folded = placed[group][tile, planes, 0:8, :] + placed[group][tile, planes, 16:24, :]
        tiles.append(jnp.concatenate([folded, placed[group][tile, planes, 8:16, :]], 1).reshape(count * NY, 128))
    return dot(two_terms(jnp.concatenate(tiles, 1), 1), back[...]).reshape(count, NY, NZ)


def along_z(field2, rows, zst_ref):
    return dot(field2[rows, :], zst_ref[0:256, :]) + dot(field2[rows, 0:128], zst_ref[256:384, :])


def stencil_plane(padded, plane):
    total = 3.0 * STENCIL[0] * padded[plane, 8:24, :]
    for reach in range(1, 7):
        along_x = padded[plane + reach, 8:24, :] + padded[plane - reach, 8:24, :]
        along_y = padded[plane, 8 + reach : 24 + reach, :] + padded[plane, 8 - reach : 24 - reach, :]
        total = total + STENCIL[reach] * (along_x + along_y)
    return total


def potential_plane(p, low_ref, pot_ref, high_ref):
    source, tile = (
        (low_ref, TILE_POT + 2 * p) if p < 6 else (pot_ref, 2 * (p - 6)) if p < 18 else (high_ref, TILE_POT + 2 * (p - 18))
    )
    return source[tile : tile + 2].reshape(NY, NZ)


def clear(boxed):
    for ref in boxed:
        ref[...] = jnp.zeros_like(ref)


def load_fields(fields, padded, field2):
    for n, value in enumerate(fields):
        fill(padded, 12 * n, value.reshape(CX, NY, NZ))
        field2[192 * n : 192 * n + 192, :] = two_terms(value.reshape(192, NZ), 1)


def head_kernel(up_ref, high_ref, low_ref, pot_ref, table_ref, zst_ref, sums_ref, hot_ref, back_ref,
                half_ref, values_ref, partial_ref, hots_ref, backs_ref,
                low_xy, own_xy, high_xy, padded, field2, gathered, placed, local, work, sems):
    boxes = Boxes((low_ref, up_ref, high_ref), (low_xy, own_xy, high_xy), sems)
    load_fields([r[TILE_Y : TILE_Y + 24] for r in (low_ref, up_ref, high_ref)], padded, field2)
    clear(placed)
    gathered[2][:, 12:SPAN] = jnp.zeros((2, SPAN - 12, 24, 128), jnp.float32)
    for n, source in enumerate((low_ref, high_ref)):
        write_one_hot(source, hots_ref.at[n], backs_ref.at[n])
    gather_columns(1, field2, 12, SPAN, 0, gathered, hot_ref)
    gather_columns(0, field2, 0, SPAN, 0, gathered, hots_ref.at[0])
    gather_columns(2, field2, 24, 12, 0, gathered, hots_ref.at[1])
    local[...] = along_z(field2, slice(96, 480), zst_ref).reshape(24, NY, NZ)
    for p in range(24):
        laplace = stencil_plane(padded, p + 6) + local[p]
        pot = potential_plane(p, low_ref, pot_ref, high_ref)
        local[p] = (-0.5 * laplace + (pot - CENTER) * padded[p + 6, 8:24, :]) * (1.0 / HALF)
    for n, source in enumerate((low_ref, high_ref)):
        spread_projectors(lambda part, a: source[TILE_P + 16 * part + a], work, half_ref.at[n])
    boxes.wait()
    contributions(1, read_windows(1, gathered, boxes), table_ref, placed, boxes, sums_ref[...])
    for n, group in enumerate((0, 2)):
        values = read_windows(group, gathered, boxes)
        for i in range(BX):
            for tile in range(2):
                values_ref[n, i, tile] = values[i][tile]
    partial_ref[0:6] = local[0:6]
    partial_ref[6:23] = local[6:23] + spread_group(1, 0, 17, placed, back_ref) * (1.0 / HALF)
    partial_ref[23] = local[23]


def second_step(boxes, hots, backs, padded1, field2, gathered, placed, local, nonlocal_, pot_ref, tables, zst_ref, sums):
    for group, first, planes, skip in ((0, 0, 11, 6), (1, 6, SPAN, 0)):
        gather_columns(group, field2, first, planes, skip, gathered, hots[group])
    for group in range(2):
        contributions(group, read_windows(group, gathered, boxes), tables[group], placed, boxes, sums)
    local[0:12] = along_z(field2, slice(96, 288), zst_ref).reshape(12, NY, NZ)
    for p in range(12):
        here = padded1[p + 6, 8:24, :]
        laplace = stencil_plane(padded1, p + 6) + local[p]
        pot = potential_plane(p + 6, None, pot_ref, None)
        local[p] = -0.5 * laplace + (pot - CENTER) * here
    nonlocal_[0:12] = spread_group(1, 0, 12, placed, backs[1])
    nonlocal_[0:5] += spread_group(0, 12, 5, placed, backs[0])
    for p in range(12):
        yield p, (local[p] + nonlocal_[p]) * (2.0 / HALF)


def tail_kernel(up_ref, high_ref, low_ref, pot_ref, table_ref, zst_ref, sums_ref, hot_ref, back_ref,
                half_ref, values_ref, partial_ref, hots_ref, backs_ref, highsib_ref, lowsib_ref,
                out_ref, kept_ref, tables_ref,
                low_xy, own_xy, high_xy, padded1, field2, gathered, placed, local, nonlocal_, work, sems):
    core = lax.axis_index("band") % 2
    boxes = Boxes((low_ref, up_ref, high_ref), (low_xy, own_xy, high_xy), sems)
    clear(placed)
    gathered[0][:, 0:6] = jnp.zeros((2, 6, 24, 128), jnp.float32)
    for n, source in enumerate((lowsib_ref, highsib_ref)):
        spread_projectors(lambda part, a: source[TILE_P + 16 * part + a], work, tables_ref.at[n, 1 - core])
        tables_ref[n, core] = half_ref[n]
    hots, backs = (hots_ref.at[0], hot_ref), (backs_ref.at[0], back_ref, backs_ref.at[1])
    boxes.wait()
    sums = sums_ref[...]
    for n, group in enumerate((0, 2)):
        values = [[values_ref[n, i, tile] for tile in range(2)] for i in range(BX)]
        contributions(group, values, tables_ref.at[n], placed, boxes, sums)
    nonlocal_[0:11] = spread_group(0, 6, 11, placed, backs[0])
    nonlocal_[11:18] = jnp.zeros((7, NY, NZ), jnp.float32)
    nonlocal_[18:24] = spread_group(2, 0, 6, placed, backs[2])
    for p in range(24):
        updated = partial_ref[p] + nonlocal_[p] * (1.0 / HALF)
        kept_ref[p] = updated
        fill(padded1, p, updated[None])
        field2[16 * p : 16 * p + 16, :] = two_terms(updated, 1)
    tables = (tables_ref.at[0], table_ref)
    for p, value in second_step(boxes, hots, backs, padded1, field2, gathered, placed, local, nonlocal_, pot_ref, tables,
                                zst_ref, sums):
        out_ref[2 * p : 2 * p + 2] = (value - up_ref[TILE_Y + 2 * p : TILE_Y + 2 * p + 2].reshape(NY, NZ)).reshape(2, 8, 128)


def last_kernel(up_ref, high_ref, low_ref, pot_ref, table_ref, zst_ref, sums_ref, hot_ref, back_ref,
                kept_ref, tables_ref, hots_ref, backs_ref,
                mid_ref, highy_ref, lowy_ref,
                out_ref,
                low_xy, own_xy, high_xy, padded, padded1, field2, gathered, placed, local, nonlocal_, sems):
    boxes = Boxes((low_ref, up_ref, high_ref), (low_xy, own_xy, high_xy), sems)
    load_fields([r[...] for r in (lowy_ref, mid_ref, highy_ref)], padded, field2)
    clear(placed)
    gathered[2][:, 12:SPAN] = jnp.zeros((2, SPAN - 12, 24, 128), jnp.float32)
    hots, backs = (hots_ref.at[0], hot_ref, hots_ref.at[1]), (backs_ref.at[0], back_ref, backs_ref.at[1])
    sums = sums_ref[...]
    tables = (tables_ref.at[0], table_ref, tables_ref.at[1])
    for group, planes in ((0, SPAN), (1, SPAN), (2, 12)):
        gather_columns(group, field2, 12 * group, planes, 0, gathered, hots[group])
    local[...] = along_z(field2, slice(96, 480), zst_ref).reshape(24, NY, NZ)
    for p in range(24):
        laplace = stencil_plane(padded, p + 6) + local[p]
        pot = potential_plane(p, low_ref, pot_ref, high_ref)
        applied = -0.5 * laplace + (pot - CENTER) * padded[p + 6, 8:24, :]
        local[p] = applied * (2.0 / HALF) - kept_ref[p]
    boxes.wait()
    windows = [read_windows(group, gathered, boxes) for group in range(3)]
    for group in range(3):
        contributions(group, windows[group], tables[group], placed, boxes, sums)
    nonlocal_[0:11] = spread_group(0, 6, 11, placed, backs[0])
    nonlocal_[11:24] = jnp.zeros((13, NY, NZ), jnp.float32)
    nonlocal_[6:23] += spread_group(1, 0, 17, placed, backs[1])
    nonlocal_[18:24] += spread_group(2, 0, 6, placed, backs[2])
    for p in range(24):
        updated = local[p] + nonlocal_[p] * (2.0 / HALF)
        fill(padded1, p, updated[None])
        field2[16 * p : 16 * p + 16, :] = two_terms(updated, 1)
    for p, value in second_step(boxes, hots, backs, padded1, field2, gathered, placed, local, nonlocal_, pot_ref, tables,
                                zst_ref, sums):
        out_ref[2 * p : 2 * p + 2] = (value - padded[p + 12, 8:24, :]).reshape(2, 8, 128)


XY = [pltpu.SMEM((8, 128), jnp.float32)] * 3
PADDED = pltpu.VMEM((36, 32, NZ), jnp.float32)
PADDED1 = pltpu.VMEM((24, 32, NZ), jnp.float32)
FIELD2 = pltpu.VMEM((576, 2 * NZ), jnp.bfloat16)
BOXED = [pltpu.VMEM((2, SPAN, 24, 128), jnp.float32)] * 3
PLANES = pltpu.VMEM((24, NY, NZ), jnp.float32)
WORK = pltpu.VMEM((BX, BY * NPROJ, 128), jnp.float32)
COPIES = pltpu.SemaphoreType.DMA((3,))


def parts_kernel(factors_ref, own_ref, other_ref, base_ref, one_ref, two_ref, three_ref):
    own, other = own_ref[...], other_ref[...]
    for hop, target in enumerate((base_ref, one_ref, two_ref, three_ref)):
        target[...] = factors_ref[2 * hop] * own + factors_ref[2 * hop + 1] * other


def store_kernel(own_ref, out_ref):
    out_ref[...] = own_ref[...]


def total_kernel(base_ref, one_ref, two_ref, three_ref, out_ref):
    out_ref[...] = (base_ref[...] + one_ref[...]) + (two_ref[...] + three_ref[...])


def ring(axis, step):
    count = lax.axis_size(axis)
    return [(i, (i + step) % count) for i in range(count)]


def meet(axis, bits):
    return [(i, i ^ bits) for i in range(lax.axis_size(axis))]


def shards(orbitals, potential, atom_pos, atom_count, projectors, gammas, ritz):
    stay = lambda v: pltpu.with_memory_space_constraint(v, pltpu.HBM)
    up, down, pot, proj = call(
        pack_kernel,
        [shape(TILES, 8, 128), shape(TILES, 8, 128), shape(24, 8, 128), shape(3 * ATOMS, 8, 128)],
        [HBM] * 5 + [SMEM],
        (
            stay(orbitals.reshape(24, 8, 128)),
            stay(potential.reshape(24, 8, 128)),
            stay(projectors),
            stay(gammas.T),
            stay(atom_pos.T),
            atom_count,
        ),
        "pack",
        [pltpu.VMEM((NPROJ, ATOMS), jnp.float32), pltpu.VMEM((3, ATOMS), jnp.int32), pltpu.SemaphoreType.DMA((16,))],
    )
    low = lax.ppermute(up, "dom", ring("dom", 1))
    high = lax.ppermute(down, "dom", ring("dom", -1))
    table, zst, sums, hot, back, factors = call(
        prepare_kernel,
        [
            shape(2, PAIRS, 8, 128),
            shape(384, NZ, dtype=jnp.bfloat16),
            shape(LANES, LANES, dtype=jnp.bfloat16),
            shape(2 * NZ, LANES, dtype=jnp.bfloat16),
            shape(2 * LANES, NZ, dtype=jnp.bfloat16),
            shape(8, 8, 128),
        ],
        [VMEM] * 3,
        (proj, down, ritz),
        "prepare",
        [WORK],
    )
    highsib = lax.ppermute(high, "band", meet("band", 1))
    lowsib = lax.ppermute(low, "band", meet("band", 1))
    common = (down, high, low, pot, table, zst, sums, hot, back)
    halves, values, partial, hots, backs = call(
        head_kernel,
        [
            shape(2, PAIRS, 8, 128),
            shape(2, BX, 2, 8, 128),
            shape(24, NY, NZ),
            shape(2, 2 * NZ, LANES, dtype=jnp.bfloat16),
            shape(2, 2 * LANES, NZ, dtype=jnp.bfloat16),
        ],
        [VMEM] * 9,
        common,
        "head",
        XY + [PADDED, FIELD2, BOXED, BOXED, PLANES, WORK, COPIES],
        flops=10_000_000_000,
    )
    second, first, tables = call(
        tail_kernel,
        [shape(24, 8, 128), shape(24, NY, NZ), shape(2, 2, PAIRS, 8, 128)],
        [VMEM] * 16,
        common + (halves, values, partial, hots, backs, highsib, lowsib),
        "tail",
        XY + [PADDED1, FIELD2, BOXED, BOXED, PLANES, PLANES, WORK, COPIES],
    )
    low_y = lax.ppermute(second, "dom", ring("dom", 1))
    high_y = lax.ppermute(second, "dom", ring("dom", -1))
    (fourth,) = call(
        last_kernel,
        [shape(24, 8, 128)],
        [VMEM] * 16,
        common + (first, tables, hots, backs, second, high_y, low_y),
        "last",
        XY + [PADDED, PADDED1, FIELD2, BOXED, BOXED, PLANES, PLANES, COPIES],
    )
    other = lax.ppermute(fourth, "band", meet("band", 1))
    field = shape(24, 8, 128)
    base, one, two, three = call(
        parts_kernel, [field] * 4, [VMEM] * 3, (factors, fourth, other), "parts"
    )
    arrived = [lax.ppermute(v, "band", meet("band", 2 * hop)) for hop, v in ((2, two), (1, one), (3, three))]
    (filtered,) = call(store_kernel, [field], [VMEM], (fourth,), "store")
    (rotated,) = call(total_kernel, [field], [VMEM] * 4, (base, *arrived), "total")
    return (filtered.reshape(orbitals.shape), rotated.reshape(orbitals.shape))


def solution(mesh):
    in_specs = (
        P("band", "dom", None, None),
        P("dom", None, None),
        P("dom", None),
        P("dom"),
        P("dom", None, None),
        P("dom", None),
        P(),
    )
    out_specs = (P("band", "dom", None, None), P("band", "dom", None, None))
    return jax.shard_map(shards, mesh=mesh, in_specs=in_specs, out_specs=out_specs, check_vma=False)
```

```python
import jax
import jax.numpy as jnp
from jax import lax
from jax.experimental import pallas as pl
from jax.experimental.pallas import tpu as pltpu
from jax.sharding import PartitionSpec as P

STENCIL = (
    -5369.0 / 1800.0,
    12.0 / 7.0,
    -15.0 / 56.0,
    10.0 / 189.0,
    -1.0 / 112.0,
    2.0 / 1925.0,
    -1.0 / 16632.0,
)
LOWER = -1.6
UPPER = 24.0
CENTER = 0.5 * (UPPER + LOWER)
HALF = 0.5 * (UPPER - LOWER)

CX, NY, NZ = 12, 16, 128
ATOMS = 32
NPROJ, BX, BY, BZ = 8, 6, 8, 8
LANES = ATOMS * BZ
SPAN = CX + BX - 1
PAIRS = NPROJ * BX
TILE_Y, TILE_POT, TILE_P, TILE_META, TILES = 0, 24, 36, 84, 88
ROW_Z, ROW_X0, ROW_Y0 = 0, 1, 2

VMEM = pl.BlockSpec(memory_space=pltpu.VMEM)
HBM = pl.BlockSpec(memory_space=pltpu.HBM)
SMEM = pl.BlockSpec(memory_space=pltpu.SMEM)


def shape(*dims, dtype=jnp.float32):
    return jax.ShapeDtypeStruct(dims, dtype)


def call(kernel, outs, ins, args, name, scratch=(), out_specs=None, flops=1_000_000, moved=2_000_000):
    return pl.pallas_call(
        kernel,
        out_shape=outs,
        in_specs=ins,
        out_specs=out_specs or [VMEM] * len(outs),
        scratch_shapes=list(scratch),
        compiler_params=pltpu.CompilerParams(vmem_limit_bytes=32 * 2**20),
        cost_estimate=pl.CostEstimate(flops=flops, bytes_accessed=moved, transcendentals=0),
        name=name,
    )(*args)


def two_terms(value, axis):
    high = value.astype(jnp.bfloat16)
    low = (value - high.astype(jnp.float32)).astype(jnp.bfloat16)
    return jnp.concatenate([high, low], axis)


def dot(left, right):
    return jnp.dot(left, right, preferred_element_type=jnp.float32)


def half(tile):
    return slice(128 * tile, 128 * tile + 128)


def pack_kernel(y_hbm, pot_hbm, proj_hbm, gamma_hbm, pos_hbm, count_ref,
                up_ref, down_ref, pot_ref, proj_ref, gamma_ref, pos_ref, sems):
    core = lax.axis_index("band") % 2
    first = 16 * core
    copies = [
        pltpu.make_async_copy(gamma_hbm, gamma_ref, sems.at[0]),
        pltpu.make_async_copy(pos_hbm, pos_ref, sems.at[1]),
    ]
    moves = [
        (pot_hbm, pot_ref),
        (pot_hbm.at[pl.ds(12, 12)], up_ref.at[pl.ds(TILE_POT, 12)]),
        (pot_hbm.at[pl.ds(0, 12)], down_ref.at[pl.ds(TILE_POT, 12)]),
    ]
    for out in (up_ref, down_ref):
        moves.append((y_hbm, out.at[pl.ds(TILE_Y, 24)]))
        for part in range(3):
            source = proj_hbm.at[pl.ds(first, 16), pl.ds(0, 8), pl.ds(128 * part, 128)]
            moves.append((source, out.at[pl.ds(TILE_P + 16 * part, 16)]))
    for part in range(3):
        source = proj_hbm.at[pl.ds(0, ATOMS), pl.ds(0, 8), pl.ds(128 * part, 128)]
        moves.append((source, proj_ref.at[pl.ds(ATOMS * part, ATOMS)]))
    for n, (source, target) in enumerate(moves):
        copies.append(pltpu.make_async_copy(source, target, sems.at[2 + n]))
    for copy in copies:
        copy.start()
    copies[0].wait()
    copies[1].wait()
    live = lax.broadcasted_iota(jnp.int32, (1, ATOMS), 1) < count_ref[0]
    weight = jnp.where(live, gamma_ref[...], 0.0)
    repeat = lax.broadcasted_iota(jnp.int32, (ATOMS, LANES), 1) >> 3
    repeat = jnp.where(repeat == lax.broadcasted_iota(jnp.int32, (ATOMS, LANES), 0), 1.0, 0.0)
    corner = pos_ref[...].astype(jnp.float32)
    spread = lambda v: jnp.dot(v, repeat, preferred_element_type=jnp.float32, precision=lax.Precision.HIGHEST)
    weight = spread(weight)
    column = spread(corner)[2:3] + (lax.broadcasted_iota(jnp.int32, (1, LANES), 1) & 7).astype(jnp.float32)
    column = jnp.where(column >= NZ, column - NZ, column)
    for out in (up_ref, down_ref):
        for tile in range(2):
            out[TILE_META + 2 * tile] = weight[:, half(tile)]
            out[TILE_META + 2 * tile + 1] = jnp.broadcast_to(column[:, half(tile)], (8, 128))
        out[TILE_META + 1, ROW_X0 : ROW_X0 + 1, 0:ATOMS] = corner[0:1]
        out[TILE_META + 1, ROW_Y0 : ROW_Y0 + 1, 0:ATOMS] = corner[1:2]
    for copy in copies[2:]:
        copy.wait()


def spread_projectors(read, work, table):
    lane = lax.broadcasted_iota(jnp.int32, (8, 128), 1)
    for part in range(3):
        items = [read(part, a) for a in range(16)]
        for bit in (1, 2, 4, 8):
            upper = (lane & (8 * bit)) != 0
            for p in range(16):
                if p & bit:
                    continue
                q = p | bit
                first, second = items[p], items[q]
                items[p] = jnp.where(upper, pltpu.roll(second, 8 * bit, 1), first)
                items[q] = jnp.where(upper, second, pltpu.roll(first, 128 - 8 * bit, 1))
        for g in range(16):
            i, j = 2 * part + g // 8, g % 8
            work[i, 8 * j : 8 * j + 8, :] = items[g]
    for i in range(BX):
        for l in range(NPROJ):
            table[l * BX + i] = work.at[i][pl.ds(l, 8, stride=8), :]


def prepare_kernel(proj_ref, up_ref, ritz_ref, table_ref, zst_ref, sums_ref, hot_ref, back_ref, factors_ref, work):
    write_one_hot(up_ref, hot_ref, back_ref)
    band = lax.axis_index("band")
    row = lax.broadcasted_iota(jnp.int32, (8, 8), 0)
    column = lax.broadcasted_iota(jnp.int32, (8, 8), 1)
    for hop in range(4):
        for n in range(2):
            orbital, to = (band ^ (4 + n), band) if hop == 2 else (band ^ n, band ^ (2 * hop))
            picked = jnp.where((row == orbital) & (column == to), ritz_ref[...], 0.0)
            picked = jnp.sum(jnp.sum(picked, 1, keepdims=True), 0, keepdims=True)
            factors_ref[2 * hop + n] = jnp.broadcast_to(picked, (8, 128))
    for tile in range(2):
        read = lambda part, a: proj_ref[ATOMS * part + 16 * tile + a]
        spread_projectors(read, work, table_ref.at[tile])
    apart = lax.broadcasted_iota(jnp.int32, (NZ, NZ), 0) - lax.broadcasted_iota(jnp.int32, (NZ, NZ), 1)
    full = jnp.zeros((NZ, NZ), jnp.float32)
    for reach in range(1, 7):
        near = ((apart & (NZ - 1)) == reach) | ((apart & (NZ - 1)) == NZ - reach)
        full = jnp.where(near, STENCIL[reach], full)
    high = full.astype(jnp.bfloat16)
    zst_ref[0:128, :] = high
    zst_ref[128:256, :] = high
    zst_ref[256:384, :] = (full - high.astype(jnp.float32)).astype(jnp.bfloat16)
    atom = lambda axis: lax.broadcasted_iota(jnp.int32, (LANES, LANES), axis) >> 3
    sums_ref[...] = jnp.where(atom(0) == atom(1), 1.0, 0.0).astype(jnp.bfloat16)


def fill(padded, plane, value):
    count = value.shape[0]
    padded[plane : plane + count, 8:24, :] = value
    padded[plane : plane + count, 0:8, :] = value[:, 8:16]
    padded[plane : plane + count, 24:32, :] = value[:, 0:8]


class Boxes:
    def __init__(self, sources, held, sems):
        self.sources, self.held = sources, held
        self.copies = [
            pltpu.make_async_copy(s.at[TILE_META + 1], h, sems.at[n]) for n, (s, h) in enumerate(zip(sources, held))
        ]
        for copy in self.copies:
            copy.start()

    def wait(self):
        for copy in self.copies:
            copy.wait()

    def place(self, group, atom):
        held = self.held[group]
        return held[ROW_X0, atom].astype(jnp.int32), held[ROW_Y0, atom].astype(jnp.int32)

    def weight(self, group):
        source = self.sources[group]
        return jnp.concatenate([source[TILE_META], source[TILE_META + 2]], 1)


def write_one_hot(source, hot_ref, back_ref):
    column = jnp.concatenate([source[TILE_META + 1 + 2 * t, ROW_Z : ROW_Z + 1, :] for t in range(2)], 1)
    cells = lax.broadcasted_iota(jnp.int32, (NZ, LANES), 0).astype(jnp.float32)
    hot = jnp.where(cells == column, 1.0, 0.0)
    back = hot.T.astype(jnp.bfloat16)
    hot = hot.astype(jnp.bfloat16)
    for term in range(2):
        hot_ref[NZ * term : NZ * term + NZ, :] = hot
        back_ref[LANES * term : LANES * term + LANES, :] = back


def gather_columns(group, field2, first_in, planes_in, skip, gathered, onehot):
    rows = slice(NY * first_in, NY * (first_in + planes_in))
    columns = dot(field2[rows, :], onehot[...]).reshape(planes_in, NY, LANES)
    for tile in range(2):
        part = columns[:, :, half(tile)]
        gathered[group][tile, skip : skip + planes_in, 0:16, :] = part
        gathered[group][tile, skip : skip + planes_in, 16:24, :] = part[:, 0:8]


def read_windows(group, gathered, boxes):
    lane = lax.broadcasted_iota(jnp.int32, (8, 128), 1)
    values = [[jnp.zeros((8, 128), jnp.float32)] * 2 for _ in range(BX)]
    for a in range(16):
        mine = (lane >> 3) == a
        for tile in range(2):
            x0, y0 = boxes.place(group, 16 * tile + a)
            for i in range(BX):
                values[i][tile] = jnp.where(mine, gathered[group][tile, x0 + i, pl.ds(y0, 8), :], values[i][tile])
    return values


def contributions(group, values, table, placed, boxes, sums):
    coeffs = []
    for tile in range(2):
        rows = []
        for l in range(NPROJ):
            total = values[0][tile] * table[tile, l * BX]
            for i in range(1, BX):
                total = total + values[i][tile] * table[tile, l * BX + i]
            rows.append(jnp.sum(total, 0, keepdims=True))
        coeffs.append(jnp.concatenate(rows, 0))
    both = dot(two_terms(jnp.concatenate(coeffs, 1), 0), sums)
    coeffs = (both[:8] + both[8:]) * boxes.weight(group)
    lane = lax.broadcasted_iota(jnp.int32, (8, 128), 1)
    contrib = [[None] * 2 for _ in range(BX)]
    for tile in range(2):
        rows = [jnp.broadcast_to(coeffs[l : l + 1, half(tile)], (8, 128)) for l in range(NPROJ)]
        for i in range(BX):
            total = rows[0] * table[tile, i]
            for l in range(1, NPROJ):
                total = total + rows[l] * table[tile, l * BX + i]
            contrib[i][tile] = total
    for a in range(16):
        mine = (lane >> 3) == a
        for tile in range(2):
            x0, y0 = boxes.place(group, 16 * tile + a)
            for i in range(BX):
                pltpu.store(placed[group].at[tile, x0 + i, pl.ds(y0, 8), :], contrib[i][tile], mask=mine)


def spread_group(group, first, count, placed, back):
    planes = slice(first, first + count)
    tiles = []
    for tile in range(2):
        folded = placed[group][tile, planes, 0:8, :] + placed[group][tile, planes, 16:24, :]
        tiles.append(jnp.concatenate([folded, placed[group][tile, planes, 8:16, :]], 1).reshape(count * NY, 128))
    return dot(two_terms(jnp.concatenate(tiles, 1), 1), back[...]).reshape(count, NY, NZ)


def along_z(field2, rows, zst_ref):
    return dot(field2[rows, :], zst_ref[0:256, :]) + dot(field2[rows, 0:128], zst_ref[256:384, :])


def stencil_plane(padded, plane):
    total = 3.0 * STENCIL[0] * padded[plane, 8:24, :]
    for reach in range(1, 7):
        along_x = padded[plane + reach, 8:24, :] + padded[plane - reach, 8:24, :]
        along_y = padded[plane, 8 + reach : 24 + reach, :] + padded[plane, 8 - reach : 24 - reach, :]
        total = total + STENCIL[reach] * (along_x + along_y)
    return total


def potential_plane(p, low_ref, pot_ref, high_ref):
    source, tile = (
        (low_ref, TILE_POT + 2 * p) if p < 6 else (pot_ref, 2 * (p - 6)) if p < 18 else (high_ref, TILE_POT + 2 * (p - 18))
    )
    return source[tile : tile + 2].reshape(NY, NZ)


def clear(boxed):
    for ref in boxed:
        ref[...] = jnp.zeros_like(ref)


def load_fields(fields, padded, field2):
    for n, value in enumerate(fields):
        fill(padded, 12 * n, value.reshape(CX, NY, NZ))
        field2[192 * n : 192 * n + 192, :] = two_terms(value.reshape(192, NZ), 1)


def head_kernel(up_ref, high_ref, low_ref, pot_ref, table_ref, zst_ref, sums_ref, hot_ref, back_ref,
                half_ref, values_ref, partial_ref, hots_ref, backs_ref,
                low_xy, own_xy, high_xy, padded, field2, gathered, placed, local, work, sems):
    boxes = Boxes((low_ref, up_ref, high_ref), (low_xy, own_xy, high_xy), sems)
    load_fields([r[TILE_Y : TILE_Y + 24] for r in (low_ref, up_ref, high_ref)], padded, field2)
    clear(placed)
    gathered[2][:, 12:SPAN] = jnp.zeros((2, SPAN - 12, 24, 128), jnp.float32)
    for n, source in enumerate((low_ref, high_ref)):
        write_one_hot(source, hots_ref.at[n], backs_ref.at[n])
    gather_columns(1, field2, 12, SPAN, 0, gathered, hot_ref)
    gather_columns(0, field2, 0, SPAN, 0, gathered, hots_ref.at[0])
    gather_columns(2, field2, 24, 12, 0, gathered, hots_ref.at[1])
    local[...] = along_z(field2, slice(96, 480), zst_ref).reshape(24, NY, NZ)
    for p in range(24):
        laplace = stencil_plane(padded, p + 6) + local[p]
        pot = potential_plane(p, low_ref, pot_ref, high_ref)
        local[p] = (-0.5 * laplace + (pot - CENTER) * padded[p + 6, 8:24, :]) * (1.0 / HALF)
    for n, source in enumerate((low_ref, high_ref)):
        spread_projectors(lambda part, a: source[TILE_P + 16 * part + a], work, half_ref.at[n])
    boxes.wait()
    contributions(1, read_windows(1, gathered, boxes), table_ref, placed, boxes, sums_ref[...])
    for n, group in enumerate((0, 2)):
        values = read_windows(group, gathered, boxes)
        for i in range(BX):
            for tile in range(2):
                values_ref[n, i, tile] = values[i][tile]
    partial_ref[0:6] = local[0:6]
    partial_ref[6:23] = local[6:23] + spread_group(1, 0, 17, placed, back_ref) * (1.0 / HALF)
    partial_ref[23] = local[23]


def second_step(boxes, hots, backs, padded1, field2, gathered, placed, local, nonlocal_, pot_ref, tables, zst_ref, sums):
    for group, first, planes, skip in ((0, 0, 11, 6), (1, 6, SPAN, 0)):
        gather_columns(group, field2, first, planes, skip, gathered, hots[group])
    for group in range(2):
        contributions(group, read_windows(group, gathered, boxes), tables[group], placed, boxes, sums)
    local[0:12] = along_z(field2, slice(96, 288), zst_ref).reshape(12, NY, NZ)
    for p in range(12):
        here = padded1[p + 6, 8:24, :]
        laplace = stencil_plane(padded1, p + 6) + local[p]
        pot = potential_plane(p + 6, None, pot_ref, None)
        local[p] = -0.5 * laplace + (pot - CENTER) * here
    nonlocal_[0:12] = spread_group(1, 0, 12, placed, backs[1])
    nonlocal_[0:5] += spread_group(0, 12, 5, placed, backs[0])
    for p in range(12):
        yield p, (local[p] + nonlocal_[p]) * (2.0 / HALF)


def tail_kernel(up_ref, high_ref, low_ref, pot_ref, table_ref, zst_ref, sums_ref, hot_ref, back_ref,
                half_ref, values_ref, partial_ref, hots_ref, backs_ref, highsib_ref, lowsib_ref,
                out_ref, kept_ref, tables_ref,
                low_xy, own_xy, high_xy, padded1, field2, gathered, placed, local, nonlocal_, work, sems):
    core = lax.axis_index("band") % 2
    boxes = Boxes((low_ref, up_ref, high_ref), (low_xy, own_xy, high_xy), sems)
    clear(placed)
    gathered[0][:, 0:6] = jnp.zeros((2, 6, 24, 128), jnp.float32)
    for n, source in enumerate((lowsib_ref, highsib_ref)):
        spread_projectors(lambda part, a: source[TILE_P + 16 * part + a], work, tables_ref.at[n, 1 - core])
        tables_ref[n, core] = half_ref[n]
    hots, backs = (hots_ref.at[0], hot_ref), (backs_ref.at[0], back_ref, backs_ref.at[1])
    boxes.wait()
    sums = sums_ref[...]
    for n, group in enumerate((0, 2)):
        values = [[values_ref[n, i, tile] for tile in range(2)] for i in range(BX)]
        contributions(group, values, tables_ref.at[n], placed, boxes, sums)
    nonlocal_[0:11] = spread_group(0, 6, 11, placed, backs[0])
    nonlocal_[11:18] = jnp.zeros((7, NY, NZ), jnp.float32)
    nonlocal_[18:24] = spread_group(2, 0, 6, placed, backs[2])
    for p in range(24):
        updated = partial_ref[p] + nonlocal_[p] * (1.0 / HALF)
        kept_ref[p] = updated
        fill(padded1, p, updated[None])
        field2[16 * p : 16 * p + 16, :] = two_terms(updated, 1)
    tables = (tables_ref.at[0], table_ref)
    for p, value in second_step(boxes, hots, backs, padded1, field2, gathered, placed, local, nonlocal_, pot_ref, tables,
                                zst_ref, sums):
        out_ref[2 * p : 2 * p + 2] = (value - up_ref[TILE_Y + 2 * p : TILE_Y + 2 * p + 2].reshape(NY, NZ)).reshape(2, 8, 128)


def last_kernel(up_ref, high_ref, low_ref, pot_ref, table_ref, zst_ref, sums_ref, hot_ref, back_ref,
                kept_ref, tables_ref, hots_ref, backs_ref,
                mid_ref, highy_ref, lowy_ref,
                out_ref,
                low_xy, own_xy, high_xy, padded, padded1, field2, gathered, placed, local, nonlocal_, sems):
    boxes = Boxes((low_ref, up_ref, high_ref), (low_xy, own_xy, high_xy), sems)
    load_fields([r[...] for r in (lowy_ref, mid_ref, highy_ref)], padded, field2)
    clear(placed)
    gathered[2][:, 12:SPAN] = jnp.zeros((2, SPAN - 12, 24, 128), jnp.float32)
    hots, backs = (hots_ref.at[0], hot_ref, hots_ref.at[1]), (backs_ref.at[0], back_ref, backs_ref.at[1])
    sums = sums_ref[...]
    tables = (tables_ref.at[0], table_ref, tables_ref.at[1])
    for group, planes in ((0, SPAN), (1, SPAN), (2, 12)):
        gather_columns(group, field2, 12 * group, planes, 0, gathered, hots[group])
    local[...] = along_z(field2, slice(96, 480), zst_ref).reshape(24, NY, NZ)
    for p in range(24):
        laplace = stencil_plane(padded, p + 6) + local[p]
        pot = potential_plane(p, low_ref, pot_ref, high_ref)
        applied = -0.5 * laplace + (pot - CENTER) * padded[p + 6, 8:24, :]
        local[p] = applied * (2.0 / HALF) - kept_ref[p]
    boxes.wait()
    windows = [read_windows(group, gathered, boxes) for group in range(3)]
    for group in range(3):
        contributions(group, windows[group], tables[group], placed, boxes, sums)
    nonlocal_[0:11] = spread_group(0, 6, 11, placed, backs[0])
    nonlocal_[11:24] = jnp.zeros((13, NY, NZ), jnp.float32)
    nonlocal_[6:23] += spread_group(1, 0, 17, placed, backs[1])
    nonlocal_[18:24] += spread_group(2, 0, 6, placed, backs[2])
    for p in range(24):
        updated = local[p] + nonlocal_[p] * (2.0 / HALF)
        fill(padded1, p, updated[None])
        field2[16 * p : 16 * p + 16, :] = two_terms(updated, 1)
    for p, value in second_step(boxes, hots, backs, padded1, field2, gathered, placed, local, nonlocal_, pot_ref, tables,
                                zst_ref, sums):
        out_ref[2 * p : 2 * p + 2] = (value - padded[p + 12, 8:24, :]).reshape(2, 8, 128)


XY = [pltpu.SMEM((8, 128), jnp.float32)] * 3
PADDED = pltpu.VMEM((36, 32, NZ), jnp.float32)
PADDED1 = pltpu.VMEM((24, 32, NZ), jnp.float32)
FIELD2 = pltpu.VMEM((576, 2 * NZ), jnp.bfloat16)
BOXED = [pltpu.VMEM((2, SPAN, 24, 128), jnp.float32)] * 3
PLANES = pltpu.VMEM((24, NY, NZ), jnp.float32)
WORK = pltpu.VMEM((BX, BY * NPROJ, 128), jnp.float32)
COPIES = pltpu.SemaphoreType.DMA((3,))


def parts_kernel(factors_ref, own_ref, other_ref, base_ref, one_ref, three_ref):
    own, other = own_ref[...], other_ref[...]
    for hop, target in ((0, base_ref), (1, one_ref), (3, three_ref)):
        target[...] = factors_ref[2 * hop] * own + factors_ref[2 * hop + 1] * other


def store_kernel(own_ref, out_ref):
    out_ref[...] = own_ref[...]


def most_kernel(factors_ref, base_ref, one_ref, three_ref, far_ref, out_ref):
    out_ref[...] = (base_ref[...] + factors_ref[4] * far_ref[...]) + (one_ref[...] + three_ref[...])


def total_kernel(factors_ref, most_ref, farsib_ref, out_ref):
    out_ref[...] = most_ref[...] + factors_ref[5] * farsib_ref[...]


def ring(axis, step):
    count = lax.axis_size(axis)
    return [(i, (i + step) % count) for i in range(count)]


def meet(axis, bits):
    return [(i, i ^ bits) for i in range(lax.axis_size(axis))]


def shards(orbitals, potential, atom_pos, atom_count, projectors, gammas, ritz):
    stay = lambda v: pltpu.with_memory_space_constraint(v, pltpu.HBM)
    up, down, pot, proj = call(
        pack_kernel,
        [shape(TILES, 8, 128), shape(TILES, 8, 128), shape(24, 8, 128), shape(3 * ATOMS, 8, 128)],
        [HBM] * 5 + [SMEM],
        (
            stay(orbitals.reshape(24, 8, 128)),
            stay(potential.reshape(24, 8, 128)),
            stay(projectors),
            stay(gammas.T),
            stay(atom_pos.T),
            atom_count,
        ),
        "pack",
        [pltpu.VMEM((NPROJ, ATOMS), jnp.float32), pltpu.VMEM((3, ATOMS), jnp.int32), pltpu.SemaphoreType.DMA((16,))],
    )
    low = lax.ppermute(up, "dom", ring("dom", 1))
    high = lax.ppermute(down, "dom", ring("dom", -1))
    table, zst, sums, hot, back, factors = call(
        prepare_kernel,
        [
            shape(2, PAIRS, 8, 128),
            shape(384, NZ, dtype=jnp.bfloat16),
            shape(LANES, LANES, dtype=jnp.bfloat16),
            shape(2 * NZ, LANES, dtype=jnp.bfloat16),
            shape(2 * LANES, NZ, dtype=jnp.bfloat16),
            shape(8, 8, 128),
        ],
        [VMEM] * 3,
        (proj, down, ritz),
        "prepare",
        [WORK],
    )
    highsib = lax.ppermute(high, "band", meet("band", 1))
    lowsib = lax.ppermute(low, "band", meet("band", 1))
    common = (down, high, low, pot, table, zst, sums, hot, back)
    halves, values, partial, hots, backs = call(
        head_kernel,
        [
            shape(2, PAIRS, 8, 128),
            shape(2, BX, 2, 8, 128),
            shape(24, NY, NZ),
            shape(2, 2 * NZ, LANES, dtype=jnp.bfloat16),
            shape(2, 2 * LANES, NZ, dtype=jnp.bfloat16),
        ],
        [VMEM] * 9,
        common,
        "head",
        XY + [PADDED, FIELD2, BOXED, BOXED, PLANES, WORK, COPIES],
        flops=10_000_000_000,
    )
    second, first, tables = call(
        tail_kernel,
        [shape(24, 8, 128), shape(24, NY, NZ), shape(2, 2, PAIRS, 8, 128)],
        [VMEM] * 16,
        common + (halves, values, partial, hots, backs, highsib, lowsib),
        "tail",
        XY + [PADDED1, FIELD2, BOXED, BOXED, PLANES, PLANES, WORK, COPIES],
    )
    low_y = lax.ppermute(second, "dom", ring("dom", 1))
    high_y = lax.ppermute(second, "dom", ring("dom", -1))
    (fourth,) = call(
        last_kernel,
        [shape(24, 8, 128)],
        [VMEM] * 16,
        common + (first, tables, hots, backs, second, high_y, low_y),
        "last",
        XY + [PADDED, PADDED1, FIELD2, BOXED, BOXED, PLANES, PLANES, COPIES],
    )
    far = lax.ppermute(fourth, "band", meet("band", 4))
    other = lax.ppermute(fourth, "band", meet("band", 1))
    field = shape(24, 8, 128)
    base, one, three = call(parts_kernel, [field] * 3, [VMEM] * 3, (factors, fourth, other), "parts")
    one = lax.ppermute(one, "band", meet("band", 2))
    three = lax.ppermute(three, "band", meet("band", 6))
    farsib = lax.ppermute(far, "band", meet("band", 1))
    (filtered,) = call(store_kernel, [field], [VMEM], (fourth,), "store", flops=0, moved=0)
    (most,) = call(most_kernel, [field], [VMEM] * 5, (factors, base, one, three, far), "most")
    (rotated,) = call(total_kernel, [field], [VMEM] * 3, (factors, most, farsib), "total")
    return (filtered.reshape(orbitals.shape), rotated.reshape(orbitals.shape))


def solution(mesh):
    in_specs = (
        P("band", "dom", None, None),
        P("dom", None, None),
        P("dom", None),
        P("dom"),
        P("dom", None, None),
        P("dom", None),
        P(),
    )
    out_specs = (P("band", "dom", None, None), P("band", "dom", None, None))
    return jax.shard_map(shards, mesh=mesh, in_specs=in_specs, out_specs=out_specs, check_vma=False)
```

```python
import jax
import jax.numpy as jnp
from jax import lax
from jax.experimental import pallas as pl
from jax.experimental.pallas import tpu as pltpu
from jax.sharding import PartitionSpec as P

STENCIL = (
    -5369.0 / 1800.0,
    12.0 / 7.0,
    -15.0 / 56.0,
    10.0 / 189.0,
    -1.0 / 112.0,
    2.0 / 1925.0,
    -1.0 / 16632.0,
)
LOWER = -1.6
UPPER = 24.0
CENTER = 0.5 * (UPPER + LOWER)
HALF = 0.5 * (UPPER - LOWER)

CX, NY, NZ = 12, 16, 128
ATOMS = 32
NPROJ, BX, BY, BZ = 8, 6, 8, 8
LANES = ATOMS * BZ
SPAN = CX + BX - 1
PAIRS = NPROJ * BX
TILE_Y, TILE_POT, TILE_P, TILE_META, TILES = 0, 24, 36, 84, 88
ROW_Z, ROW_X0, ROW_Y0 = 0, 1, 2

VMEM = pl.BlockSpec(memory_space=pltpu.VMEM)
HBM = pl.BlockSpec(memory_space=pltpu.HBM)
SMEM = pl.BlockSpec(memory_space=pltpu.SMEM)


def shape(*dims, dtype=jnp.float32):
    return jax.ShapeDtypeStruct(dims, dtype)


def call(kernel, outs, ins, args, name, scratch=(), out_specs=None, flops=1_000_000, moved=2_000_000):
    return pl.pallas_call(
        kernel,
        out_shape=outs,
        in_specs=ins,
        out_specs=out_specs or [VMEM] * len(outs),
        scratch_shapes=list(scratch),
        compiler_params=pltpu.CompilerParams(vmem_limit_bytes=32 * 2**20),
        cost_estimate=pl.CostEstimate(flops=flops, bytes_accessed=moved, transcendentals=0),
        name=name,
    )(*args)


def two_terms(value, axis):
    high = value.astype(jnp.bfloat16)
    low = (value - high.astype(jnp.float32)).astype(jnp.bfloat16)
    return jnp.concatenate([high, low], axis)


def dot(left, right):
    return jnp.dot(left, right, preferred_element_type=jnp.float32)


def half(tile):
    return slice(128 * tile, 128 * tile + 128)


def spread_projectors(read, work, *tables):
    lane = lax.broadcasted_iota(jnp.int32, (8, 128), 1)
    for part in range(3):
        items = [read(part, a) for a in range(16)]
        for bit in (1, 2, 4, 8):
            upper = (lane & (8 * bit)) != 0
            for p in range(16):
                if p & bit:
                    continue
                q = p | bit
                first, second = items[p], items[q]
                items[p] = jnp.where(upper, pltpu.roll(second, 8 * bit, 1), first)
                items[q] = jnp.where(upper, second, pltpu.roll(first, 128 - 8 * bit, 1))
        for g in range(16):
            i, j = 2 * part + g // 8, g % 8
            work[i, 8 * j : 8 * j + 8, :] = items[g]
    for i in range(BX):
        for l in range(NPROJ):
            laid = work.at[i][pl.ds(l, 8, stride=8), :]
            for table in tables:
                table[l * BX + i] = laid


def pack_kernel(y_hbm, pot_hbm, proj_hbm, gamma_hbm, pos_hbm, count_ref,
                up_ref, down_ref, pot_ref, rest_ref, gamma_ref, pos_ref, half_ref, work, sems):
    core = lax.axis_index("band") % 2
    copies = [
        pltpu.make_async_copy(gamma_hbm, gamma_ref, sems.at[0]),
        pltpu.make_async_copy(pos_hbm, pos_ref, sems.at[1]),
    ]
    moves = []
    for first, target in ((16 * core, half_ref), (16 - 16 * core, rest_ref)):
        for part in range(3):
            source = proj_hbm.at[pl.ds(first, 16), pl.ds(0, 8), pl.ds(128 * part, 128)]
            moves.append((source, target.at[pl.ds(16 * part, 16)]))
    moves.append((pot_hbm, pot_ref))
    for out, first in ((up_ref, 12), (down_ref, 0)):
        moves.append((y_hbm, out.at[pl.ds(TILE_Y, 24)]))
        moves.append((pot_hbm.at[pl.ds(first, 12)], out.at[pl.ds(TILE_POT, 12)]))
    for n, (source, target) in enumerate(moves):
        copies.append(pltpu.make_async_copy(source, target, sems.at[2 + n]))
    for copy in copies:
        copy.start()
    copies[0].wait()
    copies[1].wait()
    live = lax.broadcasted_iota(jnp.int32, (1, ATOMS), 1) < count_ref[0]
    weight = jnp.where(live, gamma_ref[...], 0.0)
    spread = lambda v, m: jnp.dot(v, m, preferred_element_type=jnp.float32, precision=lax.Precision.HIGHEST)
    atom = lax.broadcasted_iota(jnp.int32, (ATOMS, LANES), 0)
    lane = lax.broadcasted_iota(jnp.int32, (ATOMS, LANES), 1)
    repeat = jnp.where((lane >> 3) ^ (16 * core) == atom, 1.0, 0.0)
    order = jnp.where(lane[:, half(0)] ^ (16 * core) == atom[:, half(0)], 1.0, 0.0)
    corner = pos_ref[...].astype(jnp.float32)
    weight = spread(weight, repeat)
    column = spread(corner, repeat)[2:3] + (lax.broadcasted_iota(jnp.int32, (1, LANES), 1) & 7).astype(jnp.float32)
    column = jnp.where(column >= NZ, column - NZ, column)
    corner = spread(corner, order)
    for out in (up_ref, down_ref):
        for tile in range(2):
            out[TILE_META + 2 * tile] = weight[:, half(tile)]
            out[TILE_META + 2 * tile + 1] = jnp.broadcast_to(column[:, half(tile)], (8, 128))
        out[TILE_META + 1, ROW_X0 : ROW_X0 + 1, :] = corner[0:1]
        out[TILE_META + 1, ROW_Y0 : ROW_Y0 + 1, :] = corner[1:2]
    for copy in copies[2:5]:
        copy.wait()
    tables = [out.at[pl.ds(TILE_P, PAIRS)] for out in (up_ref, down_ref)]
    spread_projectors(lambda part, a: half_ref[16 * part + a], work, *tables)
    for copy in copies[5:]:
        copy.wait()


def prepare_kernel(rest_ref, up_ref, ritz_ref, table_ref, zst_ref, sums_ref, hot_ref, back_ref, factors_ref, work):
    write_one_hot(up_ref, hot_ref, back_ref)
    band = lax.axis_index("band")
    row = lax.broadcasted_iota(jnp.int32, (8, 8), 0)
    column = lax.broadcasted_iota(jnp.int32, (8, 8), 1)
    for hop in range(4):
        for n in range(2):
            orbital, to = (band ^ (4 + n), band) if hop == 2 else (band ^ n, band ^ (2 * hop))
            picked = jnp.where((row == orbital) & (column == to), ritz_ref[...], 0.0)
            picked = jnp.sum(jnp.sum(picked, 1, keepdims=True), 0, keepdims=True)
            factors_ref[2 * hop + n] = jnp.broadcast_to(picked, (8, 128))
    spread_projectors(lambda part, a: rest_ref[16 * part + a], work, table_ref)
    apart = lax.broadcasted_iota(jnp.int32, (NZ, NZ), 0) - lax.broadcasted_iota(jnp.int32, (NZ, NZ), 1)
    full = jnp.zeros((NZ, NZ), jnp.float32)
    for reach in range(1, 7):
        near = ((apart & (NZ - 1)) == reach) | ((apart & (NZ - 1)) == NZ - reach)
        full = jnp.where(near, STENCIL[reach], full)
    high = full.astype(jnp.bfloat16)
    zst_ref[0:128, :] = high
    zst_ref[128:256, :] = high
    zst_ref[256:384, :] = (full - high.astype(jnp.float32)).astype(jnp.bfloat16)
    atom = lambda axis: lax.broadcasted_iota(jnp.int32, (LANES, LANES), axis) >> 3
    sums_ref[...] = jnp.where(atom(0) == atom(1), 1.0, 0.0).astype(jnp.bfloat16)


def fill(padded, plane, value):
    count = value.shape[0]
    padded[plane : plane + count, 8:24, :] = value
    padded[plane : plane + count, 0:8, :] = value[:, 8:16]
    padded[plane : plane + count, 24:32, :] = value[:, 0:8]


class Boxes:
    def __init__(self, sources, held, sems):
        self.sources, self.held = sources, held
        self.copies = [
            pltpu.make_async_copy(s.at[TILE_META + 1], h, sems.at[n]) for n, (s, h) in enumerate(zip(sources, held))
        ]
        for copy in self.copies:
            copy.start()

    def wait(self):
        for copy in self.copies:
            copy.wait()

    def place(self, group, atom):
        held = self.held[group]
        return held[ROW_X0, atom].astype(jnp.int32), held[ROW_Y0, atom].astype(jnp.int32)

    def weight(self, group):
        source = self.sources[group]
        return jnp.concatenate([source[TILE_META], source[TILE_META + 2]], 1)


def write_one_hot(source, hot_ref, back_ref):
    column = jnp.concatenate([source[TILE_META + 1 + 2 * t, ROW_Z : ROW_Z + 1, :] for t in range(2)], 1)
    cells = lax.broadcasted_iota(jnp.int32, (NZ, LANES), 0).astype(jnp.float32)
    hot = jnp.where(cells == column, 1.0, 0.0)
    back = hot.T.astype(jnp.bfloat16)
    hot = hot.astype(jnp.bfloat16)
    for term in range(2):
        hot_ref[NZ * term : NZ * term + NZ, :] = hot
        back_ref[LANES * term : LANES * term + LANES, :] = back


def gather_columns(group, field2, first_in, planes_in, skip, gathered, onehot):
    rows = slice(NY * first_in, NY * (first_in + planes_in))
    columns = dot(field2[rows, :], onehot[...]).reshape(planes_in, NY, LANES)
    for tile in range(2):
        part = columns[:, :, half(tile)]
        gathered[group][tile, skip : skip + planes_in, 0:16, :] = part
        gathered[group][tile, skip : skip + planes_in, 16:24, :] = part[:, 0:8]


def read_windows(group, gathered, boxes):
    lane = lax.broadcasted_iota(jnp.int32, (8, 128), 1)
    values = [[jnp.zeros((8, 128), jnp.float32)] * 2 for _ in range(BX)]
    for a in range(16):
        mine = (lane >> 3) == a
        for tile in range(2):
            x0, y0 = boxes.place(group, 16 * tile + a)
            for i in range(BX):
                values[i][tile] = jnp.where(mine, gathered[group][tile, x0 + i, pl.ds(y0, 8), :], values[i][tile])
    return values


def contributions(group, values, table, placed, boxes, sums):
    coeffs = []
    for tile in range(2):
        rows = []
        for l in range(NPROJ):
            total = values[0][tile] * table[tile][l * BX]
            for i in range(1, BX):
                total = total + values[i][tile] * table[tile][l * BX + i]
            rows.append(jnp.sum(total, 0, keepdims=True))
        coeffs.append(jnp.concatenate(rows, 0))
    both = dot(two_terms(jnp.concatenate(coeffs, 1), 0), sums)
    coeffs = (both[:8] + both[8:]) * boxes.weight(group)
    lane = lax.broadcasted_iota(jnp.int32, (8, 128), 1)
    contrib = [[None] * 2 for _ in range(BX)]
    for tile in range(2):
        rows = [jnp.broadcast_to(coeffs[l : l + 1, half(tile)], (8, 128)) for l in range(NPROJ)]
        for i in range(BX):
            total = rows[0] * table[tile][i]
            for l in range(1, NPROJ):
                total = total + rows[l] * table[tile][l * BX + i]
            contrib[i][tile] = total
    for a in range(16):
        mine = (lane >> 3) == a
        for tile in range(2):
            x0, y0 = boxes.place(group, 16 * tile + a)
            for i in range(BX):
                pltpu.store(placed[group].at[tile, x0 + i, pl.ds(y0, 8), :], contrib[i][tile], mask=mine)


def spread_group(group, first, count, placed, back):
    planes = slice(first, first + count)
    tiles = []
    for tile in range(2):
        folded = placed[group][tile, planes, 0:8, :] + placed[group][tile, planes, 16:24, :]
        tiles.append(jnp.concatenate([folded, placed[group][tile, planes, 8:16, :]], 1).reshape(count * NY, 128))
    return dot(two_terms(jnp.concatenate(tiles, 1), 1), back[...]).reshape(count, NY, NZ)


def along_z(field2, rows, zst_ref):
    return dot(field2[rows, :], zst_ref[0:256, :]) + dot(field2[rows, 0:128], zst_ref[256:384, :])


def stencil_plane(padded, plane):
    total = 3.0 * STENCIL[0] * padded[plane, 8:24, :]
    for reach in range(1, 7):
        along_x = padded[plane + reach, 8:24, :] + padded[plane - reach, 8:24, :]
        along_y = padded[plane, 8 + reach : 24 + reach, :] + padded[plane, 8 - reach : 24 - reach, :]
        total = total + STENCIL[reach] * (along_x + along_y)
    return total


def potential_plane(p, low_ref, pot_ref, high_ref):
    source, tile = (
        (low_ref, TILE_POT + 2 * p) if p < 6 else (pot_ref, 2 * (p - 6)) if p < 18 else (high_ref, TILE_POT + 2 * (p - 18))
    )
    return source[tile : tile + 2].reshape(NY, NZ)


def clear(boxed):
    for ref in boxed:
        ref[...] = jnp.zeros_like(ref)


def laid(first, second):
    rows = pl.ds(TILE_P, PAIRS)
    return first.at[rows], second if second.shape[0] == PAIRS else second.at[rows]


def load_fields(fields, padded, field2):
    for n, value in enumerate(fields):
        fill(padded, 12 * n, value.reshape(CX, NY, NZ))
        field2[192 * n : 192 * n + 192, :] = two_terms(value.reshape(192, NZ), 1)


def head_kernel(up_ref, high_ref, low_ref, pot_ref, table_ref, zst_ref, sums_ref, hot_ref, back_ref,
                values_ref, partial_ref, hots_ref, backs_ref,
                low_xy, own_xy, high_xy, padded, field2, gathered, placed, local, sems):
    boxes = Boxes((low_ref, up_ref, high_ref), (low_xy, own_xy, high_xy), sems)
    load_fields([r[TILE_Y : TILE_Y + 24] for r in (low_ref, up_ref, high_ref)], padded, field2)
    clear(placed)
    gathered[2][:, 12:SPAN] = jnp.zeros((2, SPAN - 12, 24, 128), jnp.float32)
    for n, source in enumerate((low_ref, high_ref)):
        write_one_hot(source, hots_ref.at[n], backs_ref.at[n])
    gather_columns(1, field2, 12, SPAN, 0, gathered, hot_ref)
    gather_columns(0, field2, 0, SPAN, 0, gathered, hots_ref.at[0])
    gather_columns(2, field2, 24, 12, 0, gathered, hots_ref.at[1])
    local[...] = along_z(field2, slice(96, 480), zst_ref).reshape(24, NY, NZ)
    for p in range(24):
        laplace = stencil_plane(padded, p + 6) + local[p]
        pot = potential_plane(p, low_ref, pot_ref, high_ref)
        local[p] = (-0.5 * laplace + (pot - CENTER) * padded[p + 6, 8:24, :]) * (1.0 / HALF)
    boxes.wait()
    contributions(1, read_windows(1, gathered, boxes), laid(up_ref, table_ref), placed, boxes, sums_ref[...])
    for n, group in enumerate((0, 2)):
        values = read_windows(group, gathered, boxes)
        for i in range(BX):
            for tile in range(2):
                values_ref[n, i, tile] = values[i][tile]
    partial_ref[0:6] = local[0:6]
    partial_ref[6:23] = local[6:23] + spread_group(1, 0, 17, placed, back_ref) * (1.0 / HALF)
    partial_ref[23] = local[23]


def second_step(boxes, hots, backs, padded1, field2, gathered, placed, local, nonlocal_, pot_ref, tables, zst_ref, sums):
    for group, first, planes, skip in ((0, 0, 11, 6), (1, 6, SPAN, 0)):
        gather_columns(group, field2, first, planes, skip, gathered, hots[group])
    for group in range(2):
        contributions(group, read_windows(group, gathered, boxes), tables[group], placed, boxes, sums)
    local[0:12] = along_z(field2, slice(96, 288), zst_ref).reshape(12, NY, NZ)
    for p in range(12):
        here = padded1[p + 6, 8:24, :]
        laplace = stencil_plane(padded1, p + 6) + local[p]
        pot = potential_plane(p + 6, None, pot_ref, None)
        local[p] = -0.5 * laplace + (pot - CENTER) * here
    nonlocal_[0:12] = spread_group(1, 0, 12, placed, backs[1])
    nonlocal_[0:5] += spread_group(0, 12, 5, placed, backs[0])
    for p in range(12):
        yield p, (local[p] + nonlocal_[p]) * (2.0 / HALF)


def tail_kernel(up_ref, high_ref, low_ref, pot_ref, table_ref, zst_ref, sums_ref, hot_ref, back_ref,
                values_ref, partial_ref, hots_ref, backs_ref, highsib_ref, lowsib_ref,
                out_ref, kept_ref,
                low_xy, own_xy, high_xy, padded1, field2, gathered, placed, local, nonlocal_, sems):
    boxes = Boxes((low_ref, up_ref, high_ref), (low_xy, own_xy, high_xy), sems)
    clear(placed)
    gathered[0][:, 0:6] = jnp.zeros((2, 6, 24, 128), jnp.float32)
    tables = (laid(low_ref, lowsib_ref), laid(up_ref, table_ref), laid(high_ref, highsib_ref))
    hots, backs = (hots_ref.at[0], hot_ref), (backs_ref.at[0], back_ref, backs_ref.at[1])
    boxes.wait()
    sums = sums_ref[...]
    for n, group in enumerate((0, 2)):
        values = [[values_ref[n, i, tile] for tile in range(2)] for i in range(BX)]
        contributions(group, values, tables[group], placed, boxes, sums)
    nonlocal_[0:11] = spread_group(0, 6, 11, placed, backs[0])
    nonlocal_[11:18] = jnp.zeros((7, NY, NZ), jnp.float32)
    nonlocal_[18:24] = spread_group(2, 0, 6, placed, backs[2])
    for p in range(24):
        updated = partial_ref[p] + nonlocal_[p] * (1.0 / HALF)
        kept_ref[p] = updated
        fill(padded1, p, updated[None])
        field2[16 * p : 16 * p + 16, :] = two_terms(updated, 1)
    for p, value in second_step(boxes, hots, backs, padded1, field2, gathered, placed, local, nonlocal_, pot_ref, tables,
                                zst_ref, sums):
        out_ref[2 * p : 2 * p + 2] = (value - up_ref[TILE_Y + 2 * p : TILE_Y + 2 * p + 2].reshape(NY, NZ)).reshape(2, 8, 128)


def last_kernel(up_ref, high_ref, low_ref, pot_ref, table_ref, zst_ref, sums_ref, hot_ref, back_ref,
                kept_ref, hots_ref, backs_ref, highsib_ref, lowsib_ref,
                mid_ref, highy_ref, lowy_ref,
                out_ref,
                low_xy, own_xy, high_xy, padded, padded1, field2, gathered, placed, local, nonlocal_, sems):
    boxes = Boxes((low_ref, up_ref, high_ref), (low_xy, own_xy, high_xy), sems)
    load_fields([r[...] for r in (lowy_ref, mid_ref, highy_ref)], padded, field2)
    clear(placed)
    gathered[2][:, 12:SPAN] = jnp.zeros((2, SPAN - 12, 24, 128), jnp.float32)
    hots, backs = (hots_ref.at[0], hot_ref, hots_ref.at[1]), (backs_ref.at[0], back_ref, backs_ref.at[1])
    sums = sums_ref[...]
    tables = (laid(low_ref, lowsib_ref), laid(up_ref, table_ref), laid(high_ref, highsib_ref))
    for group, planes in ((0, SPAN), (1, SPAN), (2, 12)):
        gather_columns(group, field2, 12 * group, planes, 0, gathered, hots[group])
    local[...] = along_z(field2, slice(96, 480), zst_ref).reshape(24, NY, NZ)
    for p in range(24):
        laplace = stencil_plane(padded, p + 6) + local[p]
        pot = potential_plane(p, low_ref, pot_ref, high_ref)
        applied = -0.5 * laplace + (pot - CENTER) * padded[p + 6, 8:24, :]
        local[p] = applied * (2.0 / HALF) - kept_ref[p]
    boxes.wait()
    windows = [read_windows(group, gathered, boxes) for group in range(3)]
    for group in range(3):
        contributions(group, windows[group], tables[group], placed, boxes, sums)
    nonlocal_[0:11] = spread_group(0, 6, 11, placed, backs[0])
    nonlocal_[11:24] = jnp.zeros((13, NY, NZ), jnp.float32)
    nonlocal_[6:23] += spread_group(1, 0, 17, placed, backs[1])
    nonlocal_[18:24] += spread_group(2, 0, 6, placed, backs[2])
    for p in range(24):
        updated = local[p] + nonlocal_[p] * (2.0 / HALF)
        fill(padded1, p, updated[None])
        field2[16 * p : 16 * p + 16, :] = two_terms(updated, 1)
    for p, value in second_step(boxes, hots, backs, padded1, field2, gathered, placed, local, nonlocal_, pot_ref, tables,
                                zst_ref, sums):
        out_ref[2 * p : 2 * p + 2] = (value - padded[p + 12, 8:24, :]).reshape(2, 8, 128)


XY = [pltpu.SMEM((8, 128), jnp.float32)] * 3
PADDED = pltpu.VMEM((36, 32, NZ), jnp.float32)
PADDED1 = pltpu.VMEM((24, 32, NZ), jnp.float32)
FIELD2 = pltpu.VMEM((576, 2 * NZ), jnp.bfloat16)
BOXED = [pltpu.VMEM((2, SPAN, 24, 128), jnp.float32)] * 3
PLANES = pltpu.VMEM((24, NY, NZ), jnp.float32)
WORK = pltpu.VMEM((BX, BY * NPROJ, 128), jnp.float32)
COPIES = pltpu.SemaphoreType.DMA((3,))


def parts_kernel(factors_ref, own_ref, other_ref, base_ref, one_ref, three_ref):
    own, other = own_ref[...], other_ref[...]
    for hop, target in ((0, base_ref), (1, one_ref), (3, three_ref)):
        target[...] = factors_ref[2 * hop] * own + factors_ref[2 * hop + 1] * other


def store_kernel(own_ref, out_ref):
    out_ref[...] = own_ref[...]


def most_kernel(factors_ref, base_ref, one_ref, three_ref, far_ref, out_ref):
    out_ref[...] = (base_ref[...] + factors_ref[4] * far_ref[...]) + (one_ref[...] + three_ref[...])


def total_kernel(factors_ref, most_ref, farsib_ref, out_ref):
    out_ref[...] = most_ref[...] + factors_ref[5] * farsib_ref[...]


def ring(axis, step):
    count = lax.axis_size(axis)
    return [(i, (i + step) % count) for i in range(count)]


def meet(axis, bits):
    return [(i, i ^ bits) for i in range(lax.axis_size(axis))]


def shards(orbitals, potential, atom_pos, atom_count, projectors, gammas, ritz):
    stay = lambda v: pltpu.with_memory_space_constraint(v, pltpu.HBM)
    up, down, pot, rest = call(
        pack_kernel,
        [shape(TILES, 8, 128), shape(TILES, 8, 128), shape(24, 8, 128), shape(PAIRS, 8, 128)],
        [HBM] * 5 + [SMEM],
        (
            stay(orbitals.reshape(24, 8, 128)),
            stay(potential.reshape(24, 8, 128)),
            stay(projectors),
            stay(gammas.T),
            stay(atom_pos.T),
            atom_count,
        ),
        "pack",
        [
            pltpu.VMEM((NPROJ, ATOMS), jnp.float32),
            pltpu.VMEM((3, ATOMS), jnp.int32),
            pltpu.VMEM((PAIRS, 8, 128), jnp.float32),
            WORK,
            pltpu.SemaphoreType.DMA((13,)),
        ],
    )
    low = lax.ppermute(up, "dom", ring("dom", 1))
    high = lax.ppermute(down, "dom", ring("dom", -1))
    table, zst, sums, hot, back, factors = call(
        prepare_kernel,
        [
            shape(PAIRS, 8, 128),
            shape(384, NZ, dtype=jnp.bfloat16),
            shape(LANES, LANES, dtype=jnp.bfloat16),
            shape(2 * NZ, LANES, dtype=jnp.bfloat16),
            shape(2 * LANES, NZ, dtype=jnp.bfloat16),
            shape(8, 8, 128),
        ],
        [VMEM] * 3,
        (rest, down, ritz),
        "prepare",
        [WORK],
    )
    highsib = lax.ppermute(high, "band", meet("band", 1))
    lowsib = lax.ppermute(low, "band", meet("band", 1))
    common = (down, high, low, pot, table, zst, sums, hot, back)
    values, partial, hots, backs = call(
        head_kernel,
        [
            shape(2, BX, 2, 8, 128),
            shape(24, NY, NZ),
            shape(2, 2 * NZ, LANES, dtype=jnp.bfloat16),
            shape(2, 2 * LANES, NZ, dtype=jnp.bfloat16),
        ],
        [VMEM] * 9,
        common,
        "head",
        XY + [PADDED, FIELD2, BOXED, BOXED, PLANES, COPIES],
        flops=10_000_000_000,
    )
    second, first = call(
        tail_kernel,
        [shape(24, 8, 128), shape(24, NY, NZ)],
        [VMEM] * 15,
        common + (values, partial, hots, backs, highsib, lowsib),
        "tail",
        XY + [PADDED1, FIELD2, BOXED, BOXED, PLANES, PLANES, COPIES],
    )
    low_y = lax.ppermute(second, "dom", ring("dom", 1))
    high_y = lax.ppermute(second, "dom", ring("dom", -1))
    (fourth,) = call(
        last_kernel,
        [shape(24, 8, 128)],
        [VMEM] * 17,
        common + (first, hots, backs, highsib, lowsib, second, high_y, low_y),
        "last",
        XY + [PADDED, PADDED1, FIELD2, BOXED, BOXED, PLANES, PLANES, COPIES],
    )
    far = lax.ppermute(fourth, "band", meet("band", 4))
    other = lax.ppermute(fourth, "band", meet("band", 1))
    field = shape(24, 8, 128)
    base, one, three = call(parts_kernel, [field] * 3, [VMEM] * 3, (factors, fourth, other), "parts")
    one = lax.ppermute(one, "band", meet("band", 2))
    three = lax.ppermute(three, "band", meet("band", 6))
    farsib = lax.ppermute(far, "band", meet("band", 1))
    (filtered,) = call(store_kernel, [field], [VMEM], (fourth,), "store", flops=0, moved=0)
    (most,) = call(most_kernel, [field], [VMEM] * 5, (factors, base, one, three, far), "most")
    (rotated,) = call(total_kernel, [field], [VMEM] * 3, (factors, most, farsib), "total")
    return (filtered.reshape(orbitals.shape), rotated.reshape(orbitals.shape))


def solution(mesh):
    in_specs = (
        P("band", "dom", None, None),
        P("dom", None, None),
        P("dom", None),
        P("dom"),
        P("dom", None, None),
        P("dom", None),
        P(),
    )
    out_specs = (P("band", "dom", None, None), P("band", "dom", None, None))
    return jax.shard_map(shards, mesh=mesh, in_specs=in_specs, out_specs=out_specs, check_vma=False)
```

```python
import jax
import jax.numpy as jnp
from jax import lax
from jax.experimental import pallas as pl
from jax.experimental.pallas import tpu as pltpu
from jax.sharding import PartitionSpec as P

STENCIL = (
    -5369.0 / 1800.0,
    12.0 / 7.0,
    -15.0 / 56.0,
    10.0 / 189.0,
    -1.0 / 112.0,
    2.0 / 1925.0,
    -1.0 / 16632.0,
)
LOWER = -1.6
UPPER = 24.0
CENTER = 0.5 * (UPPER + LOWER)
HALF = 0.5 * (UPPER - LOWER)

CX, NY, NZ = 12, 16, 128
ATOMS = 32
NPROJ, BX, BY, BZ = 8, 6, 8, 8
LANES = ATOMS * BZ
SPAN = CX + BX - 1
PAIRS = NPROJ * BX
TILE_Y, TILE_POT, TILE_P, TILE_META, TILES = 0, 24, 36, 84, 88
ROW_Z, ROW_X0, ROW_Y0 = 0, 1, 2

VMEM = pl.BlockSpec(memory_space=pltpu.VMEM)
HBM = pl.BlockSpec(memory_space=pltpu.HBM)
SMEM = pl.BlockSpec(memory_space=pltpu.SMEM)


def shape(*dims, dtype=jnp.float32):
    return jax.ShapeDtypeStruct(dims, dtype)


def call(kernel, outs, ins, args, name, scratch=(), out_specs=None, flops=1_000_000, moved=2_000_000):
    return pl.pallas_call(
        kernel,
        out_shape=outs,
        in_specs=ins,
        out_specs=out_specs or [VMEM] * len(outs),
        scratch_shapes=list(scratch),
        compiler_params=pltpu.CompilerParams(vmem_limit_bytes=32 * 2**20),
        cost_estimate=pl.CostEstimate(flops=flops, bytes_accessed=moved, transcendentals=0),
        name=name,
    )(*args)


def two_terms(value, axis):
    high = value.astype(jnp.bfloat16)
    low = (value - high.astype(jnp.float32)).astype(jnp.bfloat16)
    return jnp.concatenate([high, low], axis)


def dot(left, right):
    return jnp.dot(left, right, preferred_element_type=jnp.float32)


def half(tile):
    return slice(128 * tile, 128 * tile + 128)


def spread_projectors(read, work, *tables):
    lane = lax.broadcasted_iota(jnp.int32, (8, 128), 1)
    for part in range(3):
        items = [read(part, a) for a in range(16)]
        for bit in (1, 2, 4, 8):
            upper = (lane & (8 * bit)) != 0
            for p in range(16):
                if p & bit:
                    continue
                q = p | bit
                first, second = items[p], items[q]
                items[p] = jnp.where(upper, pltpu.roll(second, 8 * bit, 1), first)
                items[q] = jnp.where(upper, second, pltpu.roll(first, 128 - 8 * bit, 1))
        for g in range(16):
            i, j = 2 * part + g // 8, g % 8
            work[i, 8 * j : 8 * j + 8, :] = items[g]
    for i in range(BX):
        for l in range(NPROJ):
            laid = work.at[i][pl.ds(l, 8, stride=8), :]
            for table in tables:
                table[l * BX + i] = laid


def pack_kernel(y_hbm, pot_hbm, proj_hbm, gamma_hbm, pos_hbm, count_ref,
                far_ref, near_ref, pot_ref, rest_ref, gamma_ref, pos_ref, half_ref, work, sems):
    core = lax.axis_index("band") % 2
    odd = lax.axis_index("dom") % 2
    copies = [
        pltpu.make_async_copy(gamma_hbm, gamma_ref, sems.at[0]),
        pltpu.make_async_copy(pos_hbm, pos_ref, sems.at[1]),
    ]
    moves = []
    for first, target in ((16 * core, half_ref), (16 - 16 * core, rest_ref)):
        for part in range(3):
            source = proj_hbm.at[pl.ds(first, 16), pl.ds(0, 8), pl.ds(128 * part, 128)]
            moves.append((source, target.at[pl.ds(16 * part, 16)]))
    moves.append((pot_hbm, pot_ref))
    for out, first in ((far_ref, 12 * odd), (near_ref, 12 - 12 * odd)):
        moves.append((y_hbm, out.at[pl.ds(TILE_Y, 24)]))
        moves.append((pot_hbm.at[pl.ds(first, 12)], out.at[pl.ds(TILE_POT, 12)]))
    for n, (source, target) in enumerate(moves):
        copies.append(pltpu.make_async_copy(source, target, sems.at[2 + n]))
    for copy in copies:
        copy.start()
    copies[0].wait()
    copies[1].wait()
    live = lax.broadcasted_iota(jnp.int32, (1, ATOMS), 1) < count_ref[0]
    weight = jnp.where(live, gamma_ref[...], 0.0)
    spread = lambda v, m: jnp.dot(v, m, preferred_element_type=jnp.float32, precision=lax.Precision.HIGHEST)
    atom = lax.broadcasted_iota(jnp.int32, (ATOMS, LANES), 0)
    lane = lax.broadcasted_iota(jnp.int32, (ATOMS, LANES), 1)
    repeat = jnp.where((lane >> 3) ^ (16 * core) == atom, 1.0, 0.0)
    order = jnp.where(lane[:, half(0)] ^ (16 * core) == atom[:, half(0)], 1.0, 0.0)
    corner = pos_ref[...].astype(jnp.float32)
    weight = spread(weight, repeat)
    column = spread(corner, repeat)[2:3] + (lax.broadcasted_iota(jnp.int32, (1, LANES), 1) & 7).astype(jnp.float32)
    column = jnp.where(column >= NZ, column - NZ, column)
    corner = spread(corner, order)
    for out in (far_ref, near_ref):
        for tile in range(2):
            out[TILE_META + 2 * tile] = weight[:, half(tile)]
            out[TILE_META + 2 * tile + 1] = jnp.broadcast_to(column[:, half(tile)], (8, 128))
        out[TILE_META + 1, ROW_X0 : ROW_X0 + 1, :] = corner[0:1]
        out[TILE_META + 1, ROW_Y0 : ROW_Y0 + 1, :] = corner[1:2]
    for copy in copies[2:5]:
        copy.wait()
    tables = [out.at[pl.ds(TILE_P, PAIRS)] for out in (far_ref, near_ref)]
    spread_projectors(lambda part, a: half_ref[16 * part + a], work, *tables)
    for copy in copies[5:]:
        copy.wait()


def prepare_kernel(rest_ref, up_ref, ritz_ref, table_ref, zst_ref, sums_ref, hot_ref, back_ref, factors_ref, work):
    write_one_hot(up_ref, hot_ref, back_ref)
    band = lax.axis_index("band")
    row = lax.broadcasted_iota(jnp.int32, (8, 8), 0)
    column = lax.broadcasted_iota(jnp.int32, (8, 8), 1)
    for hop in range(4):
        for n in range(2):
            orbital, to = (band ^ (4 + n), band) if hop == 2 else (band ^ n, band ^ (2 * hop))
            picked = jnp.where((row == orbital) & (column == to), ritz_ref[...], 0.0)
            picked = jnp.sum(jnp.sum(picked, 1, keepdims=True), 0, keepdims=True)
            factors_ref[2 * hop + n] = jnp.broadcast_to(picked, (8, 128))
    spread_projectors(lambda part, a: rest_ref[16 * part + a], work, table_ref)
    apart = lax.broadcasted_iota(jnp.int32, (NZ, NZ), 0) - lax.broadcasted_iota(jnp.int32, (NZ, NZ), 1)
    full = jnp.zeros((NZ, NZ), jnp.float32)
    for reach in range(1, 7):
        near = ((apart & (NZ - 1)) == reach) | ((apart & (NZ - 1)) == NZ - reach)
        full = jnp.where(near, STENCIL[reach], full)
    high = full.astype(jnp.bfloat16)
    zst_ref[0:128, :] = high
    zst_ref[128:256, :] = high
    zst_ref[256:384, :] = (full - high.astype(jnp.float32)).astype(jnp.bfloat16)
    atom = lambda axis: lax.broadcasted_iota(jnp.int32, (LANES, LANES), axis) >> 3
    sums_ref[...] = jnp.where(atom(0) == atom(1), 1.0, 0.0).astype(jnp.bfloat16)


def fill(padded, plane, value):
    count = value.shape[0]
    padded[plane : plane + count, 8:24, :] = value
    padded[plane : plane + count, 0:8, :] = value[:, 8:16]
    padded[plane : plane + count, 24:32, :] = value[:, 0:8]


class Side:
    def __init__(self, far, near, share):
        self.far, self.near, self.share = far, near, share
        self.shape = far.shape

    def __getitem__(self, index):
        return self.far[index] * self.share + self.near[index] * (1.0 - self.share)

    def rows(self, rows):
        return Side(self.far.at[rows], self.near.at[rows], self.share)


def sides(far, near):
    odd = (lax.axis_index("dom") % 2).astype(jnp.float32)
    return Side(far, near, 1.0 - odd), Side(far, near, odd)


class Boxes:
    def __init__(self, far, own, near, held, sems):
        low, high = sides(far, near)
        self.sources, self.held = (low, own, high), held
        odd = lax.axis_index("dom") % 2
        self.copies = [
            pltpu.make_async_copy(source.at[TILE_META + 1], held.at[slot], sems.at[n])
            for n, (source, slot) in enumerate(((far, 2 * odd), (own, 1), (near, 2 - 2 * odd)))
        ]
        for copy in self.copies:
            copy.start()

    def wait(self):
        for copy in self.copies:
            copy.wait()

    def place(self, group, atom):
        return self.held[group, ROW_X0, atom].astype(jnp.int32), self.held[group, ROW_Y0, atom].astype(jnp.int32)

    def weight(self, group):
        source = self.sources[group]
        return jnp.concatenate([source[TILE_META], source[TILE_META + 2]], 1)


def write_one_hot(source, hot_ref, back_ref):
    column = jnp.concatenate([source[TILE_META + 1 + 2 * t, ROW_Z : ROW_Z + 1, :] for t in range(2)], 1)
    cells = lax.broadcasted_iota(jnp.int32, (NZ, LANES), 0).astype(jnp.float32)
    hot = jnp.where(cells == column, 1.0, 0.0)
    back = hot.T.astype(jnp.bfloat16)
    hot = hot.astype(jnp.bfloat16)
    for term in range(2):
        hot_ref[NZ * term : NZ * term + NZ, :] = hot
        back_ref[LANES * term : LANES * term + LANES, :] = back


def gather_columns(group, field2, first_in, planes_in, skip, gathered, onehot):
    rows = slice(NY * first_in, NY * (first_in + planes_in))
    columns = dot(field2[rows, :], onehot[...]).reshape(planes_in, NY, LANES)
    for tile in range(2):
        part = columns[:, :, half(tile)]
        gathered[group][tile, skip : skip + planes_in, 0:16, :] = part
        gathered[group][tile, skip : skip + planes_in, 16:24, :] = part[:, 0:8]


def read_windows(group, gathered, boxes):
    lane = lax.broadcasted_iota(jnp.int32, (8, 128), 1)
    values = [[jnp.zeros((8, 128), jnp.float32)] * 2 for _ in range(BX)]
    for a in range(16):
        mine = (lane >> 3) == a
        for tile in range(2):
            x0, y0 = boxes.place(group, 16 * tile + a)
            for i in range(BX):
                values[i][tile] = jnp.where(mine, gathered[group][tile, x0 + i, pl.ds(y0, 8), :], values[i][tile])
    return values


def contributions(group, values, table, placed, boxes, sums):
    coeffs = []
    for tile in range(2):
        rows = []
        for l in range(NPROJ):
            total = values[0][tile] * table[tile][l * BX]
            for i in range(1, BX):
                total = total + values[i][tile] * table[tile][l * BX + i]
            rows.append(jnp.sum(total, 0, keepdims=True))
        coeffs.append(jnp.concatenate(rows, 0))
    both = dot(two_terms(jnp.concatenate(coeffs, 1), 0), sums)
    coeffs = (both[:8] + both[8:]) * boxes.weight(group)
    lane = lax.broadcasted_iota(jnp.int32, (8, 128), 1)
    contrib = [[None] * 2 for _ in range(BX)]
    for tile in range(2):
        rows = [jnp.broadcast_to(coeffs[l : l + 1, half(tile)], (8, 128)) for l in range(NPROJ)]
        for i in range(BX):
            total = rows[0] * table[tile][i]
            for l in range(1, NPROJ):
                total = total + rows[l] * table[tile][l * BX + i]
            contrib[i][tile] = total
    for a in range(16):
        mine = (lane >> 3) == a
        for tile in range(2):
            x0, y0 = boxes.place(group, 16 * tile + a)
            for i in range(BX):
                pltpu.store(placed[group].at[tile, x0 + i, pl.ds(y0, 8), :], contrib[i][tile], mask=mine)


def spread_group(group, first, count, placed, back):
    planes = slice(first, first + count)
    tiles = []
    for tile in range(2):
        folded = placed[group][tile, planes, 0:8, :] + placed[group][tile, planes, 16:24, :]
        tiles.append(jnp.concatenate([folded, placed[group][tile, planes, 8:16, :]], 1).reshape(count * NY, 128))
    return dot(two_terms(jnp.concatenate(tiles, 1), 1), back[...]).reshape(count, NY, NZ)


def along_z(field2, rows, zst_ref):
    return dot(field2[rows, :], zst_ref[0:256, :]) + dot(field2[rows, 0:128], zst_ref[256:384, :])


def stencil_plane(padded, plane):
    total = 3.0 * STENCIL[0] * padded[plane, 8:24, :]
    for reach in range(1, 7):
        along_x = padded[plane + reach, 8:24, :] + padded[plane - reach, 8:24, :]
        along_y = padded[plane, 8 + reach : 24 + reach, :] + padded[plane, 8 - reach : 24 - reach, :]
        total = total + STENCIL[reach] * (along_x + along_y)
    return total


def potential_plane(p, low_ref, pot_ref, high_ref):
    source, tile = (
        (low_ref, TILE_POT + 2 * p) if p < 6 else (pot_ref, 2 * (p - 6)) if p < 18 else (high_ref, TILE_POT + 2 * (p - 18))
    )
    return source[tile : tile + 2].reshape(NY, NZ)


def clear(boxed):
    for ref in boxed:
        ref[...] = jnp.zeros_like(ref)


def laid(first, second):
    rows = pl.ds(TILE_P, PAIRS)
    return tuple(v.rows(rows) if isinstance(v, Side) else v if v.shape[0] == PAIRS else v.at[rows] for v in (first, second))


def load_fields(fields, padded, field2):
    for n, value in enumerate(fields):
        fill(padded, 12 * n, value.reshape(CX, NY, NZ))
        field2[192 * n : 192 * n + 192, :] = two_terms(value.reshape(192, NZ), 1)


def head_kernel(up_ref, near_ref, far_ref, pot_ref, table_ref, zst_ref, sums_ref, hot_ref, back_ref,
                values_ref, partial_ref, hots_ref, backs_ref,
                xy, padded, field2, gathered, placed, local, sems):
    boxes = Boxes(far_ref, up_ref, near_ref, xy, sems)
    low_ref, high_ref = sides(far_ref, near_ref)
    load_fields([r[TILE_Y : TILE_Y + 24] for r in (low_ref, up_ref, high_ref)], padded, field2)
    clear(placed)
    gathered[2][:, 12:SPAN] = jnp.zeros((2, SPAN - 12, 24, 128), jnp.float32)
    for n, source in enumerate((low_ref, high_ref)):
        write_one_hot(source, hots_ref.at[n], backs_ref.at[n])
    gather_columns(1, field2, 12, SPAN, 0, gathered, hot_ref)
    gather_columns(0, field2, 0, SPAN, 0, gathered, hots_ref.at[0])
    gather_columns(2, field2, 24, 12, 0, gathered, hots_ref.at[1])
    local[...] = along_z(field2, slice(96, 480), zst_ref).reshape(24, NY, NZ)
    for p in range(24):
        laplace = stencil_plane(padded, p + 6) + local[p]
        pot = potential_plane(p, low_ref, pot_ref, high_ref)
        local[p] = (-0.5 * laplace + (pot - CENTER) * padded[p + 6, 8:24, :]) * (1.0 / HALF)
    boxes.wait()
    contributions(1, read_windows(1, gathered, boxes), laid(up_ref, table_ref), placed, boxes, sums_ref[...])
    for n, group in enumerate((0, 2)):
        values = read_windows(group, gathered, boxes)
        for i in range(BX):
            for tile in range(2):
                values_ref[n, i, tile] = values[i][tile]
    partial_ref[0:6] = local[0:6]
    partial_ref[6:23] = local[6:23] + spread_group(1, 0, 17, placed, back_ref) * (1.0 / HALF)
    partial_ref[23] = local[23]


def second_step(boxes, hots, backs, padded1, field2, gathered, placed, local, nonlocal_, pot_ref, tables, zst_ref, sums):
    for group, first, planes, skip in ((0, 0, 11, 6), (1, 6, SPAN, 0)):
        gather_columns(group, field2, first, planes, skip, gathered, hots[group])
    for group in range(2):
        contributions(group, read_windows(group, gathered, boxes), tables[group], placed, boxes, sums)
    local[0:12] = along_z(field2, slice(96, 288), zst_ref).reshape(12, NY, NZ)
    for p in range(12):
        here = padded1[p + 6, 8:24, :]
        laplace = stencil_plane(padded1, p + 6) + local[p]
        pot = potential_plane(p + 6, None, pot_ref, None)
        local[p] = -0.5 * laplace + (pot - CENTER) * here
    nonlocal_[0:12] = spread_group(1, 0, 12, placed, backs[1])
    nonlocal_[0:5] += spread_group(0, 12, 5, placed, backs[0])
    for p in range(12):
        yield p, (local[p] + nonlocal_[p]) * (2.0 / HALF)


def tail_kernel(up_ref, near_ref, far_ref, pot_ref, table_ref, zst_ref, sums_ref, hot_ref, back_ref,
                values_ref, partial_ref, hots_ref, backs_ref, nearsib_ref, farsib_ref,
                out_ref, kept_ref,
                xy, padded1, field2, gathered, placed, local, nonlocal_, sems):
    boxes = Boxes(far_ref, up_ref, near_ref, xy, sems)
    low_ref, high_ref = sides(far_ref, near_ref)
    lowsib_ref, highsib_ref = sides(farsib_ref, nearsib_ref)
    clear(placed)
    gathered[0][:, 0:6] = jnp.zeros((2, 6, 24, 128), jnp.float32)
    tables = (laid(low_ref, lowsib_ref), laid(up_ref, table_ref), laid(high_ref, highsib_ref))
    hots, backs = (hots_ref.at[0], hot_ref), (backs_ref.at[0], back_ref, backs_ref.at[1])
    boxes.wait()
    sums = sums_ref[...]
    for n, group in enumerate((0, 2)):
        values = [[values_ref[n, i, tile] for tile in range(2)] for i in range(BX)]
        contributions(group, values, tables[group], placed, boxes, sums)
    nonlocal_[0:11] = spread_group(0, 6, 11, placed, backs[0])
    nonlocal_[11:18] = jnp.zeros((7, NY, NZ), jnp.float32)
    nonlocal_[18:24] = spread_group(2, 0, 6, placed, backs[2])
    for p in range(24):
        updated = partial_ref[p] + nonlocal_[p] * (1.0 / HALF)
        kept_ref[p] = updated
        fill(padded1, p, updated[None])
        field2[16 * p : 16 * p + 16, :] = two_terms(updated, 1)
    for p, value in second_step(boxes, hots, backs, padded1, field2, gathered, placed, local, nonlocal_, pot_ref, tables,
                                zst_ref, sums):
        out_ref[2 * p : 2 * p + 2] = (value - up_ref[TILE_Y + 2 * p : TILE_Y + 2 * p + 2].reshape(NY, NZ)).reshape(2, 8, 128)


def last_kernel(up_ref, near_ref, far_ref, pot_ref, table_ref, zst_ref, sums_ref, hot_ref, back_ref,
                kept_ref, hots_ref, backs_ref, nearsib_ref, farsib_ref,
                mid_ref, neary_ref, fary_ref,
                out_ref,
                xy, padded, padded1, field2, gathered, placed, local, nonlocal_, sems):
    boxes = Boxes(far_ref, up_ref, near_ref, xy, sems)
    low_ref, high_ref = sides(far_ref, near_ref)
    lowy_ref, highy_ref = sides(fary_ref, neary_ref)
    lowsib_ref, highsib_ref = sides(farsib_ref, nearsib_ref)
    load_fields([r[...] for r in (lowy_ref, mid_ref, highy_ref)], padded, field2)
    clear(placed)
    gathered[2][:, 12:SPAN] = jnp.zeros((2, SPAN - 12, 24, 128), jnp.float32)
    hots, backs = (hots_ref.at[0], hot_ref, hots_ref.at[1]), (backs_ref.at[0], back_ref, backs_ref.at[1])
    sums = sums_ref[...]
    tables = (laid(low_ref, lowsib_ref), laid(up_ref, table_ref), laid(high_ref, highsib_ref))
    for group, planes in ((0, SPAN), (1, SPAN), (2, 12)):
        gather_columns(group, field2, 12 * group, planes, 0, gathered, hots[group])
    local[...] = along_z(field2, slice(96, 480), zst_ref).reshape(24, NY, NZ)
    for p in range(24):
        laplace = stencil_plane(padded, p + 6) + local[p]
        pot = potential_plane(p, low_ref, pot_ref, high_ref)
        applied = -0.5 * laplace + (pot - CENTER) * padded[p + 6, 8:24, :]
        local[p] = applied * (2.0 / HALF) - kept_ref[p]
    boxes.wait()
    windows = [read_windows(group, gathered, boxes) for group in range(3)]
    for group in range(3):
        contributions(group, windows[group], tables[group], placed, boxes, sums)
    nonlocal_[0:11] = spread_group(0, 6, 11, placed, backs[0])
    nonlocal_[11:24] = jnp.zeros((13, NY, NZ), jnp.float32)
    nonlocal_[6:23] += spread_group(1, 0, 17, placed, backs[1])
    nonlocal_[18:24] += spread_group(2, 0, 6, placed, backs[2])
    for p in range(24):
        updated = local[p] + nonlocal_[p] * (2.0 / HALF)
        fill(padded1, p, updated[None])
        field2[16 * p : 16 * p + 16, :] = two_terms(updated, 1)
    for p, value in second_step(boxes, hots, backs, padded1, field2, gathered, placed, local, nonlocal_, pot_ref, tables,
                                zst_ref, sums):
        out_ref[2 * p : 2 * p + 2] = (value - padded[p + 12, 8:24, :]).reshape(2, 8, 128)


XY = [pltpu.SMEM((3, 8, 128), jnp.float32)]
PADDED = pltpu.VMEM((36, 32, NZ), jnp.float32)
PADDED1 = pltpu.VMEM((24, 32, NZ), jnp.float32)
FIELD2 = pltpu.VMEM((576, 2 * NZ), jnp.bfloat16)
BOXED = [pltpu.VMEM((2, SPAN, 24, 128), jnp.float32)] * 3
PLANES = pltpu.VMEM((24, NY, NZ), jnp.float32)
WORK = pltpu.VMEM((BX, BY * NPROJ, 128), jnp.float32)
COPIES = pltpu.SemaphoreType.DMA((3,))


def parts_kernel(factors_ref, own_ref, other_ref, base_ref, one_ref, three_ref):
    own, other = own_ref[...], other_ref[...]
    for hop, target in ((0, base_ref), (1, one_ref), (3, three_ref)):
        target[...] = factors_ref[2 * hop] * own + factors_ref[2 * hop + 1] * other


def store_kernel(own_ref, out_ref):
    out_ref[...] = own_ref[...]


def most_kernel(factors_ref, base_ref, one_ref, three_ref, far_ref, out_ref):
    out_ref[...] = (base_ref[...] + factors_ref[4] * far_ref[...]) + (one_ref[...] + three_ref[...])


def total_kernel(factors_ref, most_ref, farsib_ref, out_ref):
    out_ref[...] = most_ref[...] + factors_ref[5] * farsib_ref[...]


def couples(first):
    count = lax.axis_size("dom")
    pairs = [(i % count, (i + 1) % count) for i in range(first, first + count, 2)]
    return pairs + [(target, source) for source, target in pairs]


def meet(axis, bits):
    return [(i, i ^ bits) for i in range(lax.axis_size(axis))]


def shards(orbitals, potential, atom_pos, atom_count, projectors, gammas, ritz):
    stay = lambda v: pltpu.with_memory_space_constraint(v, pltpu.HBM)
    far, near, pot, rest = call(
        pack_kernel,
        [shape(TILES, 8, 128), shape(TILES, 8, 128), shape(24, 8, 128), shape(PAIRS, 8, 128)],
        [HBM] * 5 + [SMEM],
        (
            stay(orbitals.reshape(24, 8, 128)),
            stay(potential.reshape(24, 8, 128)),
            stay(projectors),
            stay(gammas.T),
            stay(atom_pos.T),
            atom_count,
        ),
        "pack",
        [
            pltpu.VMEM((NPROJ, ATOMS), jnp.float32),
            pltpu.VMEM((3, ATOMS), jnp.int32),
            pltpu.VMEM((PAIRS, 8, 128), jnp.float32),
            WORK,
            pltpu.SemaphoreType.DMA((13,)),
        ],
    )
    from_far = lax.ppermute(far, "dom", couples(1))
    from_near = lax.ppermute(near, "dom", couples(0))
    table, zst, sums, hot, back, factors = call(
        prepare_kernel,
        [
            shape(PAIRS, 8, 128),
            shape(384, NZ, dtype=jnp.bfloat16),
            shape(LANES, LANES, dtype=jnp.bfloat16),
            shape(2 * NZ, LANES, dtype=jnp.bfloat16),
            shape(2 * LANES, NZ, dtype=jnp.bfloat16),
            shape(8, 8, 128),
        ],
        [VMEM] * 3,
        (rest, near, ritz),
        "prepare",
        [WORK],
    )
    nearsib = lax.ppermute(from_near, "band", meet("band", 1))
    farsib = lax.ppermute(from_far, "band", meet("band", 1))
    common = (near, from_near, from_far, pot, table, zst, sums, hot, back)
    values, partial, hots, backs = call(
        head_kernel,
        [
            shape(2, BX, 2, 8, 128),
            shape(24, NY, NZ),
            shape(2, 2 * NZ, LANES, dtype=jnp.bfloat16),
            shape(2, 2 * LANES, NZ, dtype=jnp.bfloat16),
        ],
        [VMEM] * 9,
        common,
        "head",
        XY + [PADDED, FIELD2, BOXED, BOXED, PLANES, COPIES],
        flops=10_000_000_000,
    )
    second, first = call(
        tail_kernel,
        [shape(24, 8, 128), shape(24, NY, NZ)],
        [VMEM] * 15,
        common + (values, partial, hots, backs, nearsib, farsib),
        "tail",
        XY + [PADDED1, FIELD2, BOXED, BOXED, PLANES, PLANES, COPIES],
    )
    far_y = lax.ppermute(second, "dom", couples(1))
    near_y = lax.ppermute(second, "dom", couples(0))
    (fourth,) = call(
        last_kernel,
        [shape(24, 8, 128)],
        [VMEM] * 17,
        common + (first, hots, backs, nearsib, farsib, second, near_y, far_y),
        "last",
        XY + [PADDED, PADDED1, FIELD2, BOXED, BOXED, PLANES, PLANES, COPIES],
    )
    far = lax.ppermute(fourth, "band", meet("band", 4))
    other = lax.ppermute(fourth, "band", meet("band", 1))
    field = shape(24, 8, 128)
    base, one, three = call(parts_kernel, [field] * 3, [VMEM] * 3, (factors, fourth, other), "parts")
    one = lax.ppermute(one, "band", meet("band", 2))
    three = lax.ppermute(three, "band", meet("band", 6))
    farsib = lax.ppermute(far, "band", meet("band", 1))
    (filtered,) = call(store_kernel, [field], [VMEM], (fourth,), "store", flops=0, moved=0)
    (most,) = call(most_kernel, [field], [VMEM] * 5, (factors, base, one, three, far), "most")
    (rotated,) = call(total_kernel, [field], [VMEM] * 3, (factors, most, farsib), "total")
    return (filtered.reshape(orbitals.shape), rotated.reshape(orbitals.shape))


def solution(mesh):
    in_specs = (
        P("band", "dom", None, None),
        P("dom", None, None),
        P("dom", None),
        P("dom"),
        P("dom", None, None),
        P("dom", None),
        P(),
    )
    out_specs = (P("band", "dom", None, None), P("band", "dom", None, None))
    return jax.shard_map(shards, mesh=mesh, in_specs=in_specs, out_specs=out_specs, check_vma=False)
```

```python
import jax
import jax.numpy as jnp
from jax import lax
from jax.experimental import pallas as pl
from jax.experimental.pallas import tpu as pltpu
from jax.sharding import PartitionSpec as P

STENCIL = (
    -5369.0 / 1800.0,
    12.0 / 7.0,
    -15.0 / 56.0,
    10.0 / 189.0,
    -1.0 / 112.0,
    2.0 / 1925.0,
    -1.0 / 16632.0,
)
LOWER = -1.6
UPPER = 24.0
CENTER = 0.5 * (UPPER + LOWER)
HALF = 0.5 * (UPPER - LOWER)

CX, NY, NZ = 12, 16, 128
ATOMS = 32
NPROJ, BX, BY, BZ = 8, 6, 8, 8
LANES = ATOMS * BZ
SPAN = CX + BX - 1
PAIRS = NPROJ * BX
TILE_Y, TILE_POT, TILE_P, TILE_META, TILES = 0, 24, 30, 78, 82
ROW_Z, ROW_X0, ROW_Y0 = 0, 1, 2

VMEM = pl.BlockSpec(memory_space=pltpu.VMEM)
HBM = pl.BlockSpec(memory_space=pltpu.HBM)
SMEM = pl.BlockSpec(memory_space=pltpu.SMEM)


def shape(*dims, dtype=jnp.float32):
    return jax.ShapeDtypeStruct(dims, dtype)


def call(kernel, outs, ins, args, name, scratch=(), out_specs=None, flops=1_000_000, moved=2_000_000):
    return pl.pallas_call(
        kernel,
        out_shape=outs,
        in_specs=ins,
        out_specs=out_specs or [VMEM] * len(outs),
        scratch_shapes=list(scratch),
        compiler_params=pltpu.CompilerParams(vmem_limit_bytes=32 * 2**20),
        cost_estimate=pl.CostEstimate(flops=flops, bytes_accessed=moved, transcendentals=0),
        name=name,
    )(*args)


def two_terms(value, axis):
    high = value.astype(jnp.bfloat16)
    low = (value - high.astype(jnp.float32)).astype(jnp.bfloat16)
    return jnp.concatenate([high, low], axis)


def dot(left, right):
    return jnp.dot(left, right, preferred_element_type=jnp.float32)


def half(tile):
    return slice(128 * tile, 128 * tile + 128)


def spread_projectors(read, work, *tables):
    lane = lax.broadcasted_iota(jnp.int32, (8, 128), 1)
    for part in range(3):
        items = [read(part, a) for a in range(16)]
        for bit in (1, 2, 4, 8):
            upper = (lane & (8 * bit)) != 0
            for p in range(16):
                if p & bit:
                    continue
                q = p | bit
                first, second = items[p], items[q]
                items[p] = jnp.where(upper, pltpu.roll(second, 8 * bit, 1), first)
                items[q] = jnp.where(upper, second, pltpu.roll(first, 128 - 8 * bit, 1))
        for g in range(16):
            i, j = 2 * part + g // 8, g % 8
            work[i, 8 * j : 8 * j + 8, :] = items[g]
    for i in range(BX):
        for l in range(NPROJ):
            laid = work.at[i][pl.ds(l, 8, stride=8), :]
            for table in tables:
                table[l * BX + i] = laid


def pack_kernel(y_hbm, pot_hbm, proj_hbm, gamma_hbm, pos_hbm, count_ref,
                up_ref, down_ref, pot_ref, rest_ref, gamma_ref, pos_ref, half_ref, work, sems):
    core = lax.axis_index("band") % 2
    copies = [
        pltpu.make_async_copy(gamma_hbm, gamma_ref, sems.at[0]),
        pltpu.make_async_copy(pos_hbm, pos_ref, sems.at[1]),
    ]
    moves = []
    for first, target in ((16 * core, half_ref), (16 - 16 * core, rest_ref)):
        for part in range(3):
            source = proj_hbm.at[pl.ds(first, 16), pl.ds(0, 8), pl.ds(128 * part, 128)]
            moves.append((source, target.at[pl.ds(16 * part, 16)]))
    moves.append((pot_hbm, pot_ref))
    for out, first in ((up_ref, 12), (down_ref, 0)):
        moves.append((y_hbm, out.at[pl.ds(TILE_Y, 24)]))
        moves.append((pot_hbm.at[pl.ds(first + 6 * core, 6)], out.at[pl.ds(TILE_POT, 6)]))
    for n, (source, target) in enumerate(moves):
        copies.append(pltpu.make_async_copy(source, target, sems.at[2 + n]))
    for copy in copies:
        copy.start()
    copies[0].wait()
    copies[1].wait()
    live = lax.broadcasted_iota(jnp.int32, (1, ATOMS), 1) < count_ref[0]
    weight = jnp.where(live, gamma_ref[...], 0.0)
    spread = lambda v, m: jnp.dot(v, m, preferred_element_type=jnp.float32, precision=lax.Precision.HIGHEST)
    atom = lax.broadcasted_iota(jnp.int32, (ATOMS, LANES), 0)
    lane = lax.broadcasted_iota(jnp.int32, (ATOMS, LANES), 1)
    repeat = jnp.where((lane >> 3) ^ (16 * core) == atom, 1.0, 0.0)
    order = jnp.where(lane[:, half(0)] ^ (16 * core) == atom[:, half(0)], 1.0, 0.0)
    corner = pos_ref[...].astype(jnp.float32)
    weight = spread(weight, repeat)
    column = spread(corner, repeat)[2:3] + (lax.broadcasted_iota(jnp.int32, (1, LANES), 1) & 7).astype(jnp.float32)
    column = jnp.where(column >= NZ, column - NZ, column)
    corner = spread(corner, order)
    for out in (up_ref, down_ref):
        for tile in range(2):
            out[TILE_META + 2 * tile] = weight[:, half(tile)]
            out[TILE_META + 2 * tile + 1] = jnp.broadcast_to(column[:, half(tile)], (8, 128))
        out[TILE_META + 1, ROW_X0 : ROW_X0 + 1, :] = corner[0:1]
        out[TILE_META + 1, ROW_Y0 : ROW_Y0 + 1, :] = corner[1:2]
    for copy in copies[2:5]:
        copy.wait()
    tables = [out.at[pl.ds(TILE_P, PAIRS)] for out in (up_ref, down_ref)]
    spread_projectors(lambda part, a: half_ref[16 * part + a], work, *tables)
    for copy in copies[5:]:
        copy.wait()


def prepare_kernel(rest_ref, up_ref, ritz_ref, table_ref, zst_ref, sums_ref, hot_ref, back_ref, factors_ref, work):
    write_one_hot(up_ref, hot_ref, back_ref)
    band = lax.axis_index("band")
    row = lax.broadcasted_iota(jnp.int32, (8, 8), 0)
    column = lax.broadcasted_iota(jnp.int32, (8, 8), 1)
    for hop in range(4):
        for n in range(2):
            orbital, to = (band ^ (4 + n), band) if hop == 2 else (band ^ n, band ^ (2 * hop))
            picked = jnp.where((row == orbital) & (column == to), ritz_ref[...], 0.0)
            picked = jnp.sum(jnp.sum(picked, 1, keepdims=True), 0, keepdims=True)
            factors_ref[2 * hop + n] = jnp.broadcast_to(picked, (8, 128))
    spread_projectors(lambda part, a: rest_ref[16 * part + a], work, table_ref)
    apart = lax.broadcasted_iota(jnp.int32, (NZ, NZ), 0) - lax.broadcasted_iota(jnp.int32, (NZ, NZ), 1)
    full = jnp.zeros((NZ, NZ), jnp.float32)
    for reach in range(1, 7):
        near = ((apart & (NZ - 1)) == reach) | ((apart & (NZ - 1)) == NZ - reach)
        full = jnp.where(near, STENCIL[reach], full)
    high = full.astype(jnp.bfloat16)
    zst_ref[0:128, :] = high
    zst_ref[128:256, :] = high
    zst_ref[256:384, :] = (full - high.astype(jnp.float32)).astype(jnp.bfloat16)
    atom = lambda axis: lax.broadcasted_iota(jnp.int32, (LANES, LANES), axis) >> 3
    sums_ref[...] = jnp.where(atom(0) == atom(1), 1.0, 0.0).astype(jnp.bfloat16)


def fill(padded, plane, value):
    count = value.shape[0]
    padded[plane : plane + count, 8:24, :] = value
    padded[plane : plane + count, 0:8, :] = value[:, 8:16]
    padded[plane : plane + count, 24:32, :] = value[:, 0:8]


class Boxes:
    def __init__(self, sources, held, sems):
        self.sources, self.held = sources, held
        self.copies = [
            pltpu.make_async_copy(s.at[TILE_META + 1], h, sems.at[n]) for n, (s, h) in enumerate(zip(sources, held))
        ]
        for copy in self.copies:
            copy.start()

    def wait(self):
        for copy in self.copies:
            copy.wait()

    def place(self, group, atom):
        held = self.held[group]
        return held[ROW_X0, atom].astype(jnp.int32), held[ROW_Y0, atom].astype(jnp.int32)

    def weight(self, group):
        source = self.sources[group]
        return jnp.concatenate([source[TILE_META], source[TILE_META + 2]], 1)


def write_one_hot(source, hot_ref, back_ref):
    column = jnp.concatenate([source[TILE_META + 1 + 2 * t, ROW_Z : ROW_Z + 1, :] for t in range(2)], 1)
    cells = lax.broadcasted_iota(jnp.int32, (NZ, LANES), 0).astype(jnp.float32)
    hot = jnp.where(cells == column, 1.0, 0.0)
    back = hot.T.astype(jnp.bfloat16)
    hot = hot.astype(jnp.bfloat16)
    for term in range(2):
        hot_ref[NZ * term : NZ * term + NZ, :] = hot
        back_ref[LANES * term : LANES * term + LANES, :] = back


def gather_columns(group, field2, first_in, planes_in, skip, gathered, onehot):
    rows = slice(NY * first_in, NY * (first_in + planes_in))
    columns = dot(field2[rows, :], onehot[...]).reshape(planes_in, NY, LANES)
    for tile in range(2):
        part = columns[:, :, half(tile)]
        gathered[group][tile, skip : skip + planes_in, 0:16, :] = part
        gathered[group][tile, skip : skip + planes_in, 16:24, :] = part[:, 0:8]


def read_windows(group, gathered, boxes):
    lane = lax.broadcasted_iota(jnp.int32, (8, 128), 1)
    values = [[jnp.zeros((8, 128), jnp.float32)] * 2 for _ in range(BX)]
    for a in range(16):
        mine = (lane >> 3) == a
        for tile in range(2):
            x0, y0 = boxes.place(group, 16 * tile + a)
            for i in range(BX):
                values[i][tile] = jnp.where(mine, gathered[group][tile, x0 + i, pl.ds(y0, 8), :], values[i][tile])
    return values


def contributions(group, values, table, placed, boxes, sums):
    coeffs = []
    for tile in range(2):
        rows = []
        for l in range(NPROJ):
            total = values[0][tile] * table[tile][l * BX]
            for i in range(1, BX):
                total = total + values[i][tile] * table[tile][l * BX + i]
            rows.append(jnp.sum(total, 0, keepdims=True))
        coeffs.append(jnp.concatenate(rows, 0))
    both = dot(two_terms(jnp.concatenate(coeffs, 1), 0), sums)
    coeffs = (both[:8] + both[8:]) * boxes.weight(group)
    lane = lax.broadcasted_iota(jnp.int32, (8, 128), 1)
    contrib = [[None] * 2 for _ in range(BX)]
    for tile in range(2):
        rows = [jnp.broadcast_to(coeffs[l : l + 1, half(tile)], (8, 128)) for l in range(NPROJ)]
        for i in range(BX):
            total = rows[0] * table[tile][i]
            for l in range(1, NPROJ):
                total = total + rows[l] * table[tile][l * BX + i]
            contrib[i][tile] = total
    for a in range(16):
        mine = (lane >> 3) == a
        for tile in range(2):
            x0, y0 = boxes.place(group, 16 * tile + a)
            for i in range(BX):
                pltpu.store(placed[group].at[tile, x0 + i, pl.ds(y0, 8), :], contrib[i][tile], mask=mine)


def spread_group(group, first, count, placed, back):
    planes = slice(first, first + count)
    tiles = []
    for tile in range(2):
        folded = placed[group][tile, planes, 0:8, :] + placed[group][tile, planes, 16:24, :]
        tiles.append(jnp.concatenate([folded, placed[group][tile, planes, 8:16, :]], 1).reshape(count * NY, 128))
    return dot(two_terms(jnp.concatenate(tiles, 1), 1), back[...]).reshape(count, NY, NZ)


def along_z(field2, rows, zst_ref):
    return dot(field2[rows, :], zst_ref[0:256, :]) + dot(field2[rows, 0:128], zst_ref[256:384, :])


def stencil_plane(padded, plane):
    total = 3.0 * STENCIL[0] * padded[plane, 8:24, :]
    for reach in range(1, 7):
        along_x = padded[plane + reach, 8:24, :] + padded[plane - reach, 8:24, :]
        along_y = padded[plane, 8 + reach : 24 + reach, :] + padded[plane, 8 - reach : 24 - reach, :]
        total = total + STENCIL[reach] * (along_x + along_y)
    return total


def own_potential(p, pot_ref):
    return pot_ref[2 * (p - 6) : 2 * (p - 6) + 2].reshape(NY, NZ)


def edge_potential(p, low_refs, high_refs):
    mine, other = low_refs if p < 6 else high_refs
    plane = p if p < 6 else p - 18
    tile = TILE_POT + 2 * (plane % 3)
    upper = (lax.axis_index("band") % 2).astype(jnp.float32)
    share = upper if plane >= 3 else 1.0 - upper
    return (mine[tile : tile + 2] * share + other[tile : tile + 2] * (1.0 - share)).reshape(NY, NZ)


def clear(boxed):
    for ref in boxed:
        ref[...] = jnp.zeros_like(ref)


def laid(first, second):
    rows = pl.ds(TILE_P, PAIRS)
    return first.at[rows], second if second.shape[0] == PAIRS else second.at[rows]


def load_fields(fields, padded, field2):
    for n, value in enumerate(fields):
        fill(padded, 12 * n, value.reshape(CX, NY, NZ))
        field2[192 * n : 192 * n + 192, :] = two_terms(value.reshape(192, NZ), 1)


def head_kernel(up_ref, high_ref, low_ref, pot_ref, table_ref, zst_ref, sums_ref, hot_ref, back_ref,
                values_ref, partial_ref, hots_ref, backs_ref,
                low_xy, own_xy, high_xy, padded, field2, gathered, placed, local, sems):
    boxes = Boxes((low_ref, up_ref, high_ref), (low_xy, own_xy, high_xy), sems)
    load_fields([r[TILE_Y : TILE_Y + 24] for r in (low_ref, up_ref, high_ref)], padded, field2)
    clear(placed)
    gathered[2][:, 12:SPAN] = jnp.zeros((2, SPAN - 12, 24, 128), jnp.float32)
    for n, source in enumerate((low_ref, high_ref)):
        write_one_hot(source, hots_ref.at[n], backs_ref.at[n])
    gather_columns(1, field2, 12, SPAN, 0, gathered, hot_ref)
    gather_columns(0, field2, 0, SPAN, 0, gathered, hots_ref.at[0])
    gather_columns(2, field2, 24, 12, 0, gathered, hots_ref.at[1])
    local[...] = along_z(field2, slice(96, 480), zst_ref).reshape(24, NY, NZ)
    for p in range(24):
        laplace = stencil_plane(padded, p + 6) + local[p]
        pot = own_potential(p, pot_ref) if 6 <= p < 18 else 0.0
        local[p] = (-0.5 * laplace + (pot - CENTER) * padded[p + 6, 8:24, :]) * (1.0 / HALF)
    boxes.wait()
    contributions(1, read_windows(1, gathered, boxes), laid(up_ref, table_ref), placed, boxes, sums_ref[...])
    for n, group in enumerate((0, 2)):
        values = read_windows(group, gathered, boxes)
        for i in range(BX):
            for tile in range(2):
                values_ref[n, i, tile] = values[i][tile]
    partial_ref[0:6] = local[0:6]
    partial_ref[6:23] = local[6:23] + spread_group(1, 0, 17, placed, back_ref) * (1.0 / HALF)
    partial_ref[23] = local[23]


def second_step(boxes, hots, backs, padded1, field2, gathered, placed, local, nonlocal_, pot_ref, tables, zst_ref, sums):
    for group, first, planes, skip in ((0, 0, 11, 6), (1, 6, SPAN, 0)):
        gather_columns(group, field2, first, planes, skip, gathered, hots[group])
    for group in range(2):
        contributions(group, read_windows(group, gathered, boxes), tables[group], placed, boxes, sums)
    local[0:12] = along_z(field2, slice(96, 288), zst_ref).reshape(12, NY, NZ)
    for p in range(12):
        here = padded1[p + 6, 8:24, :]
        laplace = stencil_plane(padded1, p + 6) + local[p]
        pot = own_potential(p + 6, pot_ref)
        local[p] = -0.5 * laplace + (pot - CENTER) * here
    nonlocal_[0:12] = spread_group(1, 0, 12, placed, backs[1])
    nonlocal_[0:5] += spread_group(0, 12, 5, placed, backs[0])
    for p in range(12):
        yield p, (local[p] + nonlocal_[p]) * (2.0 / HALF)


def tail_kernel(up_ref, high_ref, low_ref, pot_ref, table_ref, zst_ref, sums_ref, hot_ref, back_ref,
                values_ref, partial_ref, hots_ref, backs_ref, highsib_ref, lowsib_ref,
                out_ref, kept_ref,
                low_xy, own_xy, high_xy, padded1, field2, gathered, placed, local, nonlocal_, sems):
    boxes = Boxes((low_ref, up_ref, high_ref), (low_xy, own_xy, high_xy), sems)
    clear(placed)
    gathered[0][:, 0:6] = jnp.zeros((2, 6, 24, 128), jnp.float32)
    tables = (laid(low_ref, lowsib_ref), laid(up_ref, table_ref), laid(high_ref, highsib_ref))
    hots, backs = (hots_ref.at[0], hot_ref), (backs_ref.at[0], back_ref, backs_ref.at[1])
    boxes.wait()
    sums = sums_ref[...]
    for n, group in enumerate((0, 2)):
        values = [[values_ref[n, i, tile] for tile in range(2)] for i in range(BX)]
        contributions(group, values, tables[group], placed, boxes, sums)
    nonlocal_[0:11] = spread_group(0, 6, 11, placed, backs[0])
    nonlocal_[11:18] = jnp.zeros((7, NY, NZ), jnp.float32)
    nonlocal_[18:24] = spread_group(2, 0, 6, placed, backs[2])
    for p in range(24):
        rest = nonlocal_[p]
        if not 6 <= p < 18:
            pot = edge_potential(p, (low_ref, lowsib_ref), (high_ref, highsib_ref))
            field, tile = (low_ref, TILE_Y + 2 * (p + 6)) if p < 6 else (high_ref, TILE_Y + 2 * (p - 18))
            rest = rest + pot * field[tile : tile + 2].reshape(NY, NZ)
        updated = partial_ref[p] + rest * (1.0 / HALF)
        kept_ref[p] = updated
        fill(padded1, p, updated[None])
        field2[16 * p : 16 * p + 16, :] = two_terms(updated, 1)
    for p, value in second_step(boxes, hots, backs, padded1, field2, gathered, placed, local, nonlocal_, pot_ref, tables,
                                zst_ref, sums):
        out_ref[2 * p : 2 * p + 2] = (value - up_ref[TILE_Y + 2 * p : TILE_Y + 2 * p + 2].reshape(NY, NZ)).reshape(2, 8, 128)


def last_kernel(up_ref, high_ref, low_ref, pot_ref, table_ref, zst_ref, sums_ref, hot_ref, back_ref,
                kept_ref, hots_ref, backs_ref, highsib_ref, lowsib_ref,
                mid_ref, highy_ref, lowy_ref,
                out_ref,
                low_xy, own_xy, high_xy, padded, padded1, field2, gathered, placed, local, nonlocal_, sems):
    boxes = Boxes((low_ref, up_ref, high_ref), (low_xy, own_xy, high_xy), sems)
    load_fields([r[...] for r in (lowy_ref, mid_ref, highy_ref)], padded, field2)
    clear(placed)
    gathered[2][:, 12:SPAN] = jnp.zeros((2, SPAN - 12, 24, 128), jnp.float32)
    hots, backs = (hots_ref.at[0], hot_ref, hots_ref.at[1]), (backs_ref.at[0], back_ref, backs_ref.at[1])
    sums = sums_ref[...]
    tables = (laid(low_ref, lowsib_ref), laid(up_ref, table_ref), laid(high_ref, highsib_ref))
    for group, planes in ((0, SPAN), (1, SPAN), (2, 12)):
        gather_columns(group, field2, 12 * group, planes, 0, gathered, hots[group])
    local[...] = along_z(field2, slice(96, 480), zst_ref).reshape(24, NY, NZ)
    for p in range(24):
        laplace = stencil_plane(padded, p + 6) + local[p]
        if 6 <= p < 18:
            pot = own_potential(p, pot_ref)
        else:
            pot = edge_potential(p, (low_ref, lowsib_ref), (high_ref, highsib_ref))
        applied = -0.5 * laplace + (pot - CENTER) * padded[p + 6, 8:24, :]
        local[p] = applied * (2.0 / HALF) - kept_ref[p]
    boxes.wait()
    windows = [read_windows(group, gathered, boxes) for group in range(3)]
    for group in range(3):
        contributions(group, windows[group], tables[group], placed, boxes, sums)
    nonlocal_[0:11] = spread_group(0, 6, 11, placed, backs[0])
    nonlocal_[11:24] = jnp.zeros((13, NY, NZ), jnp.float32)
    nonlocal_[6:23] += spread_group(1, 0, 17, placed, backs[1])
    nonlocal_[18:24] += spread_group(2, 0, 6, placed, backs[2])
    for p in range(24):
        updated = local[p] + nonlocal_[p] * (2.0 / HALF)
        fill(padded1, p, updated[None])
        field2[16 * p : 16 * p + 16, :] = two_terms(updated, 1)
    for p, value in second_step(boxes, hots, backs, padded1, field2, gathered, placed, local, nonlocal_, pot_ref, tables,
                                zst_ref, sums):
        out_ref[2 * p : 2 * p + 2] = (value - padded[p + 12, 8:24, :]).reshape(2, 8, 128)


XY = [pltpu.SMEM((8, 128), jnp.float32)] * 3
PADDED = pltpu.VMEM((36, 32, NZ), jnp.float32)
PADDED1 = pltpu.VMEM((24, 32, NZ), jnp.float32)
FIELD2 = pltpu.VMEM((576, 2 * NZ), jnp.bfloat16)
BOXED = [pltpu.VMEM((2, SPAN, 24, 128), jnp.float32)] * 3
PLANES = pltpu.VMEM((24, NY, NZ), jnp.float32)
WORK = pltpu.VMEM((BX, BY * NPROJ, 128), jnp.float32)
COPIES = pltpu.SemaphoreType.DMA((3,))


def parts_kernel(factors_ref, own_ref, other_ref, base_ref, one_ref, three_ref):
    own, other = own_ref[...], other_ref[...]
    for hop, target in ((0, base_ref), (1, one_ref), (3, three_ref)):
        target[...] = factors_ref[2 * hop] * own + factors_ref[2 * hop + 1] * other


def store_kernel(own_ref, out_ref):
    out_ref[...] = own_ref[...]


def most_kernel(factors_ref, base_ref, one_ref, three_ref, far_ref, out_ref):
    out_ref[...] = (base_ref[...] + factors_ref[4] * far_ref[...]) + (one_ref[...] + three_ref[...])


def total_kernel(factors_ref, most_ref, farsib_ref, out_ref):
    out_ref[...] = most_ref[...] + factors_ref[5] * farsib_ref[...]


def ring(axis, step):
    count = lax.axis_size(axis)
    return [(i, (i + step) % count) for i in range(count)]


def meet(axis, bits):
    return [(i, i ^ bits) for i in range(lax.axis_size(axis))]


def shards(orbitals, potential, atom_pos, atom_count, projectors, gammas, ritz):
    stay = lambda v: pltpu.with_memory_space_constraint(v, pltpu.HBM)
    up, down, pot, rest = call(
        pack_kernel,
        [shape(TILES, 8, 128), shape(TILES, 8, 128), shape(24, 8, 128), shape(PAIRS, 8, 128)],
        [HBM] * 5 + [SMEM],
        (
            stay(orbitals.reshape(24, 8, 128)),
            stay(potential.reshape(24, 8, 128)),
            stay(projectors),
            stay(gammas.T),
            stay(atom_pos.T),
            atom_count,
        ),
        "pack",
        [
            pltpu.VMEM((NPROJ, ATOMS), jnp.float32),
            pltpu.VMEM((3, ATOMS), jnp.int32),
            pltpu.VMEM((PAIRS, 8, 128), jnp.float32),
            WORK,
            pltpu.SemaphoreType.DMA((13,)),
        ],
    )
    low = lax.ppermute(up, "dom", ring("dom", 1))
    high = lax.ppermute(down, "dom", ring("dom", -1))
    table, zst, sums, hot, back, factors = call(
        prepare_kernel,
        [
            shape(PAIRS, 8, 128),
            shape(384, NZ, dtype=jnp.bfloat16),
            shape(LANES, LANES, dtype=jnp.bfloat16),
            shape(2 * NZ, LANES, dtype=jnp.bfloat16),
            shape(2 * LANES, NZ, dtype=jnp.bfloat16),
            shape(8, 8, 128),
        ],
        [VMEM] * 3,
        (rest, down, ritz),
        "prepare",
        [WORK],
    )
    highsib = lax.ppermute(high, "band", meet("band", 1))
    lowsib = lax.ppermute(low, "band", meet("band", 1))
    common = (down, high, low, pot, table, zst, sums, hot, back)
    values, partial, hots, backs = call(
        head_kernel,
        [
            shape(2, BX, 2, 8, 128),
            shape(24, NY, NZ),
            shape(2, 2 * NZ, LANES, dtype=jnp.bfloat16),
            shape(2, 2 * LANES, NZ, dtype=jnp.bfloat16),
        ],
        [VMEM] * 9,
        common,
        "head",
        XY + [PADDED, FIELD2, BOXED, BOXED, PLANES, COPIES],
        flops=10_000_000_000,
    )
    second, first = call(
        tail_kernel,
        [shape(24, 8, 128), shape(24, NY, NZ)],
        [VMEM] * 15,
        common + (values, partial, hots, backs, highsib, lowsib),
        "tail",
        XY + [PADDED1, FIELD2, BOXED, BOXED, PLANES, PLANES, COPIES],
    )
    low_y = lax.ppermute(second, "dom", ring("dom", 1))
    high_y = lax.ppermute(second, "dom", ring("dom", -1))
    (fourth,) = call(
        last_kernel,
        [shape(24, 8, 128)],
        [VMEM] * 17,
        common + (first, hots, backs, highsib, lowsib, second, high_y, low_y),
        "last",
        XY + [PADDED, PADDED1, FIELD2, BOXED, BOXED, PLANES, PLANES, COPIES],
    )
    far = lax.ppermute(fourth, "band", meet("band", 4))
    other = lax.ppermute(fourth, "band", meet("band", 1))
    field = shape(24, 8, 128)
    base, one, three = call(parts_kernel, [field] * 3, [VMEM] * 3, (factors, fourth, other), "parts")
    one = lax.ppermute(one, "band", meet("band", 2))
    three = lax.ppermute(three, "band", meet("band", 6))
    farsib = lax.ppermute(far, "band", meet("band", 1))
    (filtered,) = call(store_kernel, [field], [VMEM], (fourth,), "store", flops=0, moved=0)
    (most,) = call(most_kernel, [field], [VMEM] * 5, (factors, base, one, three, far), "most")
    (rotated,) = call(total_kernel, [field], [VMEM] * 3, (factors, most, farsib), "total")
    return (filtered.reshape(orbitals.shape), rotated.reshape(orbitals.shape))


def solution(mesh):
    in_specs = (
        P("band", "dom", None, None),
        P("dom", None, None),
        P("dom", None),
        P("dom"),
        P("dom", None, None),
        P("dom", None),
        P(),
    )
    out_specs = (P("band", "dom", None, None), P("band", "dom", None, None))
    return jax.shard_map(shards, mesh=mesh, in_specs=in_specs, out_specs=out_specs, check_vma=False)
```

```python
import jax
import jax.numpy as jnp
from jax import lax
from jax.experimental import pallas as pl
from jax.experimental.pallas import tpu as pltpu
from jax.sharding import PartitionSpec as P

STENCIL = (
    -5369.0 / 1800.0,
    12.0 / 7.0,
    -15.0 / 56.0,
    10.0 / 189.0,
    -1.0 / 112.0,
    2.0 / 1925.0,
    -1.0 / 16632.0,
)
LOWER = -1.6
UPPER = 24.0
CENTER = 0.5 * (UPPER + LOWER)
HALF = 0.5 * (UPPER - LOWER)

CX, NY, NZ = 12, 16, 128
ATOMS = 32
NPROJ, BX, BY, BZ = 8, 6, 8, 8
LANES = ATOMS * BZ
SPAN = CX + BX - 1
PAIRS = NPROJ * BX
TILE_Y, TILE_POT, TILE_P, TILE_META, TILES = 0, 24, 30, 78, 82
ROW_Z, ROW_X0, ROW_Y0 = 0, 1, 2

VMEM = pl.BlockSpec(memory_space=pltpu.VMEM)
HBM = pl.BlockSpec(memory_space=pltpu.HBM)
SMEM = pl.BlockSpec(memory_space=pltpu.SMEM)


def shape(*dims, dtype=jnp.float32):
    return jax.ShapeDtypeStruct(dims, dtype)


def call(kernel, outs, ins, args, name, scratch=(), out_specs=None, flops=1_000_000, moved=2_000_000):
    return pl.pallas_call(
        kernel,
        out_shape=outs,
        in_specs=ins,
        out_specs=out_specs or [VMEM] * len(outs),
        scratch_shapes=list(scratch),
        compiler_params=pltpu.CompilerParams(vmem_limit_bytes=32 * 2**20),
        cost_estimate=pl.CostEstimate(flops=flops, bytes_accessed=moved, transcendentals=0),
        name=name,
    )(*args)


def two_terms(value, axis):
    high = value.astype(jnp.bfloat16)
    low = (value - high.astype(jnp.float32)).astype(jnp.bfloat16)
    return jnp.concatenate([high, low], axis)


def dot(left, right):
    return jnp.dot(left, right, preferred_element_type=jnp.float32)


def half(tile):
    return slice(128 * tile, 128 * tile + 128)


def spread_projectors(read, work, *tables):
    lane = lax.broadcasted_iota(jnp.int32, (8, 128), 1)
    for part in range(3):
        items = [read(part, a) for a in range(16)]
        for bit in (1, 2, 4, 8):
            upper = (lane & (8 * bit)) != 0
            for p in range(16):
                if p & bit:
                    continue
                q = p | bit
                first, second = items[p], items[q]
                items[p] = jnp.where(upper, pltpu.roll(second, 8 * bit, 1), first)
                items[q] = jnp.where(upper, second, pltpu.roll(first, 128 - 8 * bit, 1))
        for g in range(16):
            i, j = 2 * part + g // 8, g % 8
            work[i, 8 * j : 8 * j + 8, :] = items[g]
    for i in range(BX):
        for l in range(NPROJ):
            laid = work.at[i][pl.ds(l, 8, stride=8), :]
            for table in tables:
                table[l * BX + i] = laid


def pack_kernel(y_hbm, pot_hbm, proj_hbm, gamma_hbm, pos_hbm, count_ref,
                up_ref, down_ref, pot_ref, rest_ref, gamma_ref, pos_ref, half_ref, work, sems):
    core = lax.axis_index("band") % 2
    copies = [
        pltpu.make_async_copy(gamma_hbm, gamma_ref, sems.at[0]),
        pltpu.make_async_copy(pos_hbm, pos_ref, sems.at[1]),
    ]
    moves = []
    for first, target in ((16 * core, half_ref), (16 - 16 * core, rest_ref)):
        for part in range(3):
            source = proj_hbm.at[pl.ds(first, 16), pl.ds(0, 8), pl.ds(128 * part, 128)]
            moves.append((source, target.at[pl.ds(16 * part, 16)]))
    moves.append((pot_hbm, pot_ref))
    for out, first in ((up_ref, 12), (down_ref, 0)):
        moves.append((y_hbm, out.at[pl.ds(TILE_Y, 24)]))
        moves.append((pot_hbm.at[pl.ds(first + 6 * core, 6)], out.at[pl.ds(TILE_POT, 6)]))
    for n, (source, target) in enumerate(moves):
        copies.append(pltpu.make_async_copy(source, target, sems.at[2 + n]))
    for copy in copies:
        copy.start()
    copies[0].wait()
    copies[1].wait()
    live = lax.broadcasted_iota(jnp.int32, (1, ATOMS), 1) < count_ref[0]
    weight = jnp.where(live, gamma_ref[...], 0.0)
    spread = lambda v, m: jnp.dot(v, m, preferred_element_type=jnp.float32, precision=lax.Precision.HIGHEST)
    atom = lax.broadcasted_iota(jnp.int32, (ATOMS, LANES), 0)
    lane = lax.broadcasted_iota(jnp.int32, (ATOMS, LANES), 1)
    repeat = jnp.where((lane >> 3) ^ (16 * core) == atom, 1.0, 0.0)
    order = jnp.where(lane[:, half(0)] ^ (16 * core) == atom[:, half(0)], 1.0, 0.0)
    corner = pos_ref[...].astype(jnp.float32)
    weight = spread(weight, repeat)
    column = spread(corner, repeat)[2:3] + (lax.broadcasted_iota(jnp.int32, (1, LANES), 1) & 7).astype(jnp.float32)
    column = jnp.where(column >= NZ, column - NZ, column)
    corner = spread(corner, order)
    for out in (up_ref, down_ref):
        for tile in range(2):
            out[TILE_META + 2 * tile] = weight[:, half(tile)]
            out[TILE_META + 2 * tile + 1] = jnp.broadcast_to(column[:, half(tile)], (8, 128))
        out[TILE_META + 1, ROW_X0 : ROW_X0 + 1, :] = corner[0:1]
        out[TILE_META + 1, ROW_Y0 : ROW_Y0 + 1, :] = corner[1:2]
    for copy in copies[2:5]:
        copy.wait()
    tables = [out.at[pl.ds(TILE_P, PAIRS)] for out in (up_ref, down_ref)]
    spread_projectors(lambda part, a: half_ref[16 * part + a], work, *tables)
    for copy in copies[5:]:
        copy.wait()


def prepare_kernel(rest_ref, up_ref, ritz_ref, table_ref, zst_ref, sums_ref, hot_ref, back_ref, factors_ref, work):
    write_one_hot(up_ref, hot_ref, back_ref)
    band = lax.axis_index("band")
    row = lax.broadcasted_iota(jnp.int32, (8, 8), 0)
    column = lax.broadcasted_iota(jnp.int32, (8, 8), 1)
    for hop in range(4):
        for n in range(2):
            orbital, to = (band ^ (4 + n), band) if hop == 2 else (band ^ n, band ^ (2 * hop))
            picked = jnp.where((row == orbital) & (column == to), ritz_ref[...], 0.0)
            picked = jnp.sum(jnp.sum(picked, 1, keepdims=True), 0, keepdims=True)
            factors_ref[2 * hop + n] = jnp.broadcast_to(picked, (8, 128))
    spread_projectors(lambda part, a: rest_ref[16 * part + a], work, table_ref)
    apart = lax.broadcasted_iota(jnp.int32, (NZ, NZ), 0) - lax.broadcasted_iota(jnp.int32, (NZ, NZ), 1)
    full = jnp.zeros((NZ, NZ), jnp.float32)
    for reach in range(1, 7):
        near = ((apart & (NZ - 1)) == reach) | ((apart & (NZ - 1)) == NZ - reach)
        full = jnp.where(near, STENCIL[reach], full)
    high = full.astype(jnp.bfloat16)
    zst_ref[0:128, :] = high
    zst_ref[128:256, :] = high
    zst_ref[256:384, :] = (full - high.astype(jnp.float32)).astype(jnp.bfloat16)
    atom = lambda axis: lax.broadcasted_iota(jnp.int32, (LANES, LANES), axis) >> 3
    sums_ref[...] = jnp.where(atom(0) == atom(1), 1.0, 0.0).astype(jnp.bfloat16)


def fill(padded, plane, value):
    count = value.shape[0]
    padded[plane : plane + count, 8:24, :] = value
    padded[plane : plane + count, 0:8, :] = value[:, 8:16]
    padded[plane : plane + count, 24:32, :] = value[:, 0:8]


class Boxes:
    def __init__(self, sources, held, sems):
        self.sources, self.held = sources, held
        self.copies = [
            pltpu.make_async_copy(s.at[TILE_META + 1], h, sems.at[n]) for n, (s, h) in enumerate(zip(sources, held))
        ]
        for copy in self.copies:
            copy.start()

    def wait(self):
        for copy in self.copies:
            copy.wait()

    def place(self, group, atom):
        held = self.held[group]
        return held[ROW_X0, atom].astype(jnp.int32), held[ROW_Y0, atom].astype(jnp.int32)

    def weight(self, group):
        source = self.sources[group]
        return jnp.concatenate([source[TILE_META], source[TILE_META + 2]], 1)


def write_one_hot(source, hot_ref, back_ref):
    column = jnp.concatenate([source[TILE_META + 1 + 2 * t, ROW_Z : ROW_Z + 1, :] for t in range(2)], 1)
    cells = lax.broadcasted_iota(jnp.int32, (NZ, LANES), 0).astype(jnp.float32)
    hot = jnp.where(cells == column, 1.0, 0.0)
    back = hot.T.astype(jnp.bfloat16)
    hot = hot.astype(jnp.bfloat16)
    for term in range(2):
        hot_ref[NZ * term : NZ * term + NZ, :] = hot
        back_ref[LANES * term : LANES * term + LANES, :] = back


def gather_columns(group, field2, first_in, planes_in, skip, gathered, onehot):
    rows = slice(NY * first_in, NY * (first_in + planes_in))
    columns = dot(field2[rows, :], onehot[...]).reshape(planes_in, NY, LANES)
    for tile in range(2):
        part = columns[:, :, half(tile)]
        gathered[group][tile, skip : skip + planes_in, 0:16, :] = part
        gathered[group][tile, skip : skip + planes_in, 16:24, :] = part[:, 0:8]


def read_windows(group, gathered, boxes):
    lane = lax.broadcasted_iota(jnp.int32, (8, 128), 1)
    values = [[jnp.zeros((8, 128), jnp.float32)] * 2 for _ in range(BX)]
    for a in range(16):
        mine = (lane >> 3) == a
        for tile in range(2):
            x0, y0 = boxes.place(group, 16 * tile + a)
            for i in range(BX):
                values[i][tile] = jnp.where(mine, gathered[group][tile, x0 + i, pl.ds(y0, 8), :], values[i][tile])
    return values


def contributions(group, values, table, placed, boxes, sums):
    coeffs = []
    for tile in range(2):
        rows = []
        for l in range(NPROJ):
            total = values[0][tile] * table[tile][l * BX]
            for i in range(1, BX):
                total = total + values[i][tile] * table[tile][l * BX + i]
            rows.append(jnp.sum(total, 0, keepdims=True))
        coeffs.append(jnp.concatenate(rows, 0))
    both = dot(two_terms(jnp.concatenate(coeffs, 1), 0), sums)
    coeffs = (both[:8] + both[8:]) * boxes.weight(group)
    lane = lax.broadcasted_iota(jnp.int32, (8, 128), 1)
    contrib = [[None] * 2 for _ in range(BX)]
    for tile in range(2):
        rows = [jnp.broadcast_to(coeffs[l : l + 1, half(tile)], (8, 128)) for l in range(NPROJ)]
        for i in range(BX):
            total = rows[0] * table[tile][i]
            for l in range(1, NPROJ):
                total = total + rows[l] * table[tile][l * BX + i]
            contrib[i][tile] = total
    for a in range(16):
        mine = (lane >> 3) == a
        for tile in range(2):
            x0, y0 = boxes.place(group, 16 * tile + a)
            for i in range(BX):
                pltpu.store(placed[group].at[tile, x0 + i, pl.ds(y0, 8), :], contrib[i][tile], mask=mine)


def spread_group(group, first, count, placed, back):
    planes = slice(first, first + count)
    tiles = []
    for tile in range(2):
        folded = placed[group][tile, planes, 0:8, :] + placed[group][tile, planes, 16:24, :]
        tiles.append(jnp.concatenate([folded, placed[group][tile, planes, 8:16, :]], 1).reshape(count * NY, 128))
    return dot(two_terms(jnp.concatenate(tiles, 1), 1), back[...]).reshape(count, NY, NZ)


def along_z(field2, rows, zst_ref):
    return dot(field2[rows, :], zst_ref[0:256, :]) + dot(field2[rows, 0:128], zst_ref[256:384, :])


def stencil_plane(padded, plane):
    total = 3.0 * STENCIL[0] * padded[plane, 8:24, :]
    for reach in range(1, 7):
        along_x = padded[plane + reach, 8:24, :] + padded[plane - reach, 8:24, :]
        along_y = padded[plane, 8 + reach : 24 + reach, :] + padded[plane, 8 - reach : 24 - reach, :]
        total = total + STENCIL[reach] * (along_x + along_y)
    return total


def own_potential(p, pot_ref):
    return pot_ref[2 * (p - 6) : 2 * (p - 6) + 2].reshape(NY, NZ)


def edge_potential(sides, edge_ref):
    upper = (lax.axis_index("band") % 2).astype(jnp.float32)
    upper = jnp.full((6, 8, 128), upper, jnp.float32)
    for n, (mine, other) in enumerate(sides):
        mine, other = mine[TILE_POT : TILE_POT + 6], other[TILE_POT : TILE_POT + 6]
        edge_ref[n, 0:6] = mine * (1.0 - upper) + other * upper
        edge_ref[n, 6:12] = mine * upper + other * (1.0 - upper)


def edge_plane(p, edge_ref):
    n, tile = (0, 2 * p) if p < 6 else (1, 2 * (p - 18))
    return edge_ref[n, tile : tile + 2].reshape(NY, NZ)


def clear(boxed):
    for ref in boxed:
        ref[...] = jnp.zeros_like(ref)


def laid(first, second):
    rows = pl.ds(TILE_P, PAIRS)
    return first.at[rows], second if second.shape[0] == PAIRS else second.at[rows]


def load_fields(fields, padded, field2):
    for n, value in enumerate(fields):
        fill(padded, 12 * n, value.reshape(CX, NY, NZ))
        field2[192 * n : 192 * n + 192, :] = two_terms(value.reshape(192, NZ), 1)


def head_kernel(up_ref, high_ref, low_ref, pot_ref, table_ref, zst_ref, sums_ref, hot_ref, back_ref,
                values_ref, partial_ref, hots_ref, backs_ref,
                low_xy, own_xy, high_xy, padded, field2, gathered, placed, local, sems):
    boxes = Boxes((low_ref, up_ref, high_ref), (low_xy, own_xy, high_xy), sems)
    load_fields([r[TILE_Y : TILE_Y + 24] for r in (low_ref, up_ref, high_ref)], padded, field2)
    clear(placed)
    gathered[2][:, 12:SPAN] = jnp.zeros((2, SPAN - 12, 24, 128), jnp.float32)
    for n, source in enumerate((low_ref, high_ref)):
        write_one_hot(source, hots_ref.at[n], backs_ref.at[n])
    gather_columns(1, field2, 12, SPAN, 0, gathered, hot_ref)
    gather_columns(0, field2, 0, SPAN, 0, gathered, hots_ref.at[0])
    gather_columns(2, field2, 24, 12, 0, gathered, hots_ref.at[1])
    local[...] = along_z(field2, slice(96, 480), zst_ref).reshape(24, NY, NZ)
    for p in range(24):
        laplace = stencil_plane(padded, p + 6) + local[p]
        pot = own_potential(p, pot_ref) if 6 <= p < 18 else 0.0
        local[p] = (-0.5 * laplace + (pot - CENTER) * padded[p + 6, 8:24, :]) * (1.0 / HALF)
    boxes.wait()
    contributions(1, read_windows(1, gathered, boxes), laid(up_ref, table_ref), placed, boxes, sums_ref[...])
    for n, group in enumerate((0, 2)):
        values = read_windows(group, gathered, boxes)
        for i in range(BX):
            for tile in range(2):
                values_ref[n, i, tile] = values[i][tile]
    partial_ref[0:6] = local[0:6]
    partial_ref[6:23] = local[6:23] + spread_group(1, 0, 17, placed, back_ref) * (1.0 / HALF)
    partial_ref[23] = local[23]


def second_step(boxes, hots, backs, padded1, field2, gathered, placed, local, nonlocal_, pot_ref, tables, zst_ref, sums):
    for group, first, planes, skip in ((0, 0, 11, 6), (1, 6, SPAN, 0)):
        gather_columns(group, field2, first, planes, skip, gathered, hots[group])
    for group in range(2):
        contributions(group, read_windows(group, gathered, boxes), tables[group], placed, boxes, sums)
    local[0:12] = along_z(field2, slice(96, 288), zst_ref).reshape(12, NY, NZ)
    for p in range(12):
        here = padded1[p + 6, 8:24, :]
        laplace = stencil_plane(padded1, p + 6) + local[p]
        pot = own_potential(p + 6, pot_ref)
        local[p] = -0.5 * laplace + (pot - CENTER) * here
    nonlocal_[0:12] = spread_group(1, 0, 12, placed, backs[1])
    nonlocal_[0:5] += spread_group(0, 12, 5, placed, backs[0])
    for p in range(12):
        yield p, (local[p] + nonlocal_[p]) * (2.0 / HALF)


def tail_kernel(up_ref, high_ref, low_ref, pot_ref, table_ref, zst_ref, sums_ref, hot_ref, back_ref,
                values_ref, partial_ref, hots_ref, backs_ref, highsib_ref, lowsib_ref,
                out_ref, kept_ref, edge_ref,
                low_xy, own_xy, high_xy, padded1, field2, gathered, placed, local, nonlocal_, sems):
    boxes = Boxes((low_ref, up_ref, high_ref), (low_xy, own_xy, high_xy), sems)
    clear(placed)
    gathered[0][:, 0:6] = jnp.zeros((2, 6, 24, 128), jnp.float32)
    tables = (laid(low_ref, lowsib_ref), laid(up_ref, table_ref), laid(high_ref, highsib_ref))
    edge_potential(((low_ref, lowsib_ref), (high_ref, highsib_ref)), edge_ref)
    hots, backs = (hots_ref.at[0], hot_ref), (backs_ref.at[0], back_ref, backs_ref.at[1])
    boxes.wait()
    sums = sums_ref[...]
    for n, group in enumerate((0, 2)):
        values = [[values_ref[n, i, tile] for tile in range(2)] for i in range(BX)]
        contributions(group, values, tables[group], placed, boxes, sums)
    nonlocal_[0:11] = spread_group(0, 6, 11, placed, backs[0])
    nonlocal_[11:18] = jnp.zeros((7, NY, NZ), jnp.float32)
    nonlocal_[18:24] = spread_group(2, 0, 6, placed, backs[2])
    for p in range(24):
        rest = nonlocal_[p]
        if not 6 <= p < 18:
            pot = edge_plane(p, edge_ref)
            field, tile = (low_ref, TILE_Y + 2 * (p + 6)) if p < 6 else (high_ref, TILE_Y + 2 * (p - 18))
            rest = rest + pot * field[tile : tile + 2].reshape(NY, NZ)
        updated = partial_ref[p] + rest * (1.0 / HALF)
        kept_ref[p] = updated
        fill(padded1, p, updated[None])
        field2[16 * p : 16 * p + 16, :] = two_terms(updated, 1)
    for p, value in second_step(boxes, hots, backs, padded1, field2, gathered, placed, local, nonlocal_, pot_ref, tables,
                                zst_ref, sums):
        out_ref[2 * p : 2 * p + 2] = (value - up_ref[TILE_Y + 2 * p : TILE_Y + 2 * p + 2].reshape(NY, NZ)).reshape(2, 8, 128)


def last_kernel(up_ref, high_ref, low_ref, pot_ref, table_ref, zst_ref, sums_ref, hot_ref, back_ref,
                kept_ref, edge_ref, hots_ref, backs_ref, highsib_ref, lowsib_ref,
                mid_ref, highy_ref, lowy_ref,
                out_ref,
                low_xy, own_xy, high_xy, padded, padded1, field2, gathered, placed, local, nonlocal_, sems):
    boxes = Boxes((low_ref, up_ref, high_ref), (low_xy, own_xy, high_xy), sems)
    load_fields([r[...] for r in (lowy_ref, mid_ref, highy_ref)], padded, field2)
    clear(placed)
    gathered[2][:, 12:SPAN] = jnp.zeros((2, SPAN - 12, 24, 128), jnp.float32)
    hots, backs = (hots_ref.at[0], hot_ref, hots_ref.at[1]), (backs_ref.at[0], back_ref, backs_ref.at[1])
    sums = sums_ref[...]
    tables = (laid(low_ref, lowsib_ref), laid(up_ref, table_ref), laid(high_ref, highsib_ref))
    for group, planes in ((0, SPAN), (1, SPAN), (2, 12)):
        gather_columns(group, field2, 12 * group, planes, 0, gathered, hots[group])
    local[...] = along_z(field2, slice(96, 480), zst_ref).reshape(24, NY, NZ)
    for p in range(24):
        laplace = stencil_plane(padded, p + 6) + local[p]
        if 6 <= p < 18:
            pot = own_potential(p, pot_ref)
        else:
            pot = edge_plane(p, edge_ref)
        applied = -0.5 * laplace + (pot - CENTER) * padded[p + 6, 8:24, :]
        local[p] = applied * (2.0 / HALF) - kept_ref[p]
    boxes.wait()
    windows = [read_windows(group, gathered, boxes) for group in range(3)]
    for group in range(3):
        contributions(group, windows[group], tables[group], placed, boxes, sums)
    nonlocal_[0:11] = spread_group(0, 6, 11, placed, backs[0])
    nonlocal_[11:24] = jnp.zeros((13, NY, NZ), jnp.float32)
    nonlocal_[6:23] += spread_group(1, 0, 17, placed, backs[1])
    nonlocal_[18:24] += spread_group(2, 0, 6, placed, backs[2])
    for p in range(24):
        updated = local[p] + nonlocal_[p] * (2.0 / HALF)
        fill(padded1, p, updated[None])
        field2[16 * p : 16 * p + 16, :] = two_terms(updated, 1)
    for p, value in second_step(boxes, hots, backs, padded1, field2, gathered, placed, local, nonlocal_, pot_ref, tables,
                                zst_ref, sums):
        out_ref[2 * p : 2 * p + 2] = (value - padded[p + 12, 8:24, :]).reshape(2, 8, 128)


XY = [pltpu.SMEM((8, 128), jnp.float32)] * 3
PADDED = pltpu.VMEM((36, 32, NZ), jnp.float32)
PADDED1 = pltpu.VMEM((24, 32, NZ), jnp.float32)
FIELD2 = pltpu.VMEM((576, 2 * NZ), jnp.bfloat16)
BOXED = [pltpu.VMEM((2, SPAN, 24, 128), jnp.float32)] * 3
PLANES = pltpu.VMEM((24, NY, NZ), jnp.float32)
WORK = pltpu.VMEM((BX, BY * NPROJ, 128), jnp.float32)
COPIES = pltpu.SemaphoreType.DMA((3,))


def parts_kernel(factors_ref, own_ref, other_ref, base_ref, one_ref, three_ref):
    own, other = own_ref[...], other_ref[...]
    for hop, target in ((0, base_ref), (1, one_ref), (3, three_ref)):
        target[...] = factors_ref[2 * hop] * own + factors_ref[2 * hop + 1] * other


def store_kernel(own_ref, out_ref):
    out_ref[...] = own_ref[...]


def most_kernel(factors_ref, base_ref, one_ref, three_ref, far_ref, out_ref):
    out_ref[...] = (base_ref[...] + factors_ref[4] * far_ref[...]) + (one_ref[...] + three_ref[...])


def total_kernel(factors_ref, most_ref, farsib_ref, out_ref):
    out_ref[...] = most_ref[...] + factors_ref[5] * farsib_ref[...]


def ring(axis, step):
    count = lax.axis_size(axis)
    return [(i, (i + step) % count) for i in range(count)]


def meet(axis, bits):
    return [(i, i ^ bits) for i in range(lax.axis_size(axis))]


def shards(orbitals, potential, atom_pos, atom_count, projectors, gammas, ritz):
    stay = lambda v: pltpu.with_memory_space_constraint(v, pltpu.HBM)
    up, down, pot, rest = call(
        pack_kernel,
        [shape(TILES, 8, 128), shape(TILES, 8, 128), shape(24, 8, 128), shape(PAIRS, 8, 128)],
        [HBM] * 5 + [SMEM],
        (
            stay(orbitals.reshape(24, 8, 128)),
            stay(potential.reshape(24, 8, 128)),
            stay(projectors),
            stay(gammas.T),
            stay(atom_pos.T),
            atom_count,
        ),
        "pack",
        [
            pltpu.VMEM((NPROJ, ATOMS), jnp.float32),
            pltpu.VMEM((3, ATOMS), jnp.int32),
            pltpu.VMEM((PAIRS, 8, 128), jnp.float32),
            WORK,
            pltpu.SemaphoreType.DMA((13,)),
        ],
    )
    low = lax.ppermute(up, "dom", ring("dom", 1))
    high = lax.ppermute(down, "dom", ring("dom", -1))
    table, zst, sums, hot, back, factors = call(
        prepare_kernel,
        [
            shape(PAIRS, 8, 128),
            shape(384, NZ, dtype=jnp.bfloat16),
            shape(LANES, LANES, dtype=jnp.bfloat16),
            shape(2 * NZ, LANES, dtype=jnp.bfloat16),
            shape(2 * LANES, NZ, dtype=jnp.bfloat16),
            shape(8, 8, 128),
        ],
        [VMEM] * 3,
        (rest, down, ritz),
        "prepare",
        [WORK],
    )
    highsib = lax.ppermute(high, "band", meet("band", 1))
    lowsib = lax.ppermute(low, "band", meet("band", 1))
    common = (down, high, low, pot, table, zst, sums, hot, back)
    values, partial, hots, backs = call(
        head_kernel,
        [
            shape(2, BX, 2, 8, 128),
            shape(24, NY, NZ),
            shape(2, 2 * NZ, LANES, dtype=jnp.bfloat16),
            shape(2, 2 * LANES, NZ, dtype=jnp.bfloat16),
        ],
        [VMEM] * 9,
        common,
        "head",
        XY + [PADDED, FIELD2, BOXED, BOXED, PLANES, COPIES],
        flops=10_000_000_000,
    )
    second, first, edge = call(
        tail_kernel,
        [shape(24, 8, 128), shape(24, NY, NZ), shape(2, 12, 8, 128)],
        [VMEM] * 15,
        common + (values, partial, hots, backs, highsib, lowsib),
        "tail",
        XY + [PADDED1, FIELD2, BOXED, BOXED, PLANES, PLANES, COPIES],
    )
    low_y = lax.ppermute(second, "dom", ring("dom", 1))
    high_y = lax.ppermute(second, "dom", ring("dom", -1))
    (fourth,) = call(
        last_kernel,
        [shape(24, 8, 128)],
        [VMEM] * 18,
        common + (first, edge, hots, backs, highsib, lowsib, second, high_y, low_y),
        "last",
        XY + [PADDED, PADDED1, FIELD2, BOXED, BOXED, PLANES, PLANES, COPIES],
    )
    far = lax.ppermute(fourth, "band", meet("band", 4))
    other = lax.ppermute(fourth, "band", meet("band", 1))
    field = shape(24, 8, 128)
    base, one, three = call(parts_kernel, [field] * 3, [VMEM] * 3, (factors, fourth, other), "parts")
    one = lax.ppermute(one, "band", meet("band", 2))
    three = lax.ppermute(three, "band", meet("band", 6))
    farsib = lax.ppermute(far, "band", meet("band", 1))
    (filtered,) = call(store_kernel, [field], [VMEM], (fourth,), "store", flops=0, moved=0)
    (most,) = call(most_kernel, [field], [VMEM] * 5, (factors, base, one, three, far), "most")
    (rotated,) = call(total_kernel, [field], [VMEM] * 3, (factors, most, farsib), "total")
    return (filtered.reshape(orbitals.shape), rotated.reshape(orbitals.shape))


def solution(mesh):
    in_specs = (
        P("band", "dom", None, None),
        P("dom", None, None),
        P("dom", None),
        P("dom"),
        P("dom", None, None),
        P("dom", None),
        P(),
    )
    out_specs = (P("band", "dom", None, None), P("band", "dom", None, None))
    return jax.shard_map(shards, mesh=mesh, in_specs=in_specs, out_specs=out_specs, check_vma=False)
```

```python
import jax
import jax.numpy as jnp
from jax import lax
from jax.experimental import pallas as pl
from jax.experimental.pallas import tpu as pltpu
from jax.sharding import PartitionSpec as P

STENCIL = (
    -5369.0 / 1800.0,
    12.0 / 7.0,
    -15.0 / 56.0,
    10.0 / 189.0,
    -1.0 / 112.0,
    2.0 / 1925.0,
    -1.0 / 16632.0,
)
LOWER = -1.6
UPPER = 24.0
CENTER = 0.5 * (UPPER + LOWER)
HALF = 0.5 * (UPPER - LOWER)

CX, NY, NZ = 12, 16, 128
ATOMS = 32
NPROJ, BX, BY, BZ = 8, 6, 8, 8
LANES = ATOMS * BZ
SPAN = CX + BX - 1
PAIRS = NPROJ * BX
TILE_Y, TILE_POT, TILE_P, TILE_META, TILES = 0, 24, 30, 78, 82
ROW_Z, ROW_X0, ROW_Y0 = 0, 1, 2

VMEM = pl.BlockSpec(memory_space=pltpu.VMEM)
HBM = pl.BlockSpec(memory_space=pltpu.HBM)
SMEM = pl.BlockSpec(memory_space=pltpu.SMEM)


def shape(*dims, dtype=jnp.float32):
    return jax.ShapeDtypeStruct(dims, dtype)


def call(kernel, outs, ins, args, name, scratch=(), out_specs=None, flops=1_000_000, moved=2_000_000):
    return pl.pallas_call(
        kernel,
        out_shape=outs,
        in_specs=ins,
        out_specs=out_specs or [VMEM] * len(outs),
        scratch_shapes=list(scratch),
        compiler_params=pltpu.CompilerParams(vmem_limit_bytes=32 * 2**20),
        cost_estimate=pl.CostEstimate(flops=flops, bytes_accessed=moved, transcendentals=0),
        name=name,
    )(*args)


def two_terms(value, axis):
    high = value.astype(jnp.bfloat16)
    low = (value - high.astype(jnp.float32)).astype(jnp.bfloat16)
    return jnp.concatenate([high, low], axis)


def dot(left, right):
    return jnp.dot(left, right, preferred_element_type=jnp.float32)


def half(tile):
    return slice(128 * tile, 128 * tile + 128)


def spread_projectors(read, work, *tables):
    lane = lax.broadcasted_iota(jnp.int32, (8, 128), 1)
    for part in range(3):
        items = [read(part, a) for a in range(16)]
        for bit in (1, 2, 4, 8):
            upper = (lane & (8 * bit)) != 0
            for p in range(16):
                if p & bit:
                    continue
                q = p | bit
                first, second = items[p], items[q]
                items[p] = jnp.where(upper, pltpu.roll(second, 8 * bit, 1), first)
                items[q] = jnp.where(upper, second, pltpu.roll(first, 128 - 8 * bit, 1))
        for g in range(16):
            i, j = 2 * part + g // 8, g % 8
            work[i, 8 * j : 8 * j + 8, :] = items[g]
    for i in range(BX):
        for l in range(NPROJ):
            laid = work.at[i][pl.ds(l, 8, stride=8), :]
            for table in tables:
                table[l * BX + i] = laid


def pack_kernel(y_hbm, pot_hbm, proj_hbm, gamma_hbm, pos_hbm, count_ref,
                up_ref, down_ref, pot_ref, rest_ref, gamma_ref, pos_ref, half_ref, work, sems):
    core = lax.axis_index("band") % 2
    copies = [
        pltpu.make_async_copy(gamma_hbm, gamma_ref, sems.at[0]),
        pltpu.make_async_copy(pos_hbm, pos_ref, sems.at[1]),
    ]
    moves = []
    for first, target in ((16 * core, half_ref), (16 - 16 * core, rest_ref)):
        for part in range(3):
            source = proj_hbm.at[pl.ds(first, 16), pl.ds(0, 8), pl.ds(128 * part, 128)]
            moves.append((source, target.at[pl.ds(16 * part, 16)]))
    moves.append((pot_hbm, pot_ref))
    for out, first in ((up_ref, 12), (down_ref, 0)):
        moves.append((y_hbm, out.at[pl.ds(TILE_Y, 24)]))
        moves.append((pot_hbm.at[pl.ds(first + 6 * core, 6)], out.at[pl.ds(TILE_POT, 6)]))
    for n, (source, target) in enumerate(moves):
        copies.append(pltpu.make_async_copy(source, target, sems.at[2 + n]))
    for copy in copies:
        copy.start()
    copies[0].wait()
    copies[1].wait()
    live = lax.broadcasted_iota(jnp.int32, (1, ATOMS), 1) < count_ref[0]
    weight = jnp.where(live, gamma_ref[...], 0.0)
    spread = lambda v, m: jnp.dot(v, m, preferred_element_type=jnp.float32, precision=lax.Precision.HIGHEST)
    atom = lax.broadcasted_iota(jnp.int32, (ATOMS, LANES), 0)
    lane = lax.broadcasted_iota(jnp.int32, (ATOMS, LANES), 1)
    repeat = jnp.where((lane >> 3) ^ (16 * core) == atom, 1.0, 0.0)
    order = jnp.where(lane[:, half(0)] ^ (16 * core) == atom[:, half(0)], 1.0, 0.0)
    corner = pos_ref[...].astype(jnp.float32)
    weight = spread(weight, repeat)
    column = spread(corner, repeat)[2:3] + (lax.broadcasted_iota(jnp.int32, (1, LANES), 1) & 7).astype(jnp.float32)
    column = jnp.where(column >= NZ, column - NZ, column)
    corner = spread(corner, order)
    for out in (up_ref, down_ref):
        for tile in range(2):
            out[TILE_META + 2 * tile] = weight[:, half(tile)]
            out[TILE_META + 2 * tile + 1] = jnp.broadcast_to(column[:, half(tile)], (8, 128))
        out[TILE_META + 1, ROW_X0 : ROW_X0 + 1, :] = corner[0:1]
        out[TILE_META + 1, ROW_Y0 : ROW_Y0 + 1, :] = corner[1:2]
    for copy in copies[2:5]:
        copy.wait()
    tables = [out.at[pl.ds(TILE_P, PAIRS)] for out in (up_ref, down_ref)]
    spread_projectors(lambda part, a: half_ref[16 * part + a], work, *tables)
    for copy in copies[5:]:
        copy.wait()


def prepare_kernel(rest_ref, up_ref, ritz_ref, table_ref, zst_ref, sums_ref, hot_ref, back_ref, factors_ref, work):
    write_one_hot(up_ref, hot_ref, back_ref)
    band = lax.axis_index("band")
    row = lax.broadcasted_iota(jnp.int32, (8, 8), 0)
    column = lax.broadcasted_iota(jnp.int32, (8, 8), 1)
    for hop in range(4):
        for n in range(2):
            orbital, to = (band ^ (4 + n), band) if hop == 2 else (band ^ n, band ^ (2 * hop))
            picked = jnp.where((row == orbital) & (column == to), ritz_ref[...], 0.0)
            picked = jnp.sum(jnp.sum(picked, 1, keepdims=True), 0, keepdims=True)
            factors_ref[2 * hop + n] = jnp.broadcast_to(picked, (8, 128))
    spread_projectors(lambda part, a: rest_ref[16 * part + a], work, table_ref)
    apart = lax.broadcasted_iota(jnp.int32, (NZ, NZ), 0) - lax.broadcasted_iota(jnp.int32, (NZ, NZ), 1)
    full = jnp.zeros((NZ, NZ), jnp.float32)
    for reach in range(1, 7):
        near = ((apart & (NZ - 1)) == reach) | ((apart & (NZ - 1)) == NZ - reach)
        full = jnp.where(near, STENCIL[reach], full)
    high = full.astype(jnp.bfloat16)
    zst_ref[0:128, :] = high
    zst_ref[128:256, :] = high
    zst_ref[256:384, :] = (full - high.astype(jnp.float32)).astype(jnp.bfloat16)
    atom = lambda axis: lax.broadcasted_iota(jnp.int32, (LANES, LANES), axis) >> 3
    sums_ref[...] = jnp.where(atom(0) == atom(1), 1.0, 0.0).astype(jnp.bfloat16)


def fill(padded, plane, value):
    count = value.shape[0]
    padded[plane : plane + count, 8:24, :] = value
    padded[plane : plane + count, 0:8, :] = value[:, 8:16]
    padded[plane : plane + count, 24:32, :] = value[:, 0:8]


class Boxes:
    def __init__(self, sources, held, sems):
        self.sources, self.held = sources, held
        self.copies = [
            pltpu.make_async_copy(s.at[TILE_META + 1], h, sems.at[n]) for n, (s, h) in enumerate(zip(sources, held))
        ]
        for copy in self.copies:
            copy.start()

    def wait(self):
        for copy in self.copies:
            copy.wait()

    def place(self, group, atom):
        held = self.held[group]
        return held[ROW_X0, atom].astype(jnp.int32), held[ROW_Y0, atom].astype(jnp.int32)

    def weight(self, group):
        source = self.sources[group]
        return jnp.concatenate([source[TILE_META], source[TILE_META + 2]], 1)


def write_one_hot(source, hot_ref, back_ref):
    column = jnp.concatenate([source[TILE_META + 1 + 2 * t, ROW_Z : ROW_Z + 1, :] for t in range(2)], 1)
    cells = lax.broadcasted_iota(jnp.int32, (NZ, LANES), 0).astype(jnp.float32)
    hot = jnp.where(cells == column, 1.0, 0.0)
    back = hot.T.astype(jnp.bfloat16)
    hot = hot.astype(jnp.bfloat16)
    for term in range(2):
        hot_ref[NZ * term : NZ * term + NZ, :] = hot
        back_ref[LANES * term : LANES * term + LANES, :] = back


def gather_columns(group, field2, first_in, planes_in, skip, gathered, onehot):
    rows = slice(NY * first_in, NY * (first_in + planes_in))
    columns = dot(field2[rows, :], onehot[...]).reshape(planes_in, NY, LANES)
    for tile in range(2):
        part = columns[:, :, half(tile)]
        gathered[group][tile, skip : skip + planes_in, 0:16, :] = part
        gathered[group][tile, skip : skip + planes_in, 16:24, :] = part[:, 0:8]


def read_windows(group, gathered, boxes):
    lane = lax.broadcasted_iota(jnp.int32, (8, 128), 1)
    values = [[jnp.zeros((8, 128), jnp.float32)] * 2 for _ in range(BX)]
    for a in range(16):
        mine = (lane >> 3) == a
        for tile in range(2):
            x0, y0 = boxes.place(group, 16 * tile + a)
            for i in range(BX):
                values[i][tile] = jnp.where(mine, gathered[group][tile, x0 + i, pl.ds(y0, 8), :], values[i][tile])
    return values


def contributions(group, values, table, placed, boxes, sums):
    scatter(group, on_boxes(group, values, table, boxes, sums), placed, boxes)


def on_boxes(group, values, table, boxes, sums):
    coeffs = []
    for tile in range(2):
        rows = []
        for l in range(NPROJ):
            total = values[0][tile] * table[tile][l * BX]
            for i in range(1, BX):
                total = total + values[i][tile] * table[tile][l * BX + i]
            rows.append(jnp.sum(total, 0, keepdims=True))
        coeffs.append(jnp.concatenate(rows, 0))
    both = dot(two_terms(jnp.concatenate(coeffs, 1), 0), sums)
    coeffs = (both[:8] + both[8:]) * boxes.weight(group)
    contrib = [[None] * 2 for _ in range(BX)]
    for tile in range(2):
        rows = [jnp.broadcast_to(coeffs[l : l + 1, half(tile)], (8, 128)) for l in range(NPROJ)]
        for i in range(BX):
            total = rows[0] * table[tile][i]
            for l in range(1, NPROJ):
                total = total + rows[l] * table[tile][l * BX + i]
            contrib[i][tile] = total
    return contrib


def scatter(group, contrib, placed, boxes):
    lane = lax.broadcasted_iota(jnp.int32, (8, 128), 1)
    for a in range(16):
        mine = (lane >> 3) == a
        for tile in range(2):
            x0, y0 = boxes.place(group, 16 * tile + a)
            for i in range(BX):
                pltpu.store(placed[group].at[tile, x0 + i, pl.ds(y0, 8), :], contrib[i][tile], mask=mine)


def spread_group(group, first, count, placed, back):
    planes = slice(first, first + count)
    tiles = []
    for tile in range(2):
        folded = placed[group][tile, planes, 0:8, :] + placed[group][tile, planes, 16:24, :]
        tiles.append(jnp.concatenate([folded, placed[group][tile, planes, 8:16, :]], 1).reshape(count * NY, 128))
    return dot(two_terms(jnp.concatenate(tiles, 1), 1), back[...]).reshape(count, NY, NZ)


def along_z(field2, rows, zst_ref):
    return dot(field2[rows, :], zst_ref[0:256, :]) + dot(field2[rows, 0:128], zst_ref[256:384, :])


def stencil_plane(padded, plane):
    total = 3.0 * STENCIL[0] * padded[plane, 8:24, :]
    for reach in range(1, 7):
        along_x = padded[plane + reach, 8:24, :] + padded[plane - reach, 8:24, :]
        along_y = padded[plane, 8 + reach : 24 + reach, :] + padded[plane, 8 - reach : 24 - reach, :]
        total = total + STENCIL[reach] * (along_x + along_y)
    return total


def own_potential(p, pot_ref):
    return pot_ref[2 * (p - 6) : 2 * (p - 6) + 2].reshape(NY, NZ)


def edge_potential(sides, edge_ref):
    upper = (lax.axis_index("band") % 2).astype(jnp.float32)
    upper = jnp.full((6, 8, 128), upper, jnp.float32)
    for n, (mine, other) in enumerate(sides):
        mine, other = mine[TILE_POT : TILE_POT + 6], other[TILE_POT : TILE_POT + 6]
        edge_ref[n, 0:6] = mine * (1.0 - upper) + other * upper
        edge_ref[n, 6:12] = mine * upper + other * (1.0 - upper)


def edge_plane(p, edge_ref):
    n, tile = (0, 2 * p) if p < 6 else (1, 2 * (p - 18))
    return edge_ref[n, tile : tile + 2].reshape(NY, NZ)


def clear(boxed):
    for ref in boxed:
        ref[...] = jnp.zeros_like(ref)


def laid(first, second):
    rows = pl.ds(TILE_P, PAIRS)
    return first.at[rows], second if second.shape[0] == PAIRS else second.at[rows]


def load_fields(fields, padded, field2):
    for n, value in enumerate(fields):
        fill(padded, 12 * n, value.reshape(CX, NY, NZ))
        field2[192 * n : 192 * n + 192, :] = two_terms(value.reshape(192, NZ), 1)


def head_kernel(up_ref, high_ref, low_ref, pot_ref, table_ref, zst_ref, sums_ref, hot_ref, back_ref,
                values_ref, partial_ref, hots_ref, backs_ref,
                low_xy, own_xy, high_xy, padded, field2, gathered, placed, local, sems):
    boxes = Boxes((low_ref, up_ref, high_ref), (low_xy, own_xy, high_xy), sems)
    load_fields([r[TILE_Y : TILE_Y + 24] for r in (low_ref, up_ref, high_ref)], padded, field2)
    clear(placed)
    gathered[2][:, 12:SPAN] = jnp.zeros((2, SPAN - 12, 24, 128), jnp.float32)
    for n, source in enumerate((low_ref, high_ref)):
        write_one_hot(source, hots_ref.at[n], backs_ref.at[n])
    gather_columns(1, field2, 12, SPAN, 0, gathered, hot_ref)
    gather_columns(0, field2, 0, SPAN, 0, gathered, hots_ref.at[0])
    gather_columns(2, field2, 24, 12, 0, gathered, hots_ref.at[1])
    local[...] = along_z(field2, slice(96, 480), zst_ref).reshape(24, NY, NZ)
    for p in range(24):
        laplace = stencil_plane(padded, p + 6) + local[p]
        pot = own_potential(p, pot_ref) if 6 <= p < 18 else 0.0
        local[p] = (-0.5 * laplace + (pot - CENTER) * padded[p + 6, 8:24, :]) * (1.0 / HALF)
    boxes.wait()
    contributions(1, read_windows(1, gathered, boxes), laid(up_ref, table_ref), placed, boxes, sums_ref[...])
    for n, group in enumerate((0, 2)):
        values = read_windows(group, gathered, boxes)
        for i in range(BX):
            for tile in range(2):
                values_ref[n, i, tile] = values[i][tile]
    partial_ref[0:6] = local[0:6]
    partial_ref[6:23] = local[6:23] + spread_group(1, 0, 17, placed, back_ref) * (1.0 / HALF)
    partial_ref[23] = local[23]


def second_step(boxes, hots, backs, padded1, field2, gathered, placed, local, nonlocal_, pot_ref, tables, zst_ref, sums):
    for group, first, planes, skip in ((0, 0, 11, 6), (1, 6, SPAN, 0)):
        gather_columns(group, field2, first, planes, skip, gathered, hots[group])
    for group in range(2):
        contributions(group, read_windows(group, gathered, boxes), tables[group], placed, boxes, sums)
    local[0:12] = along_z(field2, slice(96, 288), zst_ref).reshape(12, NY, NZ)
    for p in range(12):
        here = padded1[p + 6, 8:24, :]
        laplace = stencil_plane(padded1, p + 6) + local[p]
        pot = own_potential(p + 6, pot_ref)
        local[p] = -0.5 * laplace + (pot - CENTER) * here
    nonlocal_[0:12] = spread_group(1, 0, 12, placed, backs[1])
    nonlocal_[0:5] += spread_group(0, 12, 5, placed, backs[0])
    for p in range(12):
        yield p, (local[p] + nonlocal_[p]) * (2.0 / HALF)


def tail_kernel(up_ref, high_ref, low_ref, pot_ref, table_ref, zst_ref, sums_ref, hot_ref, back_ref,
                values_ref, partial_ref, hots_ref, backs_ref, highsib_ref, lowsib_ref,
                out_ref, kept_ref, edge_ref,
                low_xy, own_xy, high_xy, padded1, field2, gathered, placed, local, nonlocal_, sems):
    boxes = Boxes((low_ref, up_ref, high_ref), (low_xy, own_xy, high_xy), sems)
    clear(placed)
    gathered[0][:, 0:6] = jnp.zeros((2, 6, 24, 128), jnp.float32)
    tables = (laid(low_ref, lowsib_ref), laid(up_ref, table_ref), laid(high_ref, highsib_ref))
    edge_potential(((low_ref, lowsib_ref), (high_ref, highsib_ref)), edge_ref)
    hots, backs = (hots_ref.at[0], hot_ref), (backs_ref.at[0], back_ref, backs_ref.at[1])
    sums = sums_ref[...]
    contribs = []
    for n, group in enumerate((0, 2)):
        values = [[values_ref[n, i, tile] for tile in range(2)] for i in range(BX)]
        contribs.append(on_boxes(group, values, tables[group], boxes, sums))
    boxes.wait()
    for group, contrib in zip((0, 2), contribs):
        scatter(group, contrib, placed, boxes)
    nonlocal_[0:11] = spread_group(0, 6, 11, placed, backs[0])
    nonlocal_[11:18] = jnp.zeros((7, NY, NZ), jnp.float32)
    nonlocal_[18:24] = spread_group(2, 0, 6, placed, backs[2])
    for p in range(24):
        rest = nonlocal_[p]
        if not 6 <= p < 18:
            pot = edge_plane(p, edge_ref)
            field, tile = (low_ref, TILE_Y + 2 * (p + 6)) if p < 6 else (high_ref, TILE_Y + 2 * (p - 18))
            rest = rest + pot * field[tile : tile + 2].reshape(NY, NZ)
        updated = partial_ref[p] + rest * (1.0 / HALF)
        kept_ref[p] = updated
        fill(padded1, p, updated[None])
        field2[16 * p : 16 * p + 16, :] = two_terms(updated, 1)
    for p, value in second_step(boxes, hots, backs, padded1, field2, gathered, placed, local, nonlocal_, pot_ref, tables,
                                zst_ref, sums):
        out_ref[2 * p : 2 * p + 2] = (value - up_ref[TILE_Y + 2 * p : TILE_Y + 2 * p + 2].reshape(NY, NZ)).reshape(2, 8, 128)


def last_kernel(up_ref, high_ref, low_ref, pot_ref, table_ref, zst_ref, sums_ref, hot_ref, back_ref,
                kept_ref, edge_ref, hots_ref, backs_ref, highsib_ref, lowsib_ref,
                mid_ref, highy_ref, lowy_ref,
                out_ref,
                low_xy, own_xy, high_xy, padded, padded1, field2, gathered, placed, local, nonlocal_, sems):
    boxes = Boxes((low_ref, up_ref, high_ref), (low_xy, own_xy, high_xy), sems)
    load_fields([r[...] for r in (lowy_ref, mid_ref, highy_ref)], padded, field2)
    clear(placed)
    gathered[2][:, 12:SPAN] = jnp.zeros((2, SPAN - 12, 24, 128), jnp.float32)
    hots, backs = (hots_ref.at[0], hot_ref, hots_ref.at[1]), (backs_ref.at[0], back_ref, backs_ref.at[1])
    sums = sums_ref[...]
    tables = (laid(low_ref, lowsib_ref), laid(up_ref, table_ref), laid(high_ref, highsib_ref))
    for group, planes in ((0, SPAN), (1, SPAN), (2, 12)):
        gather_columns(group, field2, 12 * group, planes, 0, gathered, hots[group])
    local[...] = along_z(field2, slice(96, 480), zst_ref).reshape(24, NY, NZ)
    for p in range(24):
        laplace = stencil_plane(padded, p + 6) + local[p]
        if 6 <= p < 18:
            pot = own_potential(p, pot_ref)
        else:
            pot = edge_plane(p, edge_ref)
        applied = -0.5 * laplace + (pot - CENTER) * padded[p + 6, 8:24, :]
        local[p] = applied * (2.0 / HALF) - kept_ref[p]
    boxes.wait()
    windows = [read_windows(group, gathered, boxes) for group in range(3)]
    for group in range(3):
        contributions(group, windows[group], tables[group], placed, boxes, sums)
    nonlocal_[0:11] = spread_group(0, 6, 11, placed, backs[0])
    nonlocal_[11:24] = jnp.zeros((13, NY, NZ), jnp.float32)
    nonlocal_[6:23] += spread_group(1, 0, 17, placed, backs[1])
    nonlocal_[18:24] += spread_group(2, 0, 6, placed, backs[2])
    for p in range(24):
        updated = local[p] + nonlocal_[p] * (2.0 / HALF)
        fill(padded1, p, updated[None])
        field2[16 * p : 16 * p + 16, :] = two_terms(updated, 1)
    for p, value in second_step(boxes, hots, backs, padded1, field2, gathered, placed, local, nonlocal_, pot_ref, tables,
                                zst_ref, sums):
        out_ref[2 * p : 2 * p + 2] = (value - padded[p + 12, 8:24, :]).reshape(2, 8, 128)


XY = [pltpu.SMEM((8, 128), jnp.float32)] * 3
PADDED = pltpu.VMEM((36, 32, NZ), jnp.float32)
PADDED1 = pltpu.VMEM((24, 32, NZ), jnp.float32)
FIELD2 = pltpu.VMEM((576, 2 * NZ), jnp.bfloat16)
BOXED = [pltpu.VMEM((2, SPAN, 24, 128), jnp.float32)] * 3
PLANES = pltpu.VMEM((24, NY, NZ), jnp.float32)
WORK = pltpu.VMEM((BX, BY * NPROJ, 128), jnp.float32)
COPIES = pltpu.SemaphoreType.DMA((3,))


def parts_kernel(factors_ref, own_ref, other_ref, base_ref, one_ref, three_ref):
    own, other = own_ref[...], other_ref[...]
    for hop, target in ((0, base_ref), (1, one_ref), (3, three_ref)):
        target[...] = factors_ref[2 * hop] * own + factors_ref[2 * hop + 1] * other


def store_kernel(own_ref, out_ref):
    out_ref[...] = own_ref[...]


def most_kernel(factors_ref, base_ref, one_ref, three_ref, far_ref, out_ref):
    out_ref[...] = (base_ref[...] + factors_ref[4] * far_ref[...]) + (one_ref[...] + three_ref[...])


def total_kernel(factors_ref, most_ref, farsib_ref, out_ref):
    out_ref[...] = most_ref[...] + factors_ref[5] * farsib_ref[...]


def ring(axis, step):
    count = lax.axis_size(axis)
    return [(i, (i + step) % count) for i in range(count)]


def meet(axis, bits):
    return [(i, i ^ bits) for i in range(lax.axis_size(axis))]


def shards(orbitals, potential, atom_pos, atom_count, projectors, gammas, ritz):
    stay = lambda v: pltpu.with_memory_space_constraint(v, pltpu.HBM)
    up, down, pot, rest = call(
        pack_kernel,
        [shape(TILES, 8, 128), shape(TILES, 8, 128), shape(24, 8, 128), shape(PAIRS, 8, 128)],
        [HBM] * 5 + [SMEM],
        (
            stay(orbitals.reshape(24, 8, 128)),
            stay(potential.reshape(24, 8, 128)),
            stay(projectors),
            stay(gammas.T),
            stay(atom_pos.T),
            atom_count,
        ),
        "pack",
        [
            pltpu.VMEM((NPROJ, ATOMS), jnp.float32),
            pltpu.VMEM((3, ATOMS), jnp.int32),
            pltpu.VMEM((PAIRS, 8, 128), jnp.float32),
            WORK,
            pltpu.SemaphoreType.DMA((13,)),
        ],
    )
    low = lax.ppermute(up, "dom", ring("dom", 1))
    high = lax.ppermute(down, "dom", ring("dom", -1))
    table, zst, sums, hot, back, factors = call(
        prepare_kernel,
        [
            shape(PAIRS, 8, 128),
            shape(384, NZ, dtype=jnp.bfloat16),
            shape(LANES, LANES, dtype=jnp.bfloat16),
            shape(2 * NZ, LANES, dtype=jnp.bfloat16),
            shape(2 * LANES, NZ, dtype=jnp.bfloat16),
            shape(8, 8, 128),
        ],
        [VMEM] * 3,
        (rest, down, ritz),
        "prepare",
        [WORK],
    )
    highsib = lax.ppermute(high, "band", meet("band", 1))
    lowsib = lax.ppermute(low, "band", meet("band", 1))
    common = (down, high, low, pot, table, zst, sums, hot, back)
    values, partial, hots, backs = call(
        head_kernel,
        [
            shape(2, BX, 2, 8, 128),
            shape(24, NY, NZ),
            shape(2, 2 * NZ, LANES, dtype=jnp.bfloat16),
            shape(2, 2 * LANES, NZ, dtype=jnp.bfloat16),
        ],
        [VMEM] * 9,
        common,
        "head",
        XY + [PADDED, FIELD2, BOXED, BOXED, PLANES, COPIES],
        flops=10_000_000_000,
    )
    second, first, edge = call(
        tail_kernel,
        [shape(24, 8, 128), shape(24, NY, NZ), shape(2, 12, 8, 128)],
        [VMEM] * 15,
        common + (values, partial, hots, backs, highsib, lowsib),
        "tail",
        XY + [PADDED1, FIELD2, BOXED, BOXED, PLANES, PLANES, COPIES],
    )
    low_y = lax.ppermute(second, "dom", ring("dom", 1))
    high_y = lax.ppermute(second, "dom", ring("dom", -1))
    (fourth,) = call(
        last_kernel,
        [shape(24, 8, 128)],
        [VMEM] * 18,
        common + (first, edge, hots, backs, highsib, lowsib, second, high_y, low_y),
        "last",
        XY + [PADDED, PADDED1, FIELD2, BOXED, BOXED, PLANES, PLANES, COPIES],
    )
    far = lax.ppermute(fourth, "band", meet("band", 4))
    other = lax.ppermute(fourth, "band", meet("band", 1))
    field = shape(24, 8, 128)
    base, one, three = call(parts_kernel, [field] * 3, [VMEM] * 3, (factors, fourth, other), "parts")
    one = lax.ppermute(one, "band", meet("band", 2))
    three = lax.ppermute(three, "band", meet("band", 6))
    farsib = lax.ppermute(far, "band", meet("band", 1))
    (filtered,) = call(store_kernel, [field], [VMEM], (fourth,), "store", flops=0, moved=0)
    (most,) = call(most_kernel, [field], [VMEM] * 5, (factors, base, one, three, far), "most")
    (rotated,) = call(total_kernel, [field], [VMEM] * 3, (factors, most, farsib), "total")
    return (filtered.reshape(orbitals.shape), rotated.reshape(orbitals.shape))


def solution(mesh):
    in_specs = (
        P("band", "dom", None, None),
        P("dom", None, None),
        P("dom", None),
        P("dom"),
        P("dom", None, None),
        P("dom", None),
        P(),
    )
    out_specs = (P("band", "dom", None, None), P("band", "dom", None, None))
    return jax.shard_map(shards, mesh=mesh, in_specs=in_specs, out_specs=out_specs, check_vma=False)
```

```python
import jax
import jax.numpy as jnp
from jax import lax
from jax.experimental import pallas as pl
from jax.experimental.pallas import tpu as pltpu
from jax.sharding import PartitionSpec as P

STENCIL = (
    -5369.0 / 1800.0,
    12.0 / 7.0,
    -15.0 / 56.0,
    10.0 / 189.0,
    -1.0 / 112.0,
    2.0 / 1925.0,
    -1.0 / 16632.0,
)
LOWER = -1.6
UPPER = 24.0
CENTER = 0.5 * (UPPER + LOWER)
HALF = 0.5 * (UPPER - LOWER)

CX, NY, NZ = 12, 16, 128
ATOMS = 32
NPROJ, BX, BY, BZ = 8, 6, 8, 8
LANES = ATOMS * BZ
SPAN = CX + BX - 1
PAIRS = NPROJ * BX
TILE_Y, TILE_POT, TILE_P, TILE_META, TILES = 0, 24, 30, 78, 82
ROW_Z, ROW_X0, ROW_Y0 = 0, 1, 2

VMEM = pl.BlockSpec(memory_space=pltpu.VMEM)
HBM = pl.BlockSpec(memory_space=pltpu.HBM)
SMEM = pl.BlockSpec(memory_space=pltpu.SMEM)


def shape(*dims, dtype=jnp.float32):
    return jax.ShapeDtypeStruct(dims, dtype)


def call(kernel, outs, ins, args, name, scratch=(), out_specs=None, flops=1_000_000, moved=2_000_000):
    return pl.pallas_call(
        kernel,
        out_shape=outs,
        in_specs=ins,
        out_specs=out_specs or [VMEM] * len(outs),
        scratch_shapes=list(scratch),
        compiler_params=pltpu.CompilerParams(vmem_limit_bytes=32 * 2**20),
        cost_estimate=pl.CostEstimate(flops=flops, bytes_accessed=moved, transcendentals=0),
        name=name,
    )(*args)


def two_terms(value, axis):
    high = value.astype(jnp.bfloat16)
    low = (value - high.astype(jnp.float32)).astype(jnp.bfloat16)
    return jnp.concatenate([high, low], axis)


def dot(left, right):
    return jnp.dot(left, right, preferred_element_type=jnp.float32)


def half(tile):
    return slice(128 * tile, 128 * tile + 128)


def spread_projectors(read, work, *tables):
    lane = lax.broadcasted_iota(jnp.int32, (8, 128), 1)
    for part in range(3):
        items = [read(part, a) for a in range(16)]
        for bit in (1, 2, 4, 8):
            upper = (lane & (8 * bit)) != 0
            for p in range(16):
                if p & bit:
                    continue
                q = p | bit
                first, second = items[p], items[q]
                items[p] = jnp.where(upper, pltpu.roll(second, 8 * bit, 1), first)
                items[q] = jnp.where(upper, second, pltpu.roll(first, 128 - 8 * bit, 1))
        for g in range(16):
            i, j = 2 * part + g // 8, g % 8
            work[i, 8 * j : 8 * j + 8, :] = items[g]
    for i in range(BX):
        for l in range(NPROJ):
            laid = work.at[i][pl.ds(l, 8, stride=8), :]
            for table in tables:
                table[l * BX + i] = laid


def pack_kernel(y_hbm, pot_hbm, proj_hbm, gamma_hbm, pos_hbm, count_ref,
                up_ref, down_ref, pot_ref, rest_ref, gamma_ref, pos_ref, half_ref, work, sems):
    core = lax.axis_index("band") % 2
    copies = [
        pltpu.make_async_copy(gamma_hbm, gamma_ref, sems.at[0]),
        pltpu.make_async_copy(pos_hbm, pos_ref, sems.at[1]),
    ]
    moves = []
    for first, target in ((16 * core, half_ref), (16 - 16 * core, rest_ref)):
        for part in range(3):
            source = proj_hbm.at[pl.ds(first, 16), pl.ds(0, 8), pl.ds(128 * part, 128)]
            moves.append((source, target.at[pl.ds(16 * part, 16)]))
    moves.append((pot_hbm, pot_ref))
    for out, first in ((up_ref, 12), (down_ref, 0)):
        moves.append((y_hbm, out.at[pl.ds(TILE_Y, 24)]))
        moves.append((pot_hbm.at[pl.ds(first + 6 * core, 6)], out.at[pl.ds(TILE_POT, 6)]))
    for n, (source, target) in enumerate(moves):
        copies.append(pltpu.make_async_copy(source, target, sems.at[2 + n]))
    for copy in copies:
        copy.start()
    copies[0].wait()
    copies[1].wait()
    live = lax.broadcasted_iota(jnp.int32, (1, ATOMS), 1) < count_ref[0]
    weight = jnp.where(live, gamma_ref[...], 0.0)
    spread = lambda v, m: jnp.dot(v, m, preferred_element_type=jnp.float32, precision=lax.Precision.HIGHEST)
    atom = lax.broadcasted_iota(jnp.int32, (ATOMS, LANES), 0)
    lane = lax.broadcasted_iota(jnp.int32, (ATOMS, LANES), 1)
    repeat = jnp.where((lane >> 3) ^ (16 * core) == atom, 1.0, 0.0)
    order = jnp.where(lane[:, half(0)] ^ (16 * core) == atom[:, half(0)], 1.0, 0.0)
    corner = pos_ref[...].astype(jnp.float32)
    weight = spread(weight, repeat)
    column = spread(corner, repeat)[2:3] + (lax.broadcasted_iota(jnp.int32, (1, LANES), 1) & 7).astype(jnp.float32)
    column = jnp.where(column >= NZ, column - NZ, column)
    corner = spread(corner, order)
    for out in (up_ref, down_ref):
        for tile in range(2):
            out[TILE_META + 2 * tile] = weight[:, half(tile)]
            out[TILE_META + 2 * tile + 1] = jnp.broadcast_to(column[:, half(tile)], (8, 128))
        out[TILE_META + 1, ROW_X0 : ROW_X0 + 1, :] = corner[0:1]
        out[TILE_META + 1, ROW_Y0 : ROW_Y0 + 1, :] = corner[1:2]
    for copy in copies[2:5]:
        copy.wait()
    tables = [out.at[pl.ds(TILE_P, PAIRS)] for out in (up_ref, down_ref)]
    spread_projectors(lambda part, a: half_ref[16 * part + a], work, *tables)
    for copy in copies[5:]:
        copy.wait()


def prepare_kernel(rest_ref, up_ref, ritz_ref, table_ref, zst_ref, sums_ref, hot_ref, back_ref, factors_ref, work):
    write_one_hot(up_ref, hot_ref, back_ref)
    band = lax.axis_index("band")
    row = lax.broadcasted_iota(jnp.int32, (8, 8), 0)
    column = lax.broadcasted_iota(jnp.int32, (8, 8), 1)
    for hop in range(4):
        for n in range(2):
            orbital, to = (band ^ (4 + n), band) if hop == 2 else (band ^ n, band ^ (2 * hop))
            picked = jnp.where((row == orbital) & (column == to), ritz_ref[...], 0.0)
            picked = jnp.sum(jnp.sum(picked, 1, keepdims=True), 0, keepdims=True)
            factors_ref[2 * hop + n] = jnp.broadcast_to(picked, (8, 128))
    spread_projectors(lambda part, a: rest_ref[16 * part + a], work, table_ref)
    apart = lax.broadcasted_iota(jnp.int32, (NZ, NZ), 0) - lax.broadcasted_iota(jnp.int32, (NZ, NZ), 1)
    full = jnp.zeros((NZ, NZ), jnp.float32)
    for reach in range(1, 7):
        near = ((apart & (NZ - 1)) == reach) | ((apart & (NZ - 1)) == NZ - reach)
        full = jnp.where(near, STENCIL[reach], full)
    high = full.astype(jnp.bfloat16)
    zst_ref[0:128, :] = high
    zst_ref[128:256, :] = high
    zst_ref[256:384, :] = (full - high.astype(jnp.float32)).astype(jnp.bfloat16)
    atom = lambda axis: lax.broadcasted_iota(jnp.int32, (LANES, LANES), axis) >> 3
    sums_ref[...] = jnp.where(atom(0) == atom(1), 1.0, 0.0).astype(jnp.bfloat16)


def fill(padded, plane, value):
    count = value.shape[0]
    padded[plane : plane + count, 8:24, :] = value
    padded[plane : plane + count, 0:8, :] = value[:, 8:16]
    padded[plane : plane + count, 24:32, :] = value[:, 0:8]


class Boxes:
    def __init__(self, sources, held, sems):
        self.sources, self.held = sources, held
        self.copies = [
            pltpu.make_async_copy(s.at[TILE_META + 1], h, sems.at[n]) for n, (s, h) in enumerate(zip(sources, held))
        ]
        for copy in self.copies:
            copy.start()

    def wait(self):
        for copy in self.copies:
            copy.wait()

    def place(self, group, atom):
        held = self.held[group]
        return held[ROW_X0, atom].astype(jnp.int32), held[ROW_Y0, atom].astype(jnp.int32)

    def weight(self, group):
        source = self.sources[group]
        return jnp.concatenate([source[TILE_META], source[TILE_META + 2]], 1)


def write_one_hot(source, hot_ref, back_ref):
    column = jnp.concatenate([source[TILE_META + 1 + 2 * t, ROW_Z : ROW_Z + 1, :] for t in range(2)], 1)
    cells = lax.broadcasted_iota(jnp.int32, (NZ, LANES), 0).astype(jnp.float32)
    hot = jnp.where(cells == column, 1.0, 0.0)
    back = hot.T.astype(jnp.bfloat16)
    hot = hot.astype(jnp.bfloat16)
    for term in range(2):
        hot_ref[NZ * term : NZ * term + NZ, :] = hot
        back_ref[LANES * term : LANES * term + LANES, :] = back


def gather_columns(group, field2, first_in, planes_in, skip, gathered, onehot):
    rows = slice(NY * first_in, NY * (first_in + planes_in))
    columns = dot(field2[rows, :], onehot[...]).reshape(planes_in, NY, LANES)
    for tile in range(2):
        part = columns[:, :, half(tile)]
        gathered[group][tile, skip : skip + planes_in, 0:16, :] = part
        gathered[group][tile, skip : skip + planes_in, 16:24, :] = part[:, 0:8]


def read_windows(group, gathered, boxes):
    lane = lax.broadcasted_iota(jnp.int32, (8, 128), 1)
    values = [[jnp.zeros((8, 128), jnp.float32)] * 2 for _ in range(BX)]
    for a in range(16):
        mine = (lane >> 3) == a
        for tile in range(2):
            x0, y0 = boxes.place(group, 16 * tile + a)
            for i in range(BX):
                values[i][tile] = jnp.where(mine, gathered[group][tile, x0 + i, pl.ds(y0, 8), :], values[i][tile])
    return values


def contributions(group, values, table, placed, boxes, sums):
    scatter(group, on_boxes(group, values, table, boxes, sums), placed, boxes)


def on_boxes(group, values, table, boxes, sums):
    coeffs = []
    for tile in range(2):
        rows = []
        for l in range(NPROJ):
            total = values[0][tile] * table[tile][l * BX]
            for i in range(1, BX):
                total = total + values[i][tile] * table[tile][l * BX + i]
            rows.append(jnp.sum(total, 0, keepdims=True))
        coeffs.append(jnp.concatenate(rows, 0))
    both = dot(two_terms(jnp.concatenate(coeffs, 1), 0), sums)
    coeffs = (both[:8] + both[8:]) * boxes.weight(group)
    contrib = [[None] * 2 for _ in range(BX)]
    for tile in range(2):
        rows = [jnp.broadcast_to(coeffs[l : l + 1, half(tile)], (8, 128)) for l in range(NPROJ)]
        for i in range(BX):
            total = rows[0] * table[tile][i]
            for l in range(1, NPROJ):
                total = total + rows[l] * table[tile][l * BX + i]
            contrib[i][tile] = total
    return contrib


def scatter(group, contrib, placed, boxes):
    lane = lax.broadcasted_iota(jnp.int32, (8, 128), 1)
    for a in range(16):
        mine = (lane >> 3) == a
        for tile in range(2):
            x0, y0 = boxes.place(group, 16 * tile + a)
            for i in range(BX):
                pltpu.store(placed[group].at[tile, x0 + i, pl.ds(y0, 8), :], contrib[i][tile], mask=mine)


def spread_group(group, first, count, placed, back):
    planes = slice(first, first + count)
    tiles = []
    for tile in range(2):
        folded = placed[group][tile, planes, 0:8, :] + placed[group][tile, planes, 16:24, :]
        tiles.append(jnp.concatenate([folded, placed[group][tile, planes, 8:16, :]], 1).reshape(count * NY, 128))
    return dot(two_terms(jnp.concatenate(tiles, 1), 1), back[...]).reshape(count, NY, NZ)


def along_z(field2, rows, zst_ref):
    return dot(field2[rows, :], zst_ref[0:256, :]) + dot(field2[rows, 0:128], zst_ref[256:384, :])


def stencil_plane(padded, plane):
    total = 3.0 * STENCIL[0] * padded[plane, 8:24, :]
    for reach in range(1, 7):
        along_x = padded[plane + reach, 8:24, :] + padded[plane - reach, 8:24, :]
        along_y = padded[plane, 8 + reach : 24 + reach, :] + padded[plane, 8 - reach : 24 - reach, :]
        total = total + STENCIL[reach] * (along_x + along_y)
    return total


def own_potential(p, pot_ref):
    return pot_ref[2 * (p - 6) : 2 * (p - 6) + 2].reshape(NY, NZ)


def edge_potential(sides, edge_ref):
    upper = (lax.axis_index("band") % 2).astype(jnp.float32)
    upper = jnp.full((6, 8, 128), upper, jnp.float32)
    for n, (mine, other) in enumerate(sides):
        mine, other = mine[TILE_POT : TILE_POT + 6], other[TILE_POT : TILE_POT + 6]
        edge_ref[n, 0:6] = mine * (1.0 - upper) + other * upper
        edge_ref[n, 6:12] = mine * upper + other * (1.0 - upper)


def edge_plane(p, edge_ref):
    n, tile = (0, 2 * p) if p < 6 else (1, 2 * (p - 18))
    return edge_ref[n, tile : tile + 2].reshape(NY, NZ)


def clear(boxed):
    for ref in boxed:
        ref[...] = jnp.zeros_like(ref)


def laid(first, second):
    rows = pl.ds(TILE_P, PAIRS)
    return first.at[rows], second if second.shape[0] == PAIRS else second.at[rows]


def load_fields(fields, padded, field2):
    for n, value in enumerate(fields):
        fill(padded, 12 * n, value.reshape(CX, NY, NZ))
        field2[192 * n : 192 * n + 192, :] = two_terms(value.reshape(192, NZ), 1)


def head_kernel(up_ref, high_ref, low_ref, pot_ref, table_ref, zst_ref, sums_ref, hot_ref, back_ref,
                values_ref, partial_ref, hots_ref, backs_ref,
                low_xy, own_xy, high_xy, padded, field2, gathered, placed, local, sems):
    boxes = Boxes((low_ref, up_ref, high_ref), (low_xy, own_xy, high_xy), sems)
    load_fields([r[TILE_Y : TILE_Y + 24] for r in (low_ref, up_ref, high_ref)], padded, field2)
    clear(placed)
    gathered[2][:, 12:SPAN] = jnp.zeros((2, SPAN - 12, 24, 128), jnp.float32)
    for n, source in enumerate((low_ref, high_ref)):
        write_one_hot(source, hots_ref.at[n], backs_ref.at[n])
    gather_columns(1, field2, 12, SPAN, 0, gathered, hot_ref)
    gather_columns(0, field2, 0, SPAN, 0, gathered, hots_ref.at[0])
    gather_columns(2, field2, 24, 12, 0, gathered, hots_ref.at[1])
    local[...] = along_z(field2, slice(96, 480), zst_ref).reshape(24, NY, NZ)
    for p in range(24):
        laplace = stencil_plane(padded, p + 6) + local[p]
        pot = own_potential(p, pot_ref) if 6 <= p < 18 else 0.0
        local[p] = (-0.5 * laplace + (pot - CENTER) * padded[p + 6, 8:24, :]) * (1.0 / HALF)
    boxes.wait()
    contributions(1, read_windows(1, gathered, boxes), laid(up_ref, table_ref), placed, boxes, sums_ref[...])
    for n, group in enumerate((0, 2)):
        values = read_windows(group, gathered, boxes)
        for i in range(BX):
            for tile in range(2):
                values_ref[n, i, tile] = values[i][tile]
    partial_ref[0:6] = local[0:6]
    partial_ref[6:23] = local[6:23] + spread_group(1, 0, 17, placed, back_ref) * (1.0 / HALF)
    partial_ref[23] = local[23]


def second_step(boxes, hots, backs, padded1, field2, gathered, placed, local, nonlocal_, pot_ref, tables, zst_ref, sums):
    for group, first, planes, skip in ((0, 0, 11, 6), (1, 6, SPAN, 0)):
        gather_columns(group, field2, first, planes, skip, gathered, hots[group])
    windows = [read_windows(group, gathered, boxes) for group in range(2)]
    contribs = [on_boxes(group, windows[group], tables[group], boxes, sums) for group in range(2)]
    for group in range(2):
        scatter(group, contribs[group], placed, boxes)
    local[0:12] = along_z(field2, slice(96, 288), zst_ref).reshape(12, NY, NZ)
    for p in range(12):
        here = padded1[p + 6, 8:24, :]
        laplace = stencil_plane(padded1, p + 6) + local[p]
        pot = own_potential(p + 6, pot_ref)
        local[p] = -0.5 * laplace + (pot - CENTER) * here
    nonlocal_[0:12] = spread_group(1, 0, 12, placed, backs[1])
    nonlocal_[0:5] += spread_group(0, 12, 5, placed, backs[0])
    for p in range(12):
        yield p, (local[p] + nonlocal_[p]) * (2.0 / HALF)


def tail_kernel(up_ref, high_ref, low_ref, pot_ref, table_ref, zst_ref, sums_ref, hot_ref, back_ref,
                values_ref, partial_ref, hots_ref, backs_ref, highsib_ref, lowsib_ref,
                out_ref, kept_ref, edge_ref,
                low_xy, own_xy, high_xy, padded1, field2, gathered, placed, local, nonlocal_, sems):
    boxes = Boxes((low_ref, up_ref, high_ref), (low_xy, own_xy, high_xy), sems)
    clear(placed)
    gathered[0][:, 0:6] = jnp.zeros((2, 6, 24, 128), jnp.float32)
    tables = (laid(low_ref, lowsib_ref), laid(up_ref, table_ref), laid(high_ref, highsib_ref))
    edge_potential(((low_ref, lowsib_ref), (high_ref, highsib_ref)), edge_ref)
    hots, backs = (hots_ref.at[0], hot_ref), (backs_ref.at[0], back_ref, backs_ref.at[1])
    sums = sums_ref[...]
    contribs = []
    for n, group in enumerate((0, 2)):
        values = [[values_ref[n, i, tile] for tile in range(2)] for i in range(BX)]
        contribs.append(on_boxes(group, values, tables[group], boxes, sums))
    boxes.wait()
    for group, contrib in zip((0, 2), contribs):
        scatter(group, contrib, placed, boxes)
    nonlocal_[0:11] = spread_group(0, 6, 11, placed, backs[0])
    nonlocal_[11:18] = jnp.zeros((7, NY, NZ), jnp.float32)
    nonlocal_[18:24] = spread_group(2, 0, 6, placed, backs[2])
    for p in range(24):
        rest = nonlocal_[p]
        if not 6 <= p < 18:
            pot = edge_plane(p, edge_ref)
            field, tile = (low_ref, TILE_Y + 2 * (p + 6)) if p < 6 else (high_ref, TILE_Y + 2 * (p - 18))
            rest = rest + pot * field[tile : tile + 2].reshape(NY, NZ)
        updated = partial_ref[p] + rest * (1.0 / HALF)
        kept_ref[p] = updated
        fill(padded1, p, updated[None])
        field2[16 * p : 16 * p + 16, :] = two_terms(updated, 1)
    for p, value in second_step(boxes, hots, backs, padded1, field2, gathered, placed, local, nonlocal_, pot_ref, tables,
                                zst_ref, sums):
        out_ref[2 * p : 2 * p + 2] = (value - up_ref[TILE_Y + 2 * p : TILE_Y + 2 * p + 2].reshape(NY, NZ)).reshape(2, 8, 128)


def last_kernel(up_ref, high_ref, low_ref, pot_ref, table_ref, zst_ref, sums_ref, hot_ref, back_ref,
                kept_ref, edge_ref, hots_ref, backs_ref, highsib_ref, lowsib_ref,
                mid_ref, highy_ref, lowy_ref,
                out_ref,
                low_xy, own_xy, high_xy, padded, padded1, field2, gathered, placed, local, nonlocal_, sems):
    boxes = Boxes((low_ref, up_ref, high_ref), (low_xy, own_xy, high_xy), sems)
    load_fields([r[...] for r in (lowy_ref, mid_ref, highy_ref)], padded, field2)
    clear(placed)
    gathered[2][:, 12:SPAN] = jnp.zeros((2, SPAN - 12, 24, 128), jnp.float32)
    hots, backs = (hots_ref.at[0], hot_ref, hots_ref.at[1]), (backs_ref.at[0], back_ref, backs_ref.at[1])
    sums = sums_ref[...]
    tables = (laid(low_ref, lowsib_ref), laid(up_ref, table_ref), laid(high_ref, highsib_ref))
    for group, planes in ((0, SPAN), (1, SPAN), (2, 12)):
        gather_columns(group, field2, 12 * group, planes, 0, gathered, hots[group])
    local[...] = along_z(field2, slice(96, 480), zst_ref).reshape(24, NY, NZ)
    for p in range(24):
        laplace = stencil_plane(padded, p + 6) + local[p]
        if 6 <= p < 18:
            pot = own_potential(p, pot_ref)
        else:
            pot = edge_plane(p, edge_ref)
        applied = -0.5 * laplace + (pot - CENTER) * padded[p + 6, 8:24, :]
        local[p] = applied * (2.0 / HALF) - kept_ref[p]
    boxes.wait()
    windows = [read_windows(group, gathered, boxes) for group in range(3)]
    contribs = [on_boxes(group, windows[group], tables[group], boxes, sums) for group in range(3)]
    for group in range(3):
        scatter(group, contribs[group], placed, boxes)
    nonlocal_[0:11] = spread_group(0, 6, 11, placed, backs[0])
    nonlocal_[11:24] = jnp.zeros((13, NY, NZ), jnp.float32)
    nonlocal_[6:23] += spread_group(1, 0, 17, placed, backs[1])
    nonlocal_[18:24] += spread_group(2, 0, 6, placed, backs[2])
    for p in range(24):
        updated = local[p] + nonlocal_[p] * (2.0 / HALF)
        fill(padded1, p, updated[None])
        field2[16 * p : 16 * p + 16, :] = two_terms(updated, 1)
    for p, value in second_step(boxes, hots, backs, padded1, field2, gathered, placed, local, nonlocal_, pot_ref, tables,
                                zst_ref, sums):
        out_ref[2 * p : 2 * p + 2] = (value - padded[p + 12, 8:24, :]).reshape(2, 8, 128)


XY = [pltpu.SMEM((8, 128), jnp.float32)] * 3
PADDED = pltpu.VMEM((36, 32, NZ), jnp.float32)
PADDED1 = pltpu.VMEM((24, 32, NZ), jnp.float32)
FIELD2 = pltpu.VMEM((576, 2 * NZ), jnp.bfloat16)
BOXED = [pltpu.VMEM((2, SPAN, 24, 128), jnp.float32)] * 3
PLANES = pltpu.VMEM((24, NY, NZ), jnp.float32)
WORK = pltpu.VMEM((BX, BY * NPROJ, 128), jnp.float32)
COPIES = pltpu.SemaphoreType.DMA((3,))


def parts_kernel(factors_ref, own_ref, other_ref, base_ref, one_ref, three_ref):
    own, other = own_ref[...], other_ref[...]
    for hop, target in ((0, base_ref), (1, one_ref), (3, three_ref)):
        target[...] = factors_ref[2 * hop] * own + factors_ref[2 * hop + 1] * other


def store_kernel(own_ref, out_ref):
    out_ref[...] = own_ref[...]


def most_kernel(factors_ref, base_ref, one_ref, three_ref, far_ref, out_ref):
    out_ref[...] = (base_ref[...] + factors_ref[4] * far_ref[...]) + (one_ref[...] + three_ref[...])


def total_kernel(factors_ref, most_ref, farsib_ref, out_ref):
    out_ref[...] = most_ref[...] + factors_ref[5] * farsib_ref[...]


def ring(axis, step):
    count = lax.axis_size(axis)
    return [(i, (i + step) % count) for i in range(count)]


def meet(axis, bits):
    return [(i, i ^ bits) for i in range(lax.axis_size(axis))]


def shards(orbitals, potential, atom_pos, atom_count, projectors, gammas, ritz):
    stay = lambda v: pltpu.with_memory_space_constraint(v, pltpu.HBM)
    up, down, pot, rest = call(
        pack_kernel,
        [shape(TILES, 8, 128), shape(TILES, 8, 128), shape(24, 8, 128), shape(PAIRS, 8, 128)],
        [HBM] * 5 + [SMEM],
        (
            stay(orbitals.reshape(24, 8, 128)),
            stay(potential.reshape(24, 8, 128)),
            stay(projectors),
            stay(gammas.T),
            stay(atom_pos.T),
            atom_count,
        ),
        "pack",
        [
            pltpu.VMEM((NPROJ, ATOMS), jnp.float32),
            pltpu.VMEM((3, ATOMS), jnp.int32),
            pltpu.VMEM((PAIRS, 8, 128), jnp.float32),
            WORK,
            pltpu.SemaphoreType.DMA((13,)),
        ],
    )
    low = lax.ppermute(up, "dom", ring("dom", 1))
    high = lax.ppermute(down, "dom", ring("dom", -1))
    table, zst, sums, hot, back, factors = call(
        prepare_kernel,
        [
            shape(PAIRS, 8, 128),
            shape(384, NZ, dtype=jnp.bfloat16),
            shape(LANES, LANES, dtype=jnp.bfloat16),
            shape(2 * NZ, LANES, dtype=jnp.bfloat16),
            shape(2 * LANES, NZ, dtype=jnp.bfloat16),
            shape(8, 8, 128),
        ],
        [VMEM] * 3,
        (rest, down, ritz),
        "prepare",
        [WORK],
    )
    highsib = lax.ppermute(high, "band", meet("band", 1))
    lowsib = lax.ppermute(low, "band", meet("band", 1))
    common = (down, high, low, pot, table, zst, sums, hot, back)
    values, partial, hots, backs = call(
        head_kernel,
        [
            shape(2, BX, 2, 8, 128),
            shape(24, NY, NZ),
            shape(2, 2 * NZ, LANES, dtype=jnp.bfloat16),
            shape(2, 2 * LANES, NZ, dtype=jnp.bfloat16),
        ],
        [VMEM] * 9,
        common,
        "head",
        XY + [PADDED, FIELD2, BOXED, BOXED, PLANES, COPIES],
        flops=10_000_000_000,
    )
    second, first, edge = call(
        tail_kernel,
        [shape(24, 8, 128), shape(24, NY, NZ), shape(2, 12, 8, 128)],
        [VMEM] * 15,
        common + (values, partial, hots, backs, highsib, lowsib),
        "tail",
        XY + [PADDED1, FIELD2, BOXED, BOXED, PLANES, PLANES, COPIES],
    )
    low_y = lax.ppermute(second, "dom", ring("dom", 1))
    high_y = lax.ppermute(second, "dom", ring("dom", -1))
    (fourth,) = call(
        last_kernel,
        [shape(24, 8, 128)],
        [VMEM] * 18,
        common + (first, edge, hots, backs, highsib, lowsib, second, high_y, low_y),
        "last",
        XY + [PADDED, PADDED1, FIELD2, BOXED, BOXED, PLANES, PLANES, COPIES],
    )
    far = lax.ppermute(fourth, "band", meet("band", 4))
    other = lax.ppermute(fourth, "band", meet("band", 1))
    field = shape(24, 8, 128)
    base, one, three = call(parts_kernel, [field] * 3, [VMEM] * 3, (factors, fourth, other), "parts")
    one = lax.ppermute(one, "band", meet("band", 2))
    three = lax.ppermute(three, "band", meet("band", 6))
    farsib = lax.ppermute(far, "band", meet("band", 1))
    (filtered,) = call(store_kernel, [field], [VMEM], (fourth,), "store", flops=0, moved=0)
    (most,) = call(most_kernel, [field], [VMEM] * 5, (factors, base, one, three, far), "most")
    (rotated,) = call(total_kernel, [field], [VMEM] * 3, (factors, most, farsib), "total")
    return (filtered.reshape(orbitals.shape), rotated.reshape(orbitals.shape))


def solution(mesh):
    in_specs = (
        P("band", "dom", None, None),
        P("dom", None, None),
        P("dom", None),
        P("dom"),
        P("dom", None, None),
        P("dom", None),
        P(),
    )
    out_specs = (P("band", "dom", None, None), P("band", "dom", None, None))
    return jax.shard_map(shards, mesh=mesh, in_specs=in_specs, out_specs=out_specs, check_vma=False)
```
